32 devices in a mesh: lat: 8 (over z, y), mp: 4 (over x, core).
Axes of the slice: x: 2, y: 2, z: 4, core: 2. Of those that a mesh axis runs over, the one named last changes fastest.
Arguments:
- tokens: bfloat16 [16384, 1024], P(('lat', 'mp')), may hold values from -20 to 20
- gain: float32 [1024], replicated, may hold values from 0.1 to 1.9
- qkv_weight: bfloat16 [16, 192, 1024], P('mp'), may hold values from -2 to 2
- out_weight: bfloat16 [16, 64, 1024], P('mp'), may hold values from -1 to 1
- row_cells: int32 [64], replicated, may hold values from 32 to 256, as said below
- upstream: bfloat16 [16384, 1024], P(('lat', 'mp')), may hold values from -6 to 6
Outputs:
- update: bfloat16 [16384, 1024], P(('lat', 'mp'))
- grad_input: bfloat16 [16384, 1024], P(('lat', 'mp'))
- grad_qkv: float32 [16, 192, 1024], P('mp')
- grad_out: float32 [16, 64, 1024], P('mp')
The draws below stay inside these ranges and needn't reach their ends.
Inputs may be any that keep to these rules, and one draw needn't show every extreme that they name: `row_cells`: A row's live cells are its first ones; rows at the equator hold all 256, rows at the poles 256 // 8.
All inputs are finite; a program needn't handle non-finite values.
Results may differ from the reference program's by a relative error of at most 0.0085.
The reference program's roundings to bfloat16 on the way count: a program that leaves them out, or rounds other values in their place, can miss the bound.
Values may be sent and summed in bfloat16 or wider, within the bound.
No kernel may reach another device: no remote copies, remote signals or barrier semaphores. Data moves between devices by JAX's collectives and lax.ppermute only.
A program may use at most 192 MiB of HBM per device.

```python
import math
import jax
import jax.numpy as jnp
from jax import lax

WIDTH = 1024
HEAD_COUNT = 16
HEAD_WIDTH = 64
LONGITUDES = 256
LATITUDES = 64
TOKEN_COUNT = 16384


def draw_tokens(key, part):
    key = jax.random.fold_in(key, 11)
    base_key = jax.random.fold_in(key, 0)
    draws = jnp.clip(jax.random.normal(base_key, (TOKEN_COUNT, WIDTH), jnp.float32), -6.0, 6.0)
    return draws.astype(jnp.bfloat16)


def draw_qkv_weight(key, part):
    key = jax.random.fold_in(key, 12)
    query_key, keys_key, value_key = jax.random.split(key, 3)
    spread = 1.0 / math.sqrt(WIDTH)
    array_shape = (HEAD_COUNT, HEAD_WIDTH, WIDTH)
    queries = jnp.clip(jax.random.normal(query_key, array_shape, jnp.float32), -4.0, 4.0) * spread
    keys_part = jnp.clip(jax.random.normal(keys_key, array_shape, jnp.float32), -4.0, 4.0) * spread
    values = jnp.clip(jax.random.normal(value_key, array_shape, jnp.float32), -4.0, 4.0) * spread
    return jnp.concatenate([queries, keys_part, values], axis=1).astype(jnp.bfloat16)


def draw_out_weight(key, part):
    key = jax.random.fold_in(key, 13)
    base_key, order_key = jax.random.split(key)
    order = jax.random.permutation(order_key, HEAD_COUNT).astype(jnp.float32)
    exponent = order / max(1, HEAD_COUNT - 1) - 0.5
    head_scale = jnp.exp(exponent * math.log(16.0))
    head_scale = head_scale / jnp.sqrt(jnp.mean(head_scale * head_scale))
    draws = jnp.clip(jax.random.normal(base_key, (HEAD_COUNT, HEAD_WIDTH, WIDTH), jnp.float32), -4.0, 4.0)
    draws = draws * (1.0 / math.sqrt(WIDTH)) * head_scale[:, None, None]
    return draws.astype(jnp.bfloat16)


def draw_row_cells(key, part):
    key = jax.random.fold_in(key, 14)
    row_index = jnp.arange(LATITUDES, dtype=jnp.int32)
    distance = jnp.abs(2 * row_index - (LATITUDES - 1))
    jitter = jax.random.randint(key, (LATITUDES,), 0, LONGITUDES // 16 + 1, dtype=jnp.int32)
    live_cells = LONGITUDES + LONGITUDES // 16 - LONGITUDES * distance * distance // (LATITUDES * LATITUDES) - jitter
    return jnp.clip(live_cells, LONGITUDES // 8, LONGITUDES).astype(jnp.int32)


def block_levels(stream_key, shape, shards, least, largest):
    def one(axis_at, blocks):
        heights = jax.random.uniform(jax.random.fold_in(jax.random.fold_in(stream_key, 6), axis_at), (blocks,), jnp.float32, least / len(shards), largest / len(shards))
        return jnp.repeat(jnp.exp(heights), shape[axis_at] // blocks).reshape((-1,) + (1,) * (len(shape) - axis_at - 1))

    loudness = one(*shards[0])
    for cut in shards[1:]:
        loudness = loudness * one(*cut)
    return loudness


def normal_values(own_key, shape, scale, reach, shards=(), kind=jnp.bfloat16):
    result = scale * jax.random.normal(own_key, shape, jnp.float32)
    if shards:
        result = result * block_levels(own_key, shape, shards, -0.22, 0.18)
    return jnp.clip(result, -reach, reach).astype(kind)


def setup_inputs(seed: int = 0) -> dict:
    seeds = jax.random.split(jax.random.key(seed), 7)
    return {
        "tokens": draw_tokens(jax.random.fold_in(seeds[6], 71), 0),
        "gain": jnp.clip(1.0 + 0.18 * jax.random.normal(seeds[1], (WIDTH,), jnp.float32), 0.1, 1.9),
        "qkv_weight": draw_qkv_weight(jax.random.fold_in(seeds[6], 71), 0),
        "out_weight": draw_out_weight(jax.random.fold_in(seeds[6], 71), 0),
        "row_cells": draw_row_cells(jax.random.fold_in(seeds[6], 71), 0),
        "upstream": normal_values(seeds[5], (TOKEN_COUNT, WIDTH), 1.0, 6.0, ((0, 32),)),
    }


def rounded(array):
    return lax.optimization_barrier(array.astype(jnp.bfloat16))

def tile_mask(row_start, col_start, cells_pad, col_tile, key_cols):
    query_rows = jnp.arange(4, dtype=jnp.int32)
    key_rows = jnp.arange(16, dtype=jnp.int32)
    query_cols = col_start + jnp.arange(col_tile, dtype=jnp.int32)
    key_index = (col_start - 8 + jnp.arange(key_cols, dtype=jnp.int32)) % LONGITUDES
    query_cells = lax.dynamic_slice_in_dim(cells_pad, row_start + 6, 4)
    key_cells = lax.dynamic_slice_in_dim(cells_pad, row_start, 16)
    query_live = query_cols[None, :] < query_cells[:, None]
    key_live = key_index[None, :] < key_cells[:, None]
    row_near = jnp.abs(key_rows[None, :] - 6 - query_rows[:, None]) <= 6
    offset = (key_index[None, :] - query_cols[:, None]) % LONGITUDES
    col_near = (offset <= 6) | (offset >= LONGITUDES - 6)
    allowed = query_live[:, :, None, None] & key_live[None, None, :, :] & row_near[:, None, :, None] & col_near[None, :, None, :]
    return (allowed.reshape(4 * col_tile, 16 * key_cols), query_live.reshape(4 * col_tile), key_index)

def tile_probs(queries, keys_tile, allowed, query_live, score_scale):
    scores = jnp.einsum('qhd,khd->hqk', queries.astype(jnp.float32), keys_tile.astype(jnp.float32)) * score_scale
    masked = jnp.where(allowed[None], scores, -1e+30)
    highest = lax.optimization_barrier(jnp.max(masked, axis=2, keepdims=True))
    terms = jnp.where(allowed[None], jnp.exp(masked - highest), 0.0)
    total = lax.optimization_barrier(jnp.sum(terms, axis=2, keepdims=True)) + (1.0 - query_live.astype(jnp.float32))[None, :, None]
    return terms / total

def assemble(tiles, row_total, col_tile, heads, width):
    layout = tiles.reshape(row_total // 4, LONGITUDES // col_tile, 4, col_tile, heads, width)
    return layout.transpose(0, 2, 1, 3, 4, 5).reshape(row_total * LONGITUDES, heads * width)

def reference(tokens, gain, qkv_weight, out_weight, row_cells, upstream):
    score_scale = 1.0 / math.sqrt(HEAD_WIDTH)
    grad_scale = 4.0 / math.sqrt(TOKEN_COUNT)
    col_tile = min(128, LONGITUDES)
    key_cols = min(LONGITUDES, col_tile + 16)
    col_tiles = LONGITUDES // col_tile
    tile_count = LATITUDES // 4 * col_tiles
    zero_index = jnp.zeros((), jnp.int32)
    features = tokens.astype(jnp.float32)
    inverse = lax.rsqrt(lax.optimization_barrier(jnp.mean(features * features, axis=1, keepdims=True)) + 1e-06)
    normed = rounded(features * inverse * gain[None, :])
    qkv_flat_weight = qkv_weight.reshape(HEAD_COUNT * 3 * HEAD_WIDTH, WIDTH)
    qkv_flat = rounded(lax.dot_general(normed, qkv_flat_weight, (((1,), (1,)), ((), ())), preferred_element_type=jnp.float32))
    qkv_grid = qkv_flat.reshape(LATITUDES, LONGITUDES, HEAD_COUNT, 3 * HEAD_WIDTH)
    queries_all = qkv_grid[..., :HEAD_WIDTH]
    keyval_pad = jnp.pad(qkv_grid[..., HEAD_WIDTH:], ((6, 6), (0, 0), (0, 0), (0, 0)))
    cells_pad = jnp.pad(row_cells, (6, 6))

    def tile_anchor(tile_index):
        return (tile_index // col_tiles * 4, tile_index % col_tiles * col_tile)

    def tile_inputs(tile_index):
        row_start, col_start = tile_anchor(tile_index)
        allowed, query_live, key_index = tile_mask(row_start, col_start, cells_pad, col_tile, key_cols)
        queries = lax.dynamic_slice(queries_all, (row_start, col_start, zero_index, zero_index), (4, col_tile, HEAD_COUNT, HEAD_WIDTH)).reshape(4 * col_tile, HEAD_COUNT, HEAD_WIDTH)
        key_block = jnp.take(lax.dynamic_slice_in_dim(keyval_pad, row_start, 16, 0), key_index, axis=1)
        key_block = key_block.reshape(16 * key_cols, HEAD_COUNT, 2 * HEAD_WIDTH)
        return (allowed, query_live, key_index, queries, key_block)

    def forward_tile(tile_index):
        allowed, query_live, key_index, queries, key_block = tile_inputs(tile_index)
        probabilities = tile_probs(queries, key_block[..., :HEAD_WIDTH], allowed, query_live, score_scale)
        weights = rounded(probabilities).astype(jnp.float32)
        return rounded(jnp.einsum('hqk,khd->qhd', weights, key_block[..., HEAD_WIDTH:].astype(jnp.float32)))
    tile_ids = jnp.arange(tile_count, dtype=jnp.int32)
    heads_out = assemble(lax.map(forward_tile, tile_ids), LATITUDES, col_tile, HEAD_COUNT, HEAD_WIDTH)
    out_flat = out_weight.reshape(HEAD_COUNT * HEAD_WIDTH, WIDTH)
    update = jnp.dot(heads_out, out_flat, preferred_element_type=jnp.float32).astype(jnp.bfloat16)
    grad_heads = rounded(jnp.dot(upstream, out_flat.T, preferred_element_type=jnp.float32))
    grad_out = jnp.dot(heads_out.T, upstream, preferred_element_type=jnp.float32) * grad_scale
    grad_out = grad_out.reshape(HEAD_COUNT, HEAD_WIDTH, WIDTH)
    grad_grid = grad_heads.reshape(LATITUDES, LONGITUDES, HEAD_COUNT, HEAD_WIDTH)

    def backward_tile(key_accum, tile_index):
        allowed, query_live, key_index, queries, key_block = tile_inputs(tile_index)
        row_start, col_start = tile_anchor(tile_index)
        grad_tile = lax.dynamic_slice(grad_grid, (row_start, col_start, zero_index, zero_index), (4, col_tile, HEAD_COUNT, HEAD_WIDTH)).reshape(4 * col_tile, HEAD_COUNT, HEAD_WIDTH)
        grad_tile = grad_tile.astype(jnp.float32)
        keys_tile = key_block[..., :HEAD_WIDTH].astype(jnp.float32)
        values_tile = key_block[..., HEAD_WIDTH:].astype(jnp.float32)
        probabilities = tile_probs(queries, keys_tile, allowed, query_live, score_scale)
        weights = rounded(probabilities).astype(jnp.float32)
        grad_probs = jnp.einsum('qhd,khd->hqk', grad_tile, values_tile)
        row_delta = lax.optimization_barrier(jnp.sum(probabilities * grad_probs, axis=2, keepdims=True))
        grad_scores = rounded(probabilities * (grad_probs - row_delta)).astype(jnp.float32)
        grad_query = rounded(jnp.einsum('hqk,khd->qhd', grad_scores, keys_tile) * score_scale)
        grad_key = jnp.einsum('hqk,qhd->khd', grad_scores, queries.astype(jnp.float32)) * score_scale
        grad_value = jnp.einsum('hqk,qhd->khd', weights, grad_tile)
        key_grads = jnp.concatenate([grad_key, grad_value], axis=2).reshape(16, key_cols, HEAD_COUNT, 2 * HEAD_WIDTH)
        rows_hit = row_start + jnp.arange(16, dtype=jnp.int32)
        key_accum = key_accum.at[rows_hit[:, None], key_index[None, :]].add(key_grads)
        return (key_accum, grad_query)
    accum_start = jnp.zeros((LATITUDES + 12, LONGITUDES, HEAD_COUNT, 2 * HEAD_WIDTH), jnp.float32)
    key_accum, query_tiles = lax.scan(backward_tile, accum_start, tile_ids)
    grad_query_all = assemble(query_tiles, LATITUDES, col_tile, HEAD_COUNT, HEAD_WIDTH)
    grad_query_all = grad_query_all.reshape(TOKEN_COUNT, HEAD_COUNT, HEAD_WIDTH)
    grad_keyval = key_accum[6:LATITUDES + 6].astype(jnp.bfloat16).reshape(TOKEN_COUNT, HEAD_COUNT, 2 * HEAD_WIDTH)
    grad_proj = jnp.concatenate([grad_query_all, grad_keyval], axis=2).reshape(TOKEN_COUNT, HEAD_COUNT * 3 * HEAD_WIDTH)
    grad_qkv = lax.dot_general(grad_proj, normed, (((0,), (0,)), ((), ())), preferred_element_type=jnp.float32) * grad_scale
    grad_qkv = grad_qkv.reshape(HEAD_COUNT, 3 * HEAD_WIDTH, WIDTH)
    grad_normed = jnp.dot(grad_proj, qkv_flat_weight, preferred_element_type=jnp.float32)
    centred = features * inverse
    scaled = gain[None, :] * grad_normed
    grad_input = inverse * (scaled - centred * lax.optimization_barrier(jnp.mean(scaled * centred, axis=1, keepdims=True)))
    return (update, grad_input.astype(jnp.bfloat16), grad_qkv, grad_out)
```

```python
import functools
import math
import jax
import jax.numpy as jnp
from jax import lax
from jax.experimental import pallas as pl
from jax.experimental.pallas import tpu as pltpu

HEAD_WIDTH = 64
LONGITUDES = 256
BAND_ROWS = 8
HALO = 6
EXT_ROWS = BAND_ROWS + 2 * HALO
LANES = 256
QUERY_ROWS = 4
KEY_ROWS = QUERY_ROWS + 2 * HALO
BLOCK = 8
BLOCKS = LONGITUDES // BLOCK
KEYS = KEY_ROWS * BLOCK
MASKED = -1e30


def nn(a, b):
    return lax.dot_general(a, b, (((1,), (0,)), ((), ())), preferred_element_type=jnp.float32)


def nt(a, b):
    return lax.dot_general(a, b, (((1,), (1,)), ((), ())), preferred_element_type=jnp.float32)


def attention_kernel(
    heads,
    cells,
    q, go, k_top, k_own, k_bot, v_top, v_own, v_bot,
    out, dq, dk_own, dv_own, dk_top, dv_top, dk_bot, dv_bot,
    k_s, v_s, kt_s, vt_s, dk_s, dv_s, live_s, near_s,
):
    feats = heads * HEAD_WIDTH
    tile_cols = LANES // heads // QUERY_ROWS
    tile_queries = QUERY_ROWS * tile_cols
    window = tile_cols // BLOCK + 2

    def load_pair(p, carry):
        cols = pl.ds(pl.multiple_of(p * 16, 16), 16)
        for parts, rows_s, turned_s in (((k_top, k_own, k_bot), k_s, kt_s), ((v_top, v_own, v_bot), v_s, vt_s)):
            both = jnp.concatenate([part[:, cols, :].astype(jnp.float32) for part in parts], axis=0)
            for half in range(2):
                block = both[:, 8 * half:8 * half + 8, :].reshape(EXT_ROWS * BLOCK, feats)
                rows_s[2 * p + half] = block.astype(jnp.bfloat16)
                for upper in range(2):
                    first = upper * QUERY_ROWS * BLOCK
                    turned_s[upper, 2 * p + half] = block[first:first + KEYS].T.astype(jnp.bfloat16)
        for half in range(2):
            col = (2 * p + half) * BLOCK + lax.broadcasted_iota(jnp.int32, (BLOCK, 128), 0)
            for row in range(EXT_ROWS):
                live_s[2 * p + half, row * BLOCK:(row + 1) * BLOCK, :] = jnp.where(col < cells[row], 0.0, MASKED)
        return carry

    lax.fori_loop(0, BLOCKS // 2, load_pair, 0)
    dk_s[...] = jnp.zeros_like(dk_s)
    dv_s[...] = jnp.zeros_like(dv_s)

    lane = lax.broadcasted_iota(jnp.int32, (KEYS, LANES), 1) % tile_queries
    query_row = lane // tile_cols
    query_col = lane % tile_cols
    key = lax.broadcasted_iota(jnp.int32, (KEYS, LANES), 0)
    row_gap = key // BLOCK - query_row
    for j in range(window):
        col_gap = (j - 1) * BLOCK + key % BLOCK - query_col
        near = (row_gap >= 0) & (row_gap <= 2 * HALO) & (col_gap >= -HALO) & (col_gap <= HALO)
        near_s[j] = jnp.where(near, 0.0, MASKED)

    own_head = (
        lax.broadcasted_iota(jnp.int32, (LANES, feats), 0) // tile_queries
        == lax.broadcasted_iota(jnp.int32, (LANES, feats), 1) // HEAD_WIDTH
    )
    own_head_turned = (
        lax.broadcasted_iota(jnp.int32, (feats, LANES), 1) // tile_queries
        == lax.broadcasted_iota(jnp.int32, (feats, LANES), 0) // HEAD_WIDTH
    )
    query_lane = lax.broadcasted_iota(jnp.int32, (1, LANES), 1) % tile_queries

    def spread(ref, upper, cols):
        tile = ref[upper * QUERY_ROWS:(upper + 1) * QUERY_ROWS, cols, :].reshape(tile_queries, feats)
        if heads == 1:
            return tile
        stacked = jnp.concatenate([tile] * heads, axis=0)
        return jnp.where(own_head, stacked, jnp.zeros_like(stacked))

    def gather(turned):
        if heads == 1:
            tile = turned.T
        else:
            tall = jnp.where(own_head_turned, turned, 0.0).T
            tile = sum(tall[h * tile_queries:(h + 1) * tile_queries] for h in range(heads))
        return tile.astype(jnp.bfloat16).reshape(QUERY_ROWS, tile_cols, feats)

    def one_tile(upper, tile):
        start = pl.multiple_of(tile * tile_cols, 16)
        cols = pl.ds(start, tile_cols)
        rows = slice(upper * QUERY_ROWS, (upper + 1) * QUERY_ROWS)
        keys = pl.ds(upper * QUERY_ROWS * BLOCK, KEYS)
        index = [(tile * (tile_cols // BLOCK) + j + BLOCKS - 1) % BLOCKS for j in range(window)]
        queries = spread(q, upper, cols)
        grads = spread(go, upper, cols)
        scores = [
            nt(k_s[index[j], keys, :], queries)
            + near_s[j]
            + jnp.concatenate([live_s[index[j], keys, :]] * (LANES // 128), axis=1)
            for j in range(window)
        ]
        highest = jnp.max(functools.reduce(jnp.maximum, scores), axis=0, keepdims=True)
        terms = [jnp.exp(score - highest) for score in scores]
        total = jnp.sum(sum(terms), axis=0, keepdims=True)
        query_cells = jnp.zeros((1, LANES), jnp.int32)
        for row in range(QUERY_ROWS):
            cell = cells[HALO + upper * QUERY_ROWS + row]
            query_cells = jnp.where(query_lane // tile_cols == row, cell, query_cells)
        live = start + query_lane % tile_cols < query_cells
        inverse = jnp.where(live, 1.0 / total, 0.0)
        probs = [term * inverse for term in terms]
        grad_probs = [nt(v_s[index[j], keys, :], grads) for j in range(window)]
        delta = jnp.sum(sum(p * g for p, g in zip(probs, grad_probs)), axis=0, keepdims=True)
        weights = [p.astype(jnp.bfloat16) for p in probs]
        grad_scores = [(p * (g - delta)).astype(jnp.bfloat16) for p, g in zip(probs, grad_probs)]
        for j in range(window):
            dv_s[index[j], keys, :] += nn(weights[j], grads)
            dk_s[index[j], keys, :] += nn(grad_scores[j], queries)
        values_turned = jnp.concatenate([vt_s[upper, index[j]] for j in range(window)], axis=1)
        keys_turned = jnp.concatenate([kt_s[upper, index[j]] for j in range(window)], axis=1)
        out[rows, cols, :] = gather(nn(values_turned, jnp.concatenate(weights, axis=0)))
        dq[rows, cols, :] = gather(nn(keys_turned, jnp.concatenate(grad_scores, axis=0)) * (HEAD_WIDTH ** -0.5))

    def tile_pair(tile, carry):
        for upper in range(2):
            one_tile(upper, tile)
        return carry

    lax.fori_loop(0, LONGITUDES // tile_cols, tile_pair, 0)

    def store_pair(p, carry):
        cols = pl.ds(pl.multiple_of(p * 16, 16), 16)
        for sums, top, own, bot in ((dk_s, dk_top, dk_own, dk_bot), (dv_s, dv_top, dv_own, dv_bot)):
            both = jnp.concatenate(
                [sums[2 * p + half].reshape(EXT_ROWS, BLOCK, feats) for half in range(2)], axis=1
            )
            top[:, cols, :] = both[:HALO].astype(jnp.bfloat16)
            own[:, cols, :] = both[HALO:HALO + BAND_ROWS]
            bot[:, cols, :] = both[HALO + BAND_ROWS:].astype(jnp.bfloat16)
        return carry

    lax.fori_loop(0, BLOCKS // 2, store_pair, 0)


def attention(cells, q, go, k_parts, v_parts):
    feats = q.shape[-1]
    heads = feats // HEAD_WIDTH
    window = LANES // heads // QUERY_ROWS // BLOCK + 2
    vmem = pl.BlockSpec(memory_space=pltpu.VMEM)
    grid = lambda rows, kind: jax.ShapeDtypeStruct((rows, LONGITUDES, feats), kind)
    bf16, f32 = jnp.bfloat16, jnp.float32
    pairs = BAND_ROWS * LONGITUDES * heads * KEYS * window
    return pl.pallas_call(
        functools.partial(attention_kernel, heads),
        out_shape=(
            grid(BAND_ROWS, bf16), grid(BAND_ROWS, bf16),
            grid(BAND_ROWS, f32), grid(BAND_ROWS, f32),
            grid(HALO, bf16), grid(HALO, bf16), grid(HALO, bf16), grid(HALO, bf16),
        ),
        in_specs=[pl.BlockSpec(memory_space=pltpu.SMEM)] + [vmem] * 8,
        out_specs=(vmem,) * 8,
        scratch_shapes=[
            pltpu.VMEM((BLOCKS, EXT_ROWS * BLOCK, feats), bf16),
            pltpu.VMEM((BLOCKS, EXT_ROWS * BLOCK, feats), bf16),
            pltpu.VMEM((2, BLOCKS, feats, KEYS), bf16),
            pltpu.VMEM((2, BLOCKS, feats, KEYS), bf16),
            pltpu.VMEM((BLOCKS, EXT_ROWS * BLOCK, feats), f32),
            pltpu.VMEM((BLOCKS, EXT_ROWS * BLOCK, feats), f32),
            pltpu.VMEM((BLOCKS, EXT_ROWS * BLOCK, 128), f32),
            pltpu.VMEM((window, KEYS, LANES), f32),
        ],
        compiler_params=pltpu.CompilerParams(vmem_limit_bytes=60 * 2**20),
        cost_estimate=pl.CostEstimate(
            flops=12 * pairs * HEAD_WIDTH, transcendentals=pairs, bytes_accessed=20 * 2**20
        ),
    )(cells, q, go, *k_parts, *v_parts)


from jax.sharding import PartitionSpec as P

WIDTH = 1024


def passed_along(x, axis, by):
    length = lax.axis_size(axis)
    pairs = [(i, i + by) for i in range(length) if 0 <= i + by < length]
    return lax.ppermute(x, axis, pairs)


def halo_parts(x):
    before = passed_along(x[BAND_ROWS - HALO:], "lat", 1)
    after = passed_along(x[:HALO], "lat", -1)
    return before, x, after


def on_device(tokens, gain, qkv_weight, out_weight, row_cells, upstream):
    heads = qkv_weight.shape[0]
    feats = heads * HEAD_WIDTH
    band_tokens = BAND_ROWS * LONGITUDES
    grad_scale = 4.0 / math.sqrt(band_tokens * lax.axis_size("lat"))
    band_start = lax.axis_index("lat") * BAND_ROWS
    cells = lax.dynamic_slice_in_dim(jnp.pad(row_cells, (HALO, HALO)), band_start, EXT_ROWS)

    features = tokens.astype(jnp.float32)
    inverse = lax.rsqrt(jnp.mean(features * features, axis=1, keepdims=True) + 1e-06)
    normed = (features * inverse * gain[None, :]).astype(jnp.bfloat16)
    normed_band = lax.all_gather(normed, "mp", axis=0, tiled=True)
    band_upstream = lax.all_gather(upstream, "mp", axis=0, tiled=True)

    split_weight = qkv_weight.reshape(heads, 3, HEAD_WIDTH, WIDTH).transpose(1, 0, 2, 3)
    split_weight = split_weight.reshape(3 * feats, WIDTH)
    out_flat = out_weight.reshape(feats, WIDTH)
    qkv = nt(normed_band, split_weight)
    q = (qkv[:, :feats].astype(jnp.bfloat16) * HEAD_WIDTH ** -0.5).astype(jnp.bfloat16)
    k = qkv[:, feats:2 * feats].astype(jnp.bfloat16)
    v = qkv[:, 2 * feats:].astype(jnp.bfloat16)
    grid = lambda x: x.reshape(BAND_ROWS, LONGITUDES, feats)
    grad_heads = nt(band_upstream, out_flat).astype(jnp.bfloat16)
    k_parts, v_parts = halo_parts(grid(k)), halo_parts(grid(v))
    out, dq, dk, dv, dk_top, dv_top, dk_bot, dv_bot = attention(
        cells, grid(q), grid(grad_heads), k_parts, v_parts
    )
    flat = lambda x: x.reshape(band_tokens, feats)

    def joined(own, top, bot):
        from_above = passed_along(top, "lat", -1).astype(jnp.float32)
        from_below = passed_along(bot, "lat", 1).astype(jnp.float32)
        own = own + jnp.pad(from_below, ((0, BAND_ROWS - HALO), (0, 0), (0, 0)))
        own = own + jnp.pad(from_above, ((BAND_ROWS - HALO, 0), (0, 0), (0, 0)))
        return flat(own.astype(jnp.bfloat16))

    dk, dv = joined(dk, dk_top, dk_bot), joined(dv, dv_top, dv_bot)
    grad_proj = jnp.concatenate([flat(dq), dk, dv], axis=1)

    update = lax.psum_scatter(
        nn(flat(out), out_flat).astype(jnp.bfloat16), "mp", scatter_dimension=0, tiled=True
    )
    tn = lambda a, b: lax.dot_general(a, b, (((0,), (0,)), ((), ())), preferred_element_type=jnp.float32)
    grad_out = lax.psum(tn(flat(out), band_upstream).astype(jnp.bfloat16), "lat").astype(jnp.float32)
    grad_qkv = lax.psum(tn(grad_proj, normed_band).astype(jnp.bfloat16), "lat").astype(jnp.float32)
    grad_qkv = grad_qkv.reshape(3, heads, HEAD_WIDTH, WIDTH).transpose(1, 0, 2, 3)
    grad_normed = lax.psum_scatter(
        nn(grad_proj, split_weight).astype(jnp.bfloat16), "mp", scatter_dimension=0, tiled=True
    ).astype(jnp.float32)
    centred = features * inverse
    scaled = gain[None, :] * grad_normed
    grad_input = inverse * (scaled - centred * jnp.mean(scaled * centred, axis=1, keepdims=True))
    return (
        update,
        grad_input.astype(jnp.bfloat16),
        grad_qkv.reshape(heads, 3 * HEAD_WIDTH, WIDTH) * grad_scale,
        (grad_out * grad_scale).reshape(heads, HEAD_WIDTH, WIDTH),
    )


def solution(mesh):
    return jax.shard_map(
        on_device,
        mesh=mesh,
        in_specs=(
            P(("lat", "mp"), None),
            P(),
            P("mp", None, None),
            P("mp", None, None),
            P(),
            P(("lat", "mp"), None),
        ),
        out_specs=(
            P(("lat", "mp"), None),
            P(("lat", "mp"), None),
            P("mp", None, None),
            P("mp", None, None),
        ),
        check_vma=False,
    )
```

```python
import functools
import math
import jax
import jax.numpy as jnp
from jax import lax
from jax.experimental import pallas as pl
from jax.experimental.pallas import tpu as pltpu

HEAD_WIDTH = 64
LONGITUDES = 256
BAND_ROWS = 8
HALO = 6
EXT_ROWS = BAND_ROWS + 2 * HALO
LANES = 256
QUERY_ROWS = 4
KEY_ROWS = QUERY_ROWS + 2 * HALO
BLOCK = 8
BLOCKS = LONGITUDES // BLOCK
KEYS = KEY_ROWS * BLOCK
MASKED = -1e30


def nn(a, b):
    return lax.dot_general(a, b, (((1,), (0,)), ((), ())), preferred_element_type=jnp.float32)


def nt(a, b):
    return lax.dot_general(a, b, (((1,), (1,)), ((), ())), preferred_element_type=jnp.float32)


def attention_kernel(
    heads,
    cells,
    q, go, k_top, k_own, k_bot, v_top, v_own, v_bot,
    out, dq, dk_own, dv_own, dk_top, dv_top, dk_bot, dv_bot,
    k_s, v_s, kt_s, vt_s, dk_s, dv_s, live_s, near_s,
):
    feats = heads * HEAD_WIDTH
    tile_cols = LANES // heads // QUERY_ROWS
    tile_queries = QUERY_ROWS * tile_cols
    window = tile_cols // BLOCK + 2

    def load_pair(p, carry):
        cols = pl.ds(pl.multiple_of(p * 16, 16), 16)
        for parts, rows_s, turned_s in (((k_top, k_own, k_bot), k_s, kt_s), ((v_top, v_own, v_bot), v_s, vt_s)):
            both = jnp.concatenate([part[:, cols, :].astype(jnp.float32) for part in parts], axis=0)
            for half in range(2):
                block = both[:, 8 * half:8 * half + 8, :].reshape(EXT_ROWS * BLOCK, feats)
                rows_s[2 * p + half] = block.astype(jnp.bfloat16)
                for upper in range(2):
                    first = upper * QUERY_ROWS * BLOCK
                    turned_s[upper, 2 * p + half] = block[first:first + KEYS].T.astype(jnp.bfloat16)
        for half in range(2):
            col = (2 * p + half) * BLOCK + lax.broadcasted_iota(jnp.int32, (BLOCK, 128), 0)
            for row in range(EXT_ROWS):
                live_s[2 * p + half, row * BLOCK:(row + 1) * BLOCK, :] = jnp.where(col < cells[row], 0.0, MASKED)
        return carry

    lax.fori_loop(0, BLOCKS // 2, load_pair, 0)
    dk_s[...] = jnp.zeros_like(dk_s)
    dv_s[...] = jnp.zeros_like(dv_s)

    lane = lax.broadcasted_iota(jnp.int32, (KEYS, LANES), 1) % tile_queries
    query_row = lane // tile_cols
    query_col = lane % tile_cols
    key = lax.broadcasted_iota(jnp.int32, (KEYS, LANES), 0)
    row_gap = key // BLOCK - query_row
    for j in range(window):
        col_gap = (j - 1) * BLOCK + key % BLOCK - query_col
        near = (row_gap >= 0) & (row_gap <= 2 * HALO) & (col_gap >= -HALO) & (col_gap <= HALO)
        near_s[j] = jnp.where(near, 0.0, MASKED)

    own_head = (
        lax.broadcasted_iota(jnp.int32, (LANES, feats), 0) // tile_queries
        == lax.broadcasted_iota(jnp.int32, (LANES, feats), 1) // HEAD_WIDTH
    )
    own_head_turned = (
        lax.broadcasted_iota(jnp.int32, (feats, LANES), 1) // tile_queries
        == lax.broadcasted_iota(jnp.int32, (feats, LANES), 0) // HEAD_WIDTH
    )
    query_lane = lax.broadcasted_iota(jnp.int32, (1, LANES), 1) % tile_queries

    def spread(ref, upper, cols):
        tile = ref[upper * QUERY_ROWS:(upper + 1) * QUERY_ROWS, cols, :].reshape(tile_queries, feats)
        if heads == 1:
            return tile
        stacked = jnp.concatenate([tile] * heads, axis=0)
        return jnp.where(own_head, stacked, jnp.zeros_like(stacked))

    def gather(turned):
        if heads == 1:
            tile = turned.T
        else:
            tall = jnp.where(own_head_turned, turned, 0.0).T
            tile = sum(tall[h * tile_queries:(h + 1) * tile_queries] for h in range(heads))
        return tile.astype(jnp.bfloat16).reshape(QUERY_ROWS, tile_cols, feats)

    def one_tile(upper, tile):
        start = pl.multiple_of(tile * tile_cols, 16)
        cols = pl.ds(start, tile_cols)
        rows = slice(upper * QUERY_ROWS, (upper + 1) * QUERY_ROWS)
        keys = pl.ds(upper * QUERY_ROWS * BLOCK, KEYS)
        index = [(tile * (tile_cols // BLOCK) + j + BLOCKS - 1) % BLOCKS for j in range(window)]
        queries = spread(q, upper, cols)
        grads = spread(go, upper, cols)
        scores = [
            nt(k_s[index[j], keys, :], queries)
            + near_s[j]
            + jnp.concatenate([live_s[index[j], keys, :]] * (LANES // 128), axis=1)
            for j in range(window)
        ]
        highest = jnp.max(functools.reduce(jnp.maximum, scores), axis=0, keepdims=True)
        terms = [jnp.exp(score - highest) for score in scores]
        total = jnp.sum(sum(terms), axis=0, keepdims=True)
        query_cells = jnp.zeros((1, LANES), jnp.int32)
        for row in range(QUERY_ROWS):
            cell = cells[HALO + upper * QUERY_ROWS + row]
            query_cells = jnp.where(query_lane // tile_cols == row, cell, query_cells)
        live = start + query_lane % tile_cols < query_cells
        inverse = jnp.where(live, 1.0 / total, 0.0)
        probs = [term * inverse for term in terms]
        grad_probs = [nt(v_s[index[j], keys, :], grads) for j in range(window)]
        delta = jnp.sum(sum(p * g for p, g in zip(probs, grad_probs)), axis=0, keepdims=True)
        weights = [p.astype(jnp.bfloat16) for p in probs]
        grad_scores = [(p * (g - delta)).astype(jnp.bfloat16) for p, g in zip(probs, grad_probs)]
        for j in range(window):
            dv_s[index[j], keys, :] += nn(weights[j], grads)
            dk_s[index[j], keys, :] += nn(grad_scores[j], queries)
        values_turned = jnp.concatenate([vt_s[upper, index[j]] for j in range(window)], axis=1)
        keys_turned = jnp.concatenate([kt_s[upper, index[j]] for j in range(window)], axis=1)
        out[rows, cols, :] = gather(nn(values_turned, jnp.concatenate(weights, axis=0)))
        dq[rows, cols, :] = gather(nn(keys_turned, jnp.concatenate(grad_scores, axis=0)) * (HEAD_WIDTH ** -0.5))

    def tile_pair(tile, carry):
        for upper in range(2):
            one_tile(upper, tile)
        return carry

    lax.fori_loop(0, LONGITUDES // tile_cols, tile_pair, 0)

    def store_pair(p, carry):
        cols = pl.ds(pl.multiple_of(p * 16, 16), 16)
        for sums, top, own, bot in ((dk_s, dk_top, dk_own, dk_bot), (dv_s, dv_top, dv_own, dv_bot)):
            both = jnp.concatenate(
                [sums[2 * p + half].reshape(EXT_ROWS, BLOCK, feats) for half in range(2)], axis=1
            )
            top[:, cols, :] = both[:HALO].astype(jnp.bfloat16)
            own[:, cols, :] = both[HALO:HALO + BAND_ROWS]
            bot[:, cols, :] = both[HALO + BAND_ROWS:].astype(jnp.bfloat16)
        return carry

    lax.fori_loop(0, BLOCKS // 2, store_pair, 0)


def attention(cells, q, go, k_parts, v_parts):
    feats = q.shape[-1]
    heads = feats // HEAD_WIDTH
    window = LANES // heads // QUERY_ROWS // BLOCK + 2
    vmem = pl.BlockSpec(memory_space=pltpu.VMEM)
    grid = lambda rows, kind: jax.ShapeDtypeStruct((rows, LONGITUDES, feats), kind)
    bf16, f32 = jnp.bfloat16, jnp.float32
    pairs = BAND_ROWS * LONGITUDES * heads * KEYS * window
    return pl.pallas_call(
        functools.partial(attention_kernel, heads),
        out_shape=(
            grid(BAND_ROWS, bf16), grid(BAND_ROWS, bf16),
            grid(BAND_ROWS, f32), grid(BAND_ROWS, f32),
            grid(HALO, bf16), grid(HALO, bf16), grid(HALO, bf16), grid(HALO, bf16),
        ),
        in_specs=[pl.BlockSpec(memory_space=pltpu.SMEM)] + [vmem] * 8,
        out_specs=(vmem,) * 8,
        scratch_shapes=[
            pltpu.VMEM((BLOCKS, EXT_ROWS * BLOCK, feats), bf16),
            pltpu.VMEM((BLOCKS, EXT_ROWS * BLOCK, feats), bf16),
            pltpu.VMEM((2, BLOCKS, feats, KEYS), bf16),
            pltpu.VMEM((2, BLOCKS, feats, KEYS), bf16),
            pltpu.VMEM((BLOCKS, EXT_ROWS * BLOCK, feats), f32),
            pltpu.VMEM((BLOCKS, EXT_ROWS * BLOCK, feats), f32),
            pltpu.VMEM((BLOCKS, EXT_ROWS * BLOCK, 128), f32),
            pltpu.VMEM((window, KEYS, LANES), f32),
        ],
        compiler_params=pltpu.CompilerParams(vmem_limit_bytes=60 * 2**20),
        cost_estimate=pl.CostEstimate(
            flops=12 * pairs * HEAD_WIDTH, transcendentals=pairs, bytes_accessed=20 * 2**20
        ),
    )(cells, q, go, *k_parts, *v_parts)


from jax.sharding import Mesh, PartitionSpec as P

WIDTH = 1024
GROUP = ("y", "m", "c")


def tn(a, b):
    return lax.dot_general(a, b, (((0,), (0,)), ((), ())), preferred_element_type=jnp.float32)


def to_bands(halves, step):
    dm, dc = step
    place = lambda y, m, c: (y * halves + m) * 2 + c
    return [
        (place(y, m, c), place((c + dc) % 2, (m + dm) % halves, y))
        for y in range(2) for m in range(halves) for c in range(2)
    ]


def passed_along(x, by):
    length = lax.axis_size("z") * 2
    pairs = [(i, i + by) for i in range(length) if 0 <= i + by < length]
    return lax.ppermute(x, ("z", "c"), pairs)


def halo_parts(x):
    before = passed_along(x[BAND_ROWS - HALO:], 1)
    after = passed_along(x[:HALO], -1)
    return before, x, after


def on_device(tokens, gain, qkv_weight, out_weight, row_cells, upstream):
    heads = qkv_weight.shape[0]
    feats = heads * HEAD_WIDTH
    band_tokens = BAND_ROWS * LONGITUDES
    chunk = tokens.shape[0]
    halves = lax.axis_size("m")
    y, m, c = (lax.axis_index(axis) for axis in GROUP)
    steps = [(dm, dc) for dm in range(halves) for dc in range(2)]
    arrives = [((m - dm) % halves) * 2 + (y - dc) % 2 for dm, dc in steps]
    leads = [((m + dm) % halves) * 2 + (c + dc) % 2 for dm, dc in steps]
    grad_scale = 4.0 / math.sqrt(band_tokens * lax.axis_size("z") * 2)
    band_start = (lax.axis_index("z") * 2 + c) * BAND_ROWS
    cells = lax.dynamic_slice_in_dim(jnp.pad(row_cells, (HALO, HALO)), band_start, EXT_ROWS)

    def send(x, step):
        return lax.ppermute(x, GROUP, to_bands(halves, step))

    def send_back(x, step):
        return lax.ppermute(x, GROUP, [(b, a) for a, b in to_bands(halves, step)])

    def in_order(parts):
        whole = jnp.zeros((band_tokens,) + parts[0].shape[1:], parts[0].dtype)
        for part, at in zip(parts, arrives):
            whole = lax.dynamic_update_slice_in_dim(whole, part, at * chunk, 0)
        return whole

    def group_weight(weight):
        pairs = [((y * halves + m) * 2 + y, (y * halves + m) * 2 + 1 - y) for y in range(2) for m in range(halves)]
        return jnp.where(c == y, weight, lax.ppermute(weight, GROUP, pairs))

    features = tokens.astype(jnp.float32)
    inverse = lax.rsqrt(jnp.mean(features * features, axis=1, keepdims=True) + 1e-06)
    normed = (features * inverse * gain[None, :]).astype(jnp.bfloat16)
    normed_band = in_order([send(normed, step) for step in steps])

    out_full = lax.all_gather(out_weight.reshape(feats, WIDTH), ("m", "c"), axis=0, tiled=True)
    grad_heads_own = nt(upstream, out_full).astype(jnp.bfloat16)
    split_weight = qkv_weight.reshape(heads, 3, HEAD_WIDTH, WIDTH).transpose(1, 0, 2, 3)
    split_weight = group_weight(split_weight.reshape(3 * feats, WIDTH))
    qkv = nt(normed_band, split_weight)
    q = (qkv[:, :feats].astype(jnp.bfloat16) * HEAD_WIDTH ** -0.5).astype(jnp.bfloat16)
    k = qkv[:, feats:2 * feats].astype(jnp.bfloat16)
    v = qkv[:, 2 * feats:].astype(jnp.bfloat16)
    grid = lambda x: x.reshape(BAND_ROWS, LONGITUDES, feats)
    flat = lambda x: x.reshape(band_tokens, feats)
    k_parts, v_parts = halo_parts(grid(k)), halo_parts(grid(v))
    grad_heads = in_order([
        send(lax.dynamic_slice_in_dim(grad_heads_own, lead * feats, feats, 1), step)
        for step, lead in zip(steps, leads)
    ])
    held, k_parts = lax.optimization_barrier((upstream, k_parts))
    band_upstream = in_order([send(held, step) for step in steps])

    out, dq, dk, dv, dk_top, dv_top, dk_bot, dv_bot = attention(
        cells, grid(q), grid(grad_heads), k_parts, v_parts
    )
    out = flat(out)

    update = 0.0
    for step, lead, arrive in zip(steps, leads, arrives):
        part = send_back(lax.dynamic_slice_in_dim(out, arrive * chunk, chunk, 0), step)
        update += nn(part, lax.dynamic_slice_in_dim(out_full, lead * feats, feats, 0))

    def joined(own, top, bot):
        from_above = passed_along(top, -1).astype(jnp.float32)
        from_below = passed_along(bot, 1).astype(jnp.float32)
        own = own + jnp.pad(from_below, ((0, BAND_ROWS - HALO), (0, 0), (0, 0)))
        own = own + jnp.pad(from_above, ((BAND_ROWS - HALO, 0), (0, 0), (0, 0)))
        return flat(own.astype(jnp.bfloat16))

    dk, dv = joined(dk, dk_top, dk_bot), joined(dv, dv_top, dv_bot)
    grad_proj = jnp.concatenate([flat(dq), dk, dv], axis=1)

    part = nn(grad_proj, split_weight).astype(jnp.bfloat16)
    grad_normed = 0.0
    for step, arrive in zip(steps, arrives):
        grad_normed += send_back(
            lax.dynamic_slice_in_dim(part, arrive * chunk, chunk, 0), step
        ).astype(jnp.float32)
    centred = features * inverse
    scaled = gain[None, :] * grad_normed
    grad_input = inverse * (scaled - centred * jnp.mean(scaled * centred, axis=1, keepdims=True))

    grads = jnp.concatenate([tn(grad_proj, normed_band), tn(out, band_upstream)], axis=0)
    grads = lax.psum(grads.astype(jnp.bfloat16), ("z", "c"))
    pairs = [
        ((1 - y) * halves * 2 + m * 2 + 1 - y, y * halves * 2 + m * 2 + 1 - y)
        for y in range(2) for m in range(halves)
    ]
    grads = jnp.where(c == y, grads, lax.ppermute(grads, GROUP, pairs)).astype(jnp.float32) * grad_scale
    grad_qkv = grads[:3 * feats].reshape(3, heads, HEAD_WIDTH, WIDTH).transpose(1, 0, 2, 3)
    return (
        update.astype(jnp.bfloat16),
        grad_input.astype(jnp.bfloat16),
        grad_qkv.reshape(heads, 3 * HEAD_WIDTH, WIDTH),
        grads[3 * feats:].reshape(heads, HEAD_WIDTH, WIDTH),
    )


def solution(mesh):
    devices = mesh.devices.reshape(mesh.shape["lat"] // 2, 2, mesh.shape["mp"] // 2, 2)
    tokens, weights = P(("z", "y", "m", "c"), None), P(("m", "c"), None, None)
    return jax.shard_map(
        on_device,
        mesh=Mesh(devices, ("z", "y", "m", "c")),
        in_specs=(tokens, P(), weights, weights, P(), tokens),
        out_specs=(tokens, tokens, weights, weights),
        check_vma=False,
    )
```

```python
import functools
import math
import jax
import jax.numpy as jnp
from jax import lax
from jax.experimental import pallas as pl
from jax.experimental.pallas import tpu as pltpu

HEAD_WIDTH = 64
LONGITUDES = 256
BAND_ROWS = 8
HALO = 6
EXT_ROWS = BAND_ROWS + 2 * HALO
LANES = 256
QUERY_ROWS = 4
KEY_ROWS = QUERY_ROWS + 2 * HALO
BLOCK = 8
BLOCKS = LONGITUDES // BLOCK
KEYS = KEY_ROWS * BLOCK
MASKED = -1e30


def nn(a, b):
    return lax.dot_general(a, b, (((1,), (0,)), ((), ())), preferred_element_type=jnp.float32)


def nt(a, b):
    return lax.dot_general(a, b, (((1,), (1,)), ((), ())), preferred_element_type=jnp.float32)


def attention_kernel(
    heads,
    cells,
    qkv, go, kv_top, kv_bot,
    outq, dkv_own, dkv_top, dkv_bot,
    k_s, v_s, kt_s, vt_s, dk_s, dv_s, live_s, near_s,
):
    feats = heads * HEAD_WIDTH
    tile_cols = LANES // heads // QUERY_ROWS
    tile_queries = QUERY_ROWS * tile_cols
    window = tile_cols // BLOCK + 2

    def load_pair(p, carry):
        cols = pl.ds(pl.multiple_of(p * 16, 16), 16)
        for first, rows_s, turned_s in ((0, k_s, kt_s), (feats, v_s, vt_s)):
            both = jnp.concatenate([
                kv_top[:, cols, first:first + feats].astype(jnp.float32),
                qkv[:, cols, feats + first:2 * feats + first].astype(jnp.float32),
                kv_bot[:, cols, first:first + feats].astype(jnp.float32),
            ], axis=0)
            for half in range(2):
                block = both[:, 8 * half:8 * half + 8, :].reshape(EXT_ROWS * BLOCK, feats)
                rows_s[2 * p + half] = block.astype(jnp.bfloat16)
                for upper in range(2):
                    low = upper * QUERY_ROWS * BLOCK
                    turned_s[upper, 2 * p + half] = block[low:low + KEYS].T.astype(jnp.bfloat16)
        for half in range(2):
            col = (2 * p + half) * BLOCK + lax.broadcasted_iota(jnp.int32, (BLOCK, 128), 0)
            for row in range(EXT_ROWS):
                live_s[2 * p + half, row * BLOCK:(row + 1) * BLOCK, :] = jnp.where(col < cells[row], 0.0, MASKED)
        return carry

    lax.fori_loop(0, BLOCKS // 2, load_pair, 0)
    dk_s[...] = jnp.zeros_like(dk_s)
    dv_s[...] = jnp.zeros_like(dv_s)

    lane = lax.broadcasted_iota(jnp.int32, (KEYS, LANES), 1) % tile_queries
    query_row = lane // tile_cols
    query_col = lane % tile_cols
    key = lax.broadcasted_iota(jnp.int32, (KEYS, LANES), 0)
    row_gap = key // BLOCK - query_row
    for j in range(window):
        col_gap = (j - 1) * BLOCK + key % BLOCK - query_col
        near = (row_gap >= 0) & (row_gap <= 2 * HALO) & (col_gap >= -HALO) & (col_gap <= HALO)
        near_s[j] = jnp.where(near, 0.0, MASKED)

    own_head = (
        lax.broadcasted_iota(jnp.int32, (LANES, feats), 0) // tile_queries
        == lax.broadcasted_iota(jnp.int32, (LANES, feats), 1) // HEAD_WIDTH
    )
    own_head_turned = (
        lax.broadcasted_iota(jnp.int32, (feats, LANES), 1) // tile_queries
        == lax.broadcasted_iota(jnp.int32, (feats, LANES), 0) // HEAD_WIDTH
    )
    query_lane = lax.broadcasted_iota(jnp.int32, (1, LANES), 1) % tile_queries

    def spread(ref, upper, cols):
        tile = ref[upper * QUERY_ROWS:(upper + 1) * QUERY_ROWS, cols, :feats].reshape(tile_queries, feats)
        if heads == 1:
            return tile
        stacked = jnp.concatenate([tile] * heads, axis=0)
        return jnp.where(own_head, stacked, jnp.zeros_like(stacked))

    def gather(turned):
        if heads == 1:
            tile = turned.T
        else:
            tall = jnp.where(own_head_turned, turned, 0.0).T
            tile = sum(tall[h * tile_queries:(h + 1) * tile_queries] for h in range(heads))
        return tile.astype(jnp.bfloat16).reshape(QUERY_ROWS, tile_cols, feats)

    def one_tile(upper, tile):
        start = pl.multiple_of(tile * tile_cols, 16)
        cols = pl.ds(start, tile_cols)
        rows = slice(upper * QUERY_ROWS, (upper + 1) * QUERY_ROWS)
        keys = pl.ds(upper * QUERY_ROWS * BLOCK, KEYS)
        index = [(tile * (tile_cols // BLOCK) + j + BLOCKS - 1) % BLOCKS for j in range(window)]
        queries = spread(qkv, upper, cols)
        grads = spread(go, upper, cols)
        scores = [
            nt(k_s[index[j], keys, :], queries)
            + near_s[j]
            + jnp.concatenate([live_s[index[j], keys, :]] * (LANES // 128), axis=1)
            for j in range(window)
        ]
        highest = jnp.max(functools.reduce(jnp.maximum, scores), axis=0, keepdims=True)
        terms = [jnp.exp(score - highest) for score in scores]
        total = jnp.sum(sum(terms), axis=0, keepdims=True)
        query_cells = jnp.zeros((1, LANES), jnp.int32)
        for row in range(QUERY_ROWS):
            cell = cells[HALO + upper * QUERY_ROWS + row]
            query_cells = jnp.where(query_lane // tile_cols == row, cell, query_cells)
        live = start + query_lane % tile_cols < query_cells
        inverse = jnp.where(live, 1.0 / total, 0.0)
        probs = [term * inverse for term in terms]
        grad_probs = [nt(v_s[index[j], keys, :], grads) for j in range(window)]
        delta = jnp.sum(sum(p * g for p, g in zip(probs, grad_probs)), axis=0, keepdims=True)
        weights = [p.astype(jnp.bfloat16) for p in probs]
        grad_scores = [(p * (g - delta)).astype(jnp.bfloat16) for p, g in zip(probs, grad_probs)]
        for j in range(window):
            dv_s[index[j], keys, :] += nn(weights[j], grads)
            dk_s[index[j], keys, :] += nn(grad_scores[j], queries)
        values_turned = jnp.concatenate([vt_s[upper, index[j]] for j in range(window)], axis=1)
        keys_turned = jnp.concatenate([kt_s[upper, index[j]] for j in range(window)], axis=1)
        outq[rows, cols, :feats] = gather(nn(values_turned, jnp.concatenate(weights, axis=0)))
        outq[rows, cols, feats:] = gather(nn(keys_turned, jnp.concatenate(grad_scores, axis=0)))

    def tile_pair(tile, carry):
        for upper in range(2):
            one_tile(upper, tile)
        return carry

    lax.fori_loop(0, LONGITUDES // tile_cols, tile_pair, 0)

    def store_pair(p, carry):
        cols = pl.ds(pl.multiple_of(p * 16, 16), 16)
        for first, sums in ((0, dk_s), (feats, dv_s)):
            both = jnp.concatenate(
                [sums[2 * p + half].reshape(EXT_ROWS, BLOCK, feats) for half in range(2)], axis=1
            )
            dkv_top[:, cols, first:first + feats] = both[:HALO].astype(jnp.bfloat16)
            dkv_own[:, cols, first:first + feats] = both[HALO:HALO + BAND_ROWS]
            dkv_bot[:, cols, first:first + feats] = both[HALO + BAND_ROWS:].astype(jnp.bfloat16)
        return carry

    lax.fori_loop(0, BLOCKS // 2, store_pair, 0)


def attention(cells, qkv, go, kv_top, kv_bot):
    feats = go.shape[-1]
    heads = feats // HEAD_WIDTH
    window = LANES // heads // QUERY_ROWS // BLOCK + 2
    vmem = pl.BlockSpec(memory_space=pltpu.VMEM)
    grid = lambda rows, kind: jax.ShapeDtypeStruct((rows, LONGITUDES, 2 * feats), kind)
    bf16, f32 = jnp.bfloat16, jnp.float32
    pairs = BAND_ROWS * LONGITUDES * heads * KEYS * window
    return pl.pallas_call(
        functools.partial(attention_kernel, heads),
        out_shape=(grid(BAND_ROWS, bf16), grid(BAND_ROWS, f32), grid(HALO, bf16), grid(HALO, bf16)),
        in_specs=[pl.BlockSpec(memory_space=pltpu.SMEM)] + [vmem] * 4,
        out_specs=(vmem,) * 4,
        scratch_shapes=[
            pltpu.VMEM((BLOCKS, EXT_ROWS * BLOCK, feats), bf16),
            pltpu.VMEM((BLOCKS, EXT_ROWS * BLOCK, feats), bf16),
            pltpu.VMEM((2, BLOCKS, feats, KEYS), bf16),
            pltpu.VMEM((2, BLOCKS, feats, KEYS), bf16),
            pltpu.VMEM((BLOCKS, EXT_ROWS * BLOCK, feats), f32),
            pltpu.VMEM((BLOCKS, EXT_ROWS * BLOCK, feats), f32),
            pltpu.VMEM((BLOCKS, EXT_ROWS * BLOCK, 128), f32),
            pltpu.VMEM((window, KEYS, LANES), f32),
        ],
        compiler_params=pltpu.CompilerParams(vmem_limit_bytes=60 * 2**20),
        cost_estimate=pl.CostEstimate(
            flops=12 * pairs * HEAD_WIDTH, transcendentals=pairs, bytes_accessed=20 * 2**20
        ),
    )(cells, qkv, go, kv_top, kv_bot)


from jax.sharding import Mesh, PartitionSpec as P

WIDTH = 1024
GROUP = ("y", "m", "c")


def tn(a, b):
    return lax.dot_general(a, b, (((0,), (0,)), ((), ())), preferred_element_type=jnp.float32)


def to_bands(halves, step):
    dm, dc = step
    place = lambda y, m, c: (y * halves + m) * 2 + c
    return [
        (place(y, m, c), place((c + dc) % 2, (m + dm) % halves, y))
        for y in range(2) for m in range(halves) for c in range(2)
    ]


def passed_along(x, by):
    length = lax.axis_size("z") * 2
    pairs = [(i, i + by) for i in range(length) if 0 <= i + by < length]
    return lax.ppermute(x, ("z", "c"), pairs)


def after(x, *others):
    return lax.optimization_barrier((x, *others))[0]


def on_device(tokens, gain, qkv_weight, out_weight, row_cells, upstream):
    heads = qkv_weight.shape[0]
    feats = heads * HEAD_WIDTH
    band_tokens = BAND_ROWS * LONGITUDES
    chunk = tokens.shape[0]
    halves, layers = lax.axis_size("m"), lax.axis_size("z")
    z, y, m, c = (lax.axis_index(axis) for axis in ("z",) + GROUP)
    steps = [(dm, dc) for dc in range(2) for dm in range(halves)]
    arrives = [((m - dm) % halves) * 2 + (y - dc) % 2 for dm, dc in steps]
    grad_scale = 4.0 / math.sqrt(band_tokens * layers * 2)
    band_start = (z * 2 + c) * BAND_ROWS
    cells = lax.dynamic_slice_in_dim(jnp.pad(row_cells, (HALO, HALO)), band_start, EXT_ROWS)

    def send(x, step):
        return lax.ppermute(x, GROUP, to_bands(halves, step))

    def send_back(x, step):
        return lax.ppermute(x, GROUP, [(b, a) for a, b in to_bands(halves, step)])

    def in_order(parts):
        whole = jnp.zeros((band_tokens,) + parts[0].shape[1:], parts[0].dtype)
        for part, at in zip(parts, arrives):
            whole = lax.dynamic_update_slice_in_dim(whole, part, at * chunk, 0)
        return whole

    def in_steps(whole):
        return [lax.dynamic_slice_in_dim(whole, at * chunk, chunk, 0) for at in arrives]

    def from_ahead(x, dm):
        return lax.ppermute(x, "m", [((i + dm) % halves, i) for i in range(halves)])

    def from_sibling(x):
        return lax.ppermute(x, "c", [(0, 1), (1, 0)])

    out_flat = out_weight.reshape(feats, WIDTH)
    out_mine = jnp.concatenate([out_flat] + [from_ahead(out_flat, dm) for dm in range(1, halves)], axis=0)

    features = tokens.astype(jnp.float32)
    inverse = lax.rsqrt(jnp.mean(features * features, axis=1, keepdims=True) + 1e-06)
    normed = (features * inverse * gain[None, :]).astype(jnp.bfloat16)
    normed_parts = [send(normed, step) for step in steps]

    split = qkv_weight.reshape(heads, 3, HEAD_WIDTH, WIDTH).transpose(1, 0, 2, 3).reshape(3 * feats, WIDTH)
    eighth = jnp.where(jnp.arange(3 * feats) < feats, HEAD_WIDTH ** -0.5, 1.0)[:, None].astype(jnp.bfloat16)
    split = split * eighth
    pairs = [((y * halves + m) * 2 + y, (y * halves + m) * 2 + 1 - y) for y in range(2) for m in range(halves)]
    group_split = jnp.where(c == y, split, lax.ppermute(split, GROUP, pairs))

    out_blocks = jnp.concatenate([out_mine, from_sibling(out_mine)], axis=0)
    grad_heads_own = nt(upstream, out_blocks).astype(jnp.bfloat16)

    qkv = in_order([nt(part, group_split).astype(jnp.bfloat16) for part in normed_parts])
    qkv = qkv.reshape(BAND_ROWS, LONGITUDES, 3 * feats)
    kv_top = passed_along(qkv[BAND_ROWS - HALO:, :, feats:], 1)
    kv_bot = passed_along(qkv[:HALO, :, feats:], -1)
    grad_heads = in_order([
        send(after(grad_heads_own[:, i * feats:(i + 1) * feats], qkv), step) for i, step in enumerate(steps)
    ]).reshape(BAND_ROWS, LONGITUDES, feats)

    held = after(upstream, grad_heads)
    upstream_parts = [send(held, step) for step in steps]
    share = 3 * feats // layers
    held = after(lax.dynamic_slice_in_dim(split, z * share, share, 0), kv_top, kv_bot)
    others = [lax.all_gather(from_ahead(held, dm), "z", axis=0, tiled=True) for dm in range(1, halves)]
    split_mine = jnp.concatenate([split] + others, axis=0)
    split_blocks = jnp.concatenate([split_mine, from_sibling(split_mine)], axis=0)

    outq, dkv, dkv_top, dkv_bot = attention(cells, qkv, grad_heads, kv_top, kv_bot)

    from_above = passed_along(dkv_top, -1)
    from_below = passed_along(dkv_bot, 1)
    outq_parts = in_steps(outq.reshape(band_tokens, 2 * feats))
    outq_own = jnp.concatenate([send_back(part, step) for part, step in zip(outq_parts, steps)], axis=1)
    outq_own = outq_own.reshape(chunk, len(steps), 2, feats)
    out_own = outq_own[:, :, 0].reshape(chunk, len(steps) * feats)
    update = nn(out_own, out_blocks).astype(jnp.bfloat16)

    def reduced(grads):
        pairs = [
            ((1 - y) * halves * 2 + m * 2 + 1 - y, y * halves * 2 + m * 2 + 1 - y)
            for y in range(2) for m in range(halves)
        ]
        return jnp.where(c == y, grads, lax.ppermute(grads, GROUP, pairs)).astype(jnp.float32)

    outq_steps = jnp.concatenate(outq_parts, axis=0)
    normed_steps = jnp.concatenate(normed_parts, axis=0)
    upstream_steps = jnp.concatenate(upstream_parts, axis=0)
    early = jnp.concatenate([tn(outq_steps[:, :feats], upstream_steps), tn(outq_steps[:, feats:], normed_steps)])
    early_sum = lax.psum(early.astype(jnp.bfloat16), ("z", "c"))
    early = reduced(early_sum)
    grad_out = early[:feats] * grad_scale
    grad_query = early[feats:] * (grad_scale * HEAD_WIDTH ** -0.5)

    wide = lambda x, low, high: jnp.pad(x.astype(jnp.float32), ((low, high), (0, 0), (0, 0)))
    dkv = dkv + wide(from_below, 0, BAND_ROWS - HALO) + wide(from_above, BAND_ROWS - HALO, 0)
    dkv_parts = in_steps(dkv.astype(jnp.bfloat16).reshape(band_tokens, 2 * feats))
    dkv_own = [send_back(part, step) for part, step in zip(dkv_parts, steps)]
    grad_normed = 0.0
    for i, part in enumerate(dkv_own):
        block = split_blocks[i * 3 * feats:(i + 1) * 3 * feats]
        grad_normed += nn(outq_own[:, i, 1], block[:feats]) + nn(part, block[feats:])
    centred = features * inverse
    scaled = gain[None, :] * grad_normed
    grad_input = inverse * (scaled - centred * jnp.mean(scaled * centred, axis=1, keepdims=True))

    late = tn(jnp.concatenate(dkv_parts, axis=0), normed_steps).astype(jnp.bfloat16)
    late = reduced(lax.psum(after(late, early_sum), ("z", "c"))) * grad_scale
    by_head = lambda x: x.reshape(heads, HEAD_WIDTH, WIDTH)
    grad_qkv = jnp.concatenate([by_head(grad_query), by_head(late[:feats]), by_head(late[feats:])], axis=1)
    return update, grad_input.astype(jnp.bfloat16), grad_qkv, by_head(grad_out)


def solution(mesh):
    devices = mesh.devices.reshape(mesh.shape["lat"] // 2, 2, mesh.shape["mp"] // 2, 2)
    tokens, weights = P(("z", "y", "m", "c"), None), P(("m", "c"), None, None)
    return jax.shard_map(
        on_device,
        mesh=Mesh(devices, ("z", "y", "m", "c")),
        in_specs=(tokens, P(), weights, weights, P(), tokens),
        out_specs=(tokens, tokens, weights, weights),
        check_vma=False,
    )
```

```python
import functools
import math
import jax
import jax.numpy as jnp
from jax import lax
from jax.experimental import pallas as pl
from jax.experimental.pallas import tpu as pltpu

HEAD_WIDTH = 64
LONGITUDES = 256
BAND_ROWS = 8
HALO = 6
EXT_ROWS = BAND_ROWS + 2 * HALO
LANES = 256
QUERY_ROWS = 4
KEY_ROWS = QUERY_ROWS + 2 * HALO
BLOCK = 8
BLOCKS = LONGITUDES // BLOCK
KEYS = KEY_ROWS * BLOCK
MASKED = -1e30


def nn(a, b):
    return lax.dot_general(a, b, (((1,), (0,)), ((), ())), preferred_element_type=jnp.float32)


def nt(a, b):
    return lax.dot_general(a, b, (((1,), (1,)), ((), ())), preferred_element_type=jnp.float32)


def row_cols(row, start, size):
    return pl.ds(pl.multiple_of(row * LONGITUDES + start, 16), size)


def attention_kernel(
    heads, steps,
    cells, order, qkv, kv_top, kv_bot, *refs,
):
    go_parts, refs = refs[:steps], refs[steps:]
    outq_parts, refs = refs[:steps], refs[steps:]
    dkv_own, dkv_top, dkv_bot, outq, go, k_s, v_s, kt_s, vt_s, dk_s, dv_s, live_s, near_s, sems = refs
    feats = heads * HEAD_WIDTH
    chunk = BAND_ROWS * LONGITUDES // steps
    moves = [
        pltpu.make_async_copy(part, go.at[pl.ds(pl.multiple_of(order[i], 16), chunk)], sems.at[i])
        for i, part in enumerate(go_parts)
    ]
    for move in moves:
        move.start()
    tile_cols = LANES // heads // QUERY_ROWS
    tile_queries = QUERY_ROWS * tile_cols
    window = tile_cols // BLOCK + 2

    def load_pair(p, carry):
        for first, rows_s, turned_s in ((0, k_s, kt_s), (feats, v_s, vt_s)):
            both = jnp.stack(
                [kv_top[row_cols(row, p * 16, 16), first:first + feats] for row in range(HALO)]
                + [qkv[row_cols(row, p * 16, 16), feats + first:2 * feats + first] for row in range(BAND_ROWS)]
                + [kv_bot[row_cols(row, p * 16, 16), first:first + feats] for row in range(HALO)]
            ).astype(jnp.float32)
            for half in range(2):
                block = both[:, 8 * half:8 * half + 8, :].reshape(EXT_ROWS * BLOCK, feats)
                rows_s[2 * p + half] = block.astype(jnp.bfloat16)
                for upper in range(2):
                    low = upper * QUERY_ROWS * BLOCK
                    turned_s[upper, 2 * p + half] = block[low:low + KEYS].T.astype(jnp.bfloat16)
        for half in range(2):
            col = (2 * p + half) * BLOCK + lax.broadcasted_iota(jnp.int32, (BLOCK, 128), 0)
            for row in range(EXT_ROWS):
                live_s[2 * p + half, row * BLOCK:(row + 1) * BLOCK, :] = jnp.where(col < cells[row], 0.0, MASKED)
        return carry

    lax.fori_loop(0, BLOCKS // 2, load_pair, 0)
    dk_s[...] = jnp.zeros_like(dk_s)
    dv_s[...] = jnp.zeros_like(dv_s)

    lane = lax.broadcasted_iota(jnp.int32, (KEYS, LANES), 1) % tile_queries
    query_row = lane // tile_cols
    query_col = lane % tile_cols
    key = lax.broadcasted_iota(jnp.int32, (KEYS, LANES), 0)
    row_gap = key // BLOCK - query_row
    for j in range(window):
        col_gap = (j - 1) * BLOCK + key % BLOCK - query_col
        near = (row_gap >= 0) & (row_gap <= 2 * HALO) & (col_gap >= -HALO) & (col_gap <= HALO)
        near_s[j] = jnp.where(near, 0.0, MASKED)

    own_head = (
        lax.broadcasted_iota(jnp.int32, (LANES, feats), 0) // tile_queries
        == lax.broadcasted_iota(jnp.int32, (LANES, feats), 1) // HEAD_WIDTH
    )
    own_head_turned = (
        lax.broadcasted_iota(jnp.int32, (feats, LANES), 1) // tile_queries
        == lax.broadcasted_iota(jnp.int32, (feats, LANES), 0) // HEAD_WIDTH
    )
    query_lane = lax.broadcasted_iota(jnp.int32, (1, LANES), 1) % tile_queries

    def spread(ref, upper, start):
        tile = jnp.concatenate([
            ref[row_cols(upper * QUERY_ROWS + row, start, tile_cols), :feats] for row in range(QUERY_ROWS)
        ], axis=0)
        if heads == 1:
            return tile
        stacked = jnp.concatenate([tile] * heads, axis=0)
        return jnp.where(own_head, stacked, jnp.zeros_like(stacked))

    def gather(turned):
        if heads == 1:
            tile = turned.T
        else:
            tall = jnp.where(own_head_turned, turned, 0.0).T
            tile = sum(tall[h * tile_queries:(h + 1) * tile_queries] for h in range(heads))
        return tile.astype(jnp.bfloat16)

    def one_tile(upper, tile):
        start = pl.multiple_of(tile * tile_cols, 16)
        keys = pl.ds(upper * QUERY_ROWS * BLOCK, KEYS)
        index = [(tile * (tile_cols // BLOCK) + j + BLOCKS - 1) % BLOCKS for j in range(window)]
        queries = spread(qkv, upper, start)
        grads = spread(go, upper, start)
        scores = [
            nt(k_s[index[j], keys, :], queries)
            + near_s[j]
            + jnp.concatenate([live_s[index[j], keys, :]] * (LANES // 128), axis=1)
            for j in range(window)
        ]
        highest = jnp.max(functools.reduce(jnp.maximum, scores), axis=0, keepdims=True)
        terms = [jnp.exp(score - highest) for score in scores]
        total = jnp.sum(sum(terms), axis=0, keepdims=True)
        query_cells = jnp.zeros((1, LANES), jnp.int32)
        for row in range(QUERY_ROWS):
            cell = cells[HALO + upper * QUERY_ROWS + row]
            query_cells = jnp.where(query_lane // tile_cols == row, cell, query_cells)
        live = start + query_lane % tile_cols < query_cells
        inverse = jnp.where(live, 1.0 / total, 0.0)
        probs = [term * inverse for term in terms]
        grad_probs = [nt(v_s[index[j], keys, :], grads) for j in range(window)]
        delta = jnp.sum(sum(p * g for p, g in zip(probs, grad_probs)), axis=0, keepdims=True)
        weights = [p.astype(jnp.bfloat16) for p in probs]
        grad_scores = [(p * (g - delta)).astype(jnp.bfloat16) for p, g in zip(probs, grad_probs)]
        for j in range(window):
            dv_s[index[j], keys, :] += nn(weights[j], grads)
            dk_s[index[j], keys, :] += nn(grad_scores[j], queries)
        values_turned = jnp.concatenate([vt_s[upper, index[j]] for j in range(window)], axis=1)
        keys_turned = jnp.concatenate([kt_s[upper, index[j]] for j in range(window)], axis=1)
        heads_out = gather(nn(values_turned, jnp.concatenate(weights, axis=0)))
        grad_query = gather(nn(keys_turned, jnp.concatenate(grad_scores, axis=0)))
        for row in range(QUERY_ROWS):
            at = row_cols(upper * QUERY_ROWS + row, start, tile_cols)
            outq[at, :feats] = heads_out[row * tile_cols:(row + 1) * tile_cols]
            outq[at, feats:] = grad_query[row * tile_cols:(row + 1) * tile_cols]

    def tile_pair(tile, carry):
        for upper in range(2):
            one_tile(upper, tile)
        return carry

    for move in moves:
        move.wait()
    lax.fori_loop(0, LONGITUDES // tile_cols, tile_pair, 0)
    moves = [
        pltpu.make_async_copy(outq.at[pl.ds(pl.multiple_of(order[i], 16), chunk)], part, sems.at[i])
        for i, part in enumerate(outq_parts)
    ]
    for move in moves:
        move.start()

    def store_pair(p, carry):
        for first, sums in ((0, dk_s), (feats, dv_s)):
            both = jnp.concatenate(
                [sums[2 * p + half].reshape(EXT_ROWS, BLOCK, feats) for half in range(2)], axis=1
            )
            for row in range(HALO):
                dkv_top[row_cols(row, p * 16, 16), first:first + feats] = both[row].astype(jnp.bfloat16)
                dkv_bot[row_cols(row, p * 16, 16), first:first + feats] = (
                    both[HALO + BAND_ROWS + row].astype(jnp.bfloat16)
                )
            for row in range(BAND_ROWS):
                dkv_own[row_cols(row, p * 16, 16), first:first + feats] = both[HALO + row]
        return carry

    lax.fori_loop(0, BLOCKS // 2, store_pair, 0)
    for move in moves:
        move.wait()


VMEM = pl.BlockSpec(memory_space=pltpu.VMEM)
SMEM = pl.BlockSpec(memory_space=pltpu.SMEM)
HBM = pl.BlockSpec(memory_space=pl.ANY)
BF16, F32 = jnp.bfloat16, jnp.float32


def shape(rows, cols, kind=BF16):
    return jax.ShapeDtypeStruct((rows, cols), kind)


def call(kernel, out_shape, in_specs, out_specs, args, flops, scratch=(), transcendentals=0):
    moved = sum(x.size * x.dtype.itemsize for x in (*args, *out_shape))
    return pl.pallas_call(
        kernel,
        out_shape=tuple(out_shape),
        in_specs=list(in_specs),
        out_specs=tuple(out_specs),
        scratch_shapes=list(scratch),
        compiler_params=pltpu.CompilerParams(vmem_limit_bytes=60 * 2**20),
        cost_estimate=pl.CostEstimate(
            flops=flops, transcendentals=transcendentals, bytes_accessed=moved
        ),
    )(*args)


def attention(cells, order, qkv, kv_top, kv_bot, go_parts):
    steps, feats = len(go_parts), go_parts[0].shape[-1]
    heads = feats // HEAD_WIDTH
    window = LANES // heads // QUERY_ROWS // BLOCK + 2
    band, halo, chunk = BAND_ROWS * LONGITUDES, HALO * LONGITUDES, go_parts[0].shape[0]
    pairs = band * heads * KEYS * window
    results = call(
        functools.partial(attention_kernel, heads, steps),
        [shape(chunk, 2 * feats)] * steps
        + [shape(band, 2 * feats, F32), shape(halo, 2 * feats), shape(halo, 2 * feats)],
        [SMEM, SMEM, VMEM, VMEM, VMEM] + [HBM] * steps,
        [HBM] * steps + [VMEM] * 3,
        (cells, order, qkv, kv_top, kv_bot, *go_parts),
        flops=12 * pairs * HEAD_WIDTH * heads,
        transcendentals=pairs,
        scratch=[
            pltpu.VMEM((band, 2 * feats), BF16),
            pltpu.VMEM((band, feats), BF16),
            pltpu.VMEM((BLOCKS, EXT_ROWS * BLOCK, feats), BF16),
            pltpu.VMEM((BLOCKS, EXT_ROWS * BLOCK, feats), BF16),
            pltpu.VMEM((2, BLOCKS, feats, KEYS), BF16),
            pltpu.VMEM((2, BLOCKS, feats, KEYS), BF16),
            pltpu.VMEM((BLOCKS, EXT_ROWS * BLOCK, feats), F32),
            pltpu.VMEM((BLOCKS, EXT_ROWS * BLOCK, feats), F32),
            pltpu.VMEM((BLOCKS, EXT_ROWS * BLOCK, 128), F32),
            pltpu.VMEM((window, KEYS, LANES), F32),
            pltpu.SemaphoreType.DMA((steps,)),
        ],
    )
    return (results[:steps], *results[steps:])


def norm_kernel(tokens, gain, normed):
    features = tokens[...].astype(F32)
    inverse = lax.rsqrt(jnp.mean(features * features, axis=1, keepdims=True) + 1e-06)
    normed[...] = (features * inverse * gain[...]).astype(BF16)


def norm(tokens, gain):
    return call(
        norm_kernel, [shape(*tokens.shape)], [VMEM] * 2, [VMEM], (tokens, gain[None, :]), flops=4 * tokens.size
    )[0]


def grad_heads_kernel(steps, upstream, *refs):
    for block, out in zip(refs[:steps], refs[steps:]):
        out[...] = nt(upstream[...], block[...]).astype(BF16)


def grad_heads_parts(upstream, blocks):
    steps, feats = len(blocks), blocks[0].shape[0]
    return call(
        functools.partial(grad_heads_kernel, steps),
        [shape(upstream.shape[0], feats)] * steps,
        [VMEM] * (1 + steps), [VMEM] * steps, (upstream, *blocks),
        flops=2 * steps * feats * upstream.size,
    )


def projection_kernel(steps, feats, order, weight, *refs):
    parts, (qkv, kv_up, kv_down, held, sems) = refs[:steps], refs[steps:]
    chunk = held.shape[1]
    moves = [pltpu.make_async_copy(part, held.at[i], sems.at[i]) for i, part in enumerate(parts)]
    for move in moves:
        move.start()
    for i, move in enumerate(moves):
        move.wait()
        at = pl.ds(pl.multiple_of(order[i], 16), chunk)
        for first in range(0, 3 * feats, feats):
            qkv[at, first:first + feats] = nt(held[i], weight[first:first + feats, :]).astype(BF16)
    kv_up[...] = qkv[(BAND_ROWS - HALO) * LONGITUDES:, feats:]
    kv_down[...] = qkv[:HALO * LONGITUDES, feats:]


def projections(order, weight, parts):
    steps, feats = len(parts), weight.shape[0] // 3
    chunk, width = parts[0].shape
    band, halo = BAND_ROWS * LONGITUDES, HALO * LONGITUDES
    return call(
        functools.partial(projection_kernel, steps, feats),
        [shape(band, 3 * feats), shape(halo, 2 * feats), shape(halo, 2 * feats)],
        [SMEM, VMEM] + [HBM] * steps, [VMEM] * 3, (order, weight, *parts),
        flops=2 * band * weight.size,
        scratch=[pltpu.VMEM((steps, chunk, width), BF16), pltpu.SemaphoreType.DMA((steps,))],
    )


def join_kernel(steps, order, own, above, below, *refs):
    parts, (whole, sems) = refs[:steps], refs[steps:]
    chunk = parts[0].shape[0]
    low, high = (BAND_ROWS - HALO) * LONGITUDES, HALO * LONGITUDES
    whole[:low] = (own[:low] + below[:low].astype(F32)).astype(BF16)
    whole[low:high] = (own[low:high] + below[low:].astype(F32) + above[:high - low].astype(F32)).astype(BF16)
    whole[high:] = (own[high:] + above[high - low:].astype(F32)).astype(BF16)
    moves = [
        pltpu.make_async_copy(whole.at[pl.ds(pl.multiple_of(order[i], 16), chunk)], part, sems.at[i])
        for i, part in enumerate(parts)
    ]
    for move in moves:
        move.start()
    for move in moves:
        move.wait()


def joined(order, own, above, below, steps):
    band, feats = own.shape
    return call(
        functools.partial(join_kernel, steps),
        [shape(band // steps, feats)] * steps,
        [SMEM] + [VMEM] * 3, [HBM] * steps, (order, own, above, below), flops=2 * own.size,
        scratch=[pltpu.VMEM((band, feats), BF16), pltpu.SemaphoreType.DMA((steps,))],
    )


def weight_grad_kernel(steps, sides, core, *refs):
    lefts, refs = refs[:steps], refs[steps:]
    rights, (keep, give, sums) = [refs[i * steps:(i + 1) * steps] for i in range(sides)], refs[sides * steps:]
    feats = sums.shape[0] // sides
    for side, parts in enumerate(rights):
        at = slice(side * feats, (side + 1) * feats)
        for i, (left, right) in enumerate(zip(lefts, parts)):
            product = lax.dot_general(
                left[:, at], right[...], (((0,), (0,)), ((), ())), preferred_element_type=F32
            )
            sums[at, :] = product if i == 0 else sums[at, :] + product
    half = sums.shape[0] // 2
    mine, other = (pl.ds(pl.multiple_of(at * half, 16), half) for at in (core[0], 1 - core[0]))
    keep[...] = sums[mine, :]
    give[...] = sums[other, :].astype(BF16)


def weight_grad(core, lefts, *rights):
    steps, width = len(lefts), rights[0][0].shape[1]
    rows = lefts[0].shape[1]
    args = (core, *lefts, *(part for parts in rights for part in parts))
    return call(
        functools.partial(weight_grad_kernel, steps, len(rights)),
        [shape(rows // 2, width, F32), shape(rows // 2, width)],
        [SMEM] + [VMEM] * (len(args) - 1), [VMEM] * 2, args,
        flops=2 * steps * lefts[0].size * width,
        scratch=[pltpu.VMEM((rows, width), F32)],
    )


def update_kernel(steps, *refs):
    out = refs[-1]
    feats = refs[steps].shape[0]
    out[...] = sum(nn(part[:, :feats], block[...]) for part, block in zip(refs[:steps], refs[steps:])).astype(BF16)


def updates(outq_own, blocks):
    steps, (feats, width) = len(blocks), blocks[0].shape
    chunk = outq_own[0].shape[0]
    return call(
        functools.partial(update_kernel, steps), [shape(chunk, width)], [VMEM] * (2 * steps), [VMEM],
        (*outq_own, *blocks), flops=2 * steps * chunk * feats * width,
    )[0]


def grad_input_kernel(steps, tokens, gain, *refs):
    outq, dkv, blocks, grad = refs[:steps], refs[steps:2 * steps], refs[2 * steps:3 * steps], refs[-1]
    feats = blocks[0].shape[0] // 3
    grad_normed = sum(
        nn(outq[i][:, feats:], blocks[i][:feats, :]) + nn(dkv[i][...], blocks[i][feats:, :]) for i in range(steps)
    )
    features = tokens[...].astype(F32)
    inverse = lax.rsqrt(jnp.mean(features * features, axis=1, keepdims=True) + 1e-06)
    centred = features * inverse
    scaled = gain[...] * grad_normed
    grad[...] = (inverse * (scaled - centred * jnp.mean(scaled * centred, axis=1, keepdims=True))).astype(BF16)


def grad_inputs(tokens, gain, outq_own, dkv_own, blocks):
    steps = len(blocks)
    return call(
        functools.partial(grad_input_kernel, steps), [shape(*tokens.shape)], [VMEM] * (2 + 3 * steps), [VMEM],
        (tokens, gain[None, :], *outq_own, *dkv_own, *blocks),
        flops=2 * steps * tokens.shape[0] * blocks[0].size,
    )[0]


from jax.sharding import Mesh, PartitionSpec as P

WIDTH = 1024
GROUP = ("y", "m", "c")


def to_bands(halves, step):
    dm, dc = step
    place = lambda y, m, c: (y * halves + m) * 2 + c
    return [
        (place(y, m, c), place((c + dc) % 2, (m + dm) % halves, y))
        for y in range(2) for m in range(halves) for c in range(2)
    ]


def passed_along(x, by):
    length = lax.axis_size("z") * 2
    pairs = [(i, i + by) for i in range(length) if 0 <= i + by < length]
    return lax.ppermute(x, ("z", "c"), pairs)


def after(x, *others):
    return lax.optimization_barrier((x, *others))[0]


def on_device(tokens, gain, qkv_weight, out_weight, row_cells, upstream):
    heads = qkv_weight.shape[0]
    feats = heads * HEAD_WIDTH
    band_tokens = BAND_ROWS * LONGITUDES
    chunk = tokens.shape[0]
    halves, layers = lax.axis_size("m"), lax.axis_size("z")
    z, y, m, c = (lax.axis_index(axis) for axis in ("z",) + GROUP)
    core = jnp.reshape(c, (1,))
    steps = [(dm, dc) for dc in range(2) for dm in range(halves)]
    order = jnp.stack([((m - dm) % halves) * 2 + (y - dc) % 2 for dm, dc in steps]) * chunk
    grad_scale = 4.0 / math.sqrt(band_tokens * layers * 2)
    band_start = (z * 2 + c) * BAND_ROWS
    cells = lax.dynamic_slice_in_dim(jnp.pad(row_cells, (HALO, HALO)), band_start, EXT_ROWS)

    def send(parts):
        return [lax.ppermute(x, GROUP, to_bands(halves, step)) for x, step in zip(parts, steps)]

    def send_back(parts):
        return [
            lax.ppermute(x, GROUP, [(b, a) for a, b in to_bands(halves, step)]) for x, step in zip(parts, steps)
        ]

    def from_ahead(x, dm):
        return lax.ppermute(x, "m", [((i + dm) % halves, i) for i in range(halves)])

    def from_sibling(x):
        return lax.ppermute(x, "c", [(0, 1), (1, 0)])

    out_blocks = [out_weight.reshape(feats, WIDTH)]
    out_blocks += [from_ahead(out_blocks[0], dm) for dm in range(1, halves)]
    normed_parts = send([norm(tokens, gain)] * len(steps))
    out_blocks += [from_sibling(block) for block in out_blocks]

    split = qkv_weight.reshape(heads, 3, HEAD_WIDTH, WIDTH).transpose(1, 0, 2, 3).reshape(3 * feats, WIDTH)
    eighth = jnp.where(jnp.arange(3 * feats) < feats, HEAD_WIDTH ** -0.5, 1.0)[:, None].astype(BF16)
    split = split * eighth
    sibling_split = from_sibling(split)
    grad_heads_own = grad_heads_parts(upstream, out_blocks)

    qkv, kv_up, kv_down = projections(order, jnp.where(c == y, split, sibling_split), normed_parts)
    kv_top, kv_bot = passed_along(kv_up, 1), passed_along(kv_down, -1)
    grad_heads = send([after(part, qkv) for part in grad_heads_own])

    upstream_parts = send([after(upstream, *grad_heads)] * len(steps))
    share = 3 * feats // layers
    held = after(lax.dynamic_slice_in_dim(split, z * share, share, 0), kv_top, kv_bot)
    split_blocks = [split]
    split_blocks += [lax.all_gather(from_ahead(held, dm), "z", axis=0, tiled=True) for dm in range(1, halves)]
    split_blocks += [sibling_split] + [from_sibling(block) for block in split_blocks[1:]]

    outq_parts, dkv, dkv_top, dkv_bot = attention(cells, order, qkv, kv_top, kv_bot, grad_heads)

    from_above, from_below = passed_along(dkv_top, -1), passed_along(dkv_bot, 1)
    outq_own = send_back(outq_parts)
    early = weight_grad(core, outq_parts, upstream_parts, normed_parts)
    dkv_parts = joined(order, dkv, from_above, from_below, len(steps))
    dkv_own = send_back(dkv_parts)
    late = weight_grad(core, dkv_parts, normed_parts)

    update = updates(outq_own, out_blocks)
    grad_input = grad_inputs(tokens, gain, outq_own, dkv_own, split_blocks)

    def reduced(keep, give):
        both = (keep + from_sibling(give).astype(F32)).astype(BF16)
        return lax.psum(both, "z")

    def spread(half):
        other = from_sibling(half)
        whole = jnp.concatenate([jnp.where(c == 0, half, other), jnp.where(c == 0, other, half)], axis=0)
        pairs = [
            ((1 - y) * halves * 2 + m * 2 + 1 - y, y * halves * 2 + m * 2 + 1 - y)
            for y in range(2) for m in range(halves)
        ]
        return jnp.where(c == y, whole, lax.ppermute(whole, GROUP, pairs)).astype(F32)

    early_half = reduced(*early)
    late_half = reduced(after(late[0], early_half), late[1])
    early, late = spread(early_half), spread(late_half) * grad_scale
    by_head = lambda x: x.reshape(heads, HEAD_WIDTH, WIDTH)
    grad_out = by_head(early[:feats] * grad_scale)
    grad_query = early[feats:] * (grad_scale * HEAD_WIDTH ** -0.5)
    grad_qkv = jnp.concatenate([by_head(grad_query), by_head(late[:feats]), by_head(late[feats:])], axis=1)
    return update, grad_input, grad_qkv, grad_out


def solution(mesh):
    devices = mesh.devices.reshape(mesh.shape["lat"] // 2, 2, mesh.shape["mp"] // 2, 2)
    tokens, weights = P(("z", "y", "m", "c"), None), P(("m", "c"), None, None)
    return jax.shard_map(
        on_device,
        mesh=Mesh(devices, ("z", "y", "m", "c")),
        in_specs=(tokens, P(), weights, weights, P(), tokens),
        out_specs=(tokens, tokens, weights, weights),
        check_vma=False,
    )
```

```python
import functools
import math
import jax
import jax.numpy as jnp
from jax import lax
from jax.experimental import pallas as pl
from jax.experimental.pallas import tpu as pltpu

HEAD_WIDTH = 64
LONGITUDES = 256
BAND_ROWS = 8
HALO = 6
EXT_ROWS = BAND_ROWS + 2 * HALO
LANES = 256
QUERY_ROWS = 4
KEY_ROWS = QUERY_ROWS + 2 * HALO
BLOCK = 8
BLOCKS = LONGITUDES // BLOCK
KEYS = KEY_ROWS * BLOCK
MASKED = -1e30


def nn(a, b):
    return lax.dot_general(a, b, (((1,), (0,)), ((), ())), preferred_element_type=jnp.float32)


def nt(a, b):
    return lax.dot_general(a, b, (((1,), (1,)), ((), ())), preferred_element_type=jnp.float32)


def row_cols(row, start, size):
    return pl.ds(pl.multiple_of(row * LONGITUDES + start, 16), size)


def attention_kernel(
    heads, steps,
    cells, order, qkv, kv_top, kv_bot, weight, *refs,
):
    upstream, refs = refs[:steps], refs[steps:]
    outq_parts, refs = refs[:steps], refs[steps:]
    dkv_own, dkv_top, dkv_bot, held, outq, go, k_s, v_s, kt_s, vt_s, dk_s, dv_s, live_s, near_s, sems = refs
    feats = heads * HEAD_WIDTH
    chunk = BAND_ROWS * LONGITUDES // steps
    moves = [
        pltpu.make_async_copy(part, held.at[i], sems.at[i]) for i, part in enumerate(upstream)
    ]
    for move in moves:
        move.start()
    tile_cols = LANES // heads // QUERY_ROWS
    tile_queries = QUERY_ROWS * tile_cols
    window = tile_cols // BLOCK + 2

    def load_pair(p, carry):
        for first, rows_s, turned_s in ((0, k_s, kt_s), (feats, v_s, vt_s)):
            both = jnp.stack(
                [kv_top[row_cols(row, p * 16, 16), first:first + feats] for row in range(HALO)]
                + [qkv[row_cols(row, p * 16, 16), feats + first:2 * feats + first] for row in range(BAND_ROWS)]
                + [kv_bot[row_cols(row, p * 16, 16), first:first + feats] for row in range(HALO)]
            ).astype(jnp.float32)
            for half in range(2):
                block = both[:, 8 * half:8 * half + 8, :].reshape(EXT_ROWS * BLOCK, feats)
                rows_s[2 * p + half] = block.astype(jnp.bfloat16)
                for upper in range(2):
                    low = upper * QUERY_ROWS * BLOCK
                    turned_s[upper, 2 * p + half] = block[low:low + KEYS].T.astype(jnp.bfloat16)
        for half in range(2):
            col = (2 * p + half) * BLOCK + lax.broadcasted_iota(jnp.int32, (BLOCK, 128), 0)
            for row in range(EXT_ROWS):
                live_s[2 * p + half, row * BLOCK:(row + 1) * BLOCK, :] = jnp.where(col < cells[row], 0.0, MASKED)
        return carry

    lax.fori_loop(0, BLOCKS // 2, load_pair, 0)
    dk_s[...] = jnp.zeros_like(dk_s)
    dv_s[...] = jnp.zeros_like(dv_s)

    lane = lax.broadcasted_iota(jnp.int32, (KEYS, LANES), 1) % tile_queries
    query_row = lane // tile_cols
    query_col = lane % tile_cols
    key = lax.broadcasted_iota(jnp.int32, (KEYS, LANES), 0)
    row_gap = key // BLOCK - query_row
    for j in range(window):
        col_gap = (j - 1) * BLOCK + key % BLOCK - query_col
        near = (row_gap >= 0) & (row_gap <= 2 * HALO) & (col_gap >= -HALO) & (col_gap <= HALO)
        near_s[j] = jnp.where(near, 0.0, MASKED)

    own_head = (
        lax.broadcasted_iota(jnp.int32, (LANES, feats), 0) // tile_queries
        == lax.broadcasted_iota(jnp.int32, (LANES, feats), 1) // HEAD_WIDTH
    )
    own_head_turned = (
        lax.broadcasted_iota(jnp.int32, (feats, LANES), 1) // tile_queries
        == lax.broadcasted_iota(jnp.int32, (feats, LANES), 0) // HEAD_WIDTH
    )
    query_lane = lax.broadcasted_iota(jnp.int32, (1, LANES), 1) % tile_queries

    def spread(ref, upper, start):
        tile = jnp.concatenate([
            ref[row_cols(upper * QUERY_ROWS + row, start, tile_cols), :feats] for row in range(QUERY_ROWS)
        ], axis=0)
        if heads == 1:
            return tile
        stacked = jnp.concatenate([tile] * heads, axis=0)
        return jnp.where(own_head, stacked, jnp.zeros_like(stacked))

    def gather(turned):
        if heads == 1:
            tile = turned.T
        else:
            tall = jnp.where(own_head_turned, turned, 0.0).T
            tile = sum(tall[h * tile_queries:(h + 1) * tile_queries] for h in range(heads))
        return tile.astype(jnp.bfloat16)

    def one_tile(upper, tile):
        start = pl.multiple_of(tile * tile_cols, 16)
        keys = pl.ds(upper * QUERY_ROWS * BLOCK, KEYS)
        index = [(tile * (tile_cols // BLOCK) + j + BLOCKS - 1) % BLOCKS for j in range(window)]
        queries = spread(qkv, upper, start)
        grads = spread(go, upper, start)
        scores = [
            nt(k_s[index[j], keys, :], queries)
            + near_s[j]
            + jnp.concatenate([live_s[index[j], keys, :]] * (LANES // 128), axis=1)
            for j in range(window)
        ]
        highest = jnp.max(functools.reduce(jnp.maximum, scores), axis=0, keepdims=True)
        terms = [jnp.exp(score - highest) for score in scores]
        total = jnp.sum(sum(terms), axis=0, keepdims=True)
        query_cells = jnp.zeros((1, LANES), jnp.int32)
        for row in range(QUERY_ROWS):
            cell = cells[HALO + upper * QUERY_ROWS + row]
            query_cells = jnp.where(query_lane // tile_cols == row, cell, query_cells)
        live = start + query_lane % tile_cols < query_cells
        inverse = jnp.where(live, 1.0 / total, 0.0)
        probs = [term * inverse for term in terms]
        grad_probs = [nt(v_s[index[j], keys, :], grads) for j in range(window)]
        delta = jnp.sum(sum(p * g for p, g in zip(probs, grad_probs)), axis=0, keepdims=True)
        weights = [p.astype(jnp.bfloat16) for p in probs]
        grad_scores = [(p * (g - delta)).astype(jnp.bfloat16) for p, g in zip(probs, grad_probs)]
        for j in range(window):
            dv_s[index[j], keys, :] += nn(weights[j], grads)
            dk_s[index[j], keys, :] += nn(grad_scores[j], queries)
        values_turned = jnp.concatenate([vt_s[upper, index[j]] for j in range(window)], axis=1)
        keys_turned = jnp.concatenate([kt_s[upper, index[j]] for j in range(window)], axis=1)
        heads_out = gather(nn(values_turned, jnp.concatenate(weights, axis=0)))
        grad_query = gather(nn(keys_turned, jnp.concatenate(grad_scores, axis=0)))
        for row in range(QUERY_ROWS):
            at = row_cols(upper * QUERY_ROWS + row, start, tile_cols)
            outq[at, :feats] = heads_out[row * tile_cols:(row + 1) * tile_cols]
            outq[at, feats:] = grad_query[row * tile_cols:(row + 1) * tile_cols]

    def tile_pair(tile, carry):
        for upper in range(2):
            one_tile(upper, tile)
        return carry

    for i, move in enumerate(moves):
        move.wait()
        go[pl.ds(pl.multiple_of(order[i], 16), chunk)] = nt(held[i], weight[...]).astype(jnp.bfloat16)
    lax.fori_loop(0, LONGITUDES // tile_cols, tile_pair, 0)
    moves = [
        pltpu.make_async_copy(outq.at[pl.ds(pl.multiple_of(order[i], 16), chunk)], part, sems.at[i])
        for i, part in enumerate(outq_parts)
    ]
    for move in moves:
        move.start()

    def store_pair(p, carry):
        for first, sums in ((0, dk_s), (feats, dv_s)):
            both = jnp.concatenate(
                [sums[2 * p + half].reshape(EXT_ROWS, BLOCK, feats) for half in range(2)], axis=1
            )
            for row in range(HALO):
                dkv_top[row_cols(row, p * 16, 16), first:first + feats] = both[row].astype(jnp.bfloat16)
                dkv_bot[row_cols(row, p * 16, 16), first:first + feats] = (
                    both[HALO + BAND_ROWS + row].astype(jnp.bfloat16)
                )
            for row in range(BAND_ROWS):
                dkv_own[row_cols(row, p * 16, 16), first:first + feats] = both[HALO + row]
        return carry

    lax.fori_loop(0, BLOCKS // 2, store_pair, 0)
    for move in moves:
        move.wait()


VMEM = pl.BlockSpec(memory_space=pltpu.VMEM)
SMEM = pl.BlockSpec(memory_space=pltpu.SMEM)
HBM = pl.BlockSpec(memory_space=pl.ANY)
BF16, F32 = jnp.bfloat16, jnp.float32


def shape(rows, cols, kind=BF16):
    return jax.ShapeDtypeStruct((rows, cols), kind)


def call(kernel, out_shape, in_specs, out_specs, args, flops, scratch=(), transcendentals=0):
    moved = sum(x.size * x.dtype.itemsize for x in (*args, *out_shape))
    return pl.pallas_call(
        kernel,
        out_shape=tuple(out_shape),
        in_specs=list(in_specs),
        out_specs=tuple(out_specs),
        scratch_shapes=list(scratch),
        compiler_params=pltpu.CompilerParams(vmem_limit_bytes=60 * 2**20),
        cost_estimate=pl.CostEstimate(
            flops=flops, transcendentals=transcendentals, bytes_accessed=moved
        ),
    )(*args)


def attention(cells, order, qkv, kv_top, kv_bot, weight, upstream):
    steps, (feats, width), chunk = len(upstream), weight.shape, upstream[0].shape[0]
    heads = feats // HEAD_WIDTH
    window = LANES // heads // QUERY_ROWS // BLOCK + 2
    band, halo = BAND_ROWS * LONGITUDES, HALO * LONGITUDES
    pairs = band * heads * KEYS * window
    results = call(
        functools.partial(attention_kernel, heads, steps),
        [shape(chunk, 2 * feats)] * steps
        + [shape(band, 2 * feats, F32), shape(halo, 2 * feats), shape(halo, 2 * feats)],
        [SMEM, SMEM, VMEM, VMEM, VMEM, VMEM] + [HBM] * steps,
        [HBM] * steps + [VMEM] * 3,
        (cells, order, qkv, kv_top, kv_bot, weight, *upstream),
        flops=12 * pairs * HEAD_WIDTH * heads + 2 * band * weight.size,
        transcendentals=pairs,
        scratch=[
            pltpu.VMEM((steps, chunk, width), BF16),
            pltpu.VMEM((band, 2 * feats), BF16),
            pltpu.VMEM((band, feats), BF16),
            pltpu.VMEM((BLOCKS, EXT_ROWS * BLOCK, feats), BF16),
            pltpu.VMEM((BLOCKS, EXT_ROWS * BLOCK, feats), BF16),
            pltpu.VMEM((2, BLOCKS, feats, KEYS), BF16),
            pltpu.VMEM((2, BLOCKS, feats, KEYS), BF16),
            pltpu.VMEM((BLOCKS, EXT_ROWS * BLOCK, feats), F32),
            pltpu.VMEM((BLOCKS, EXT_ROWS * BLOCK, feats), F32),
            pltpu.VMEM((BLOCKS, EXT_ROWS * BLOCK, 128), F32),
            pltpu.VMEM((window, KEYS, LANES), F32),
            pltpu.SemaphoreType.DMA((steps,)),
        ],
    )
    return (results[:steps], *results[steps:])


def norm_kernel(tokens, gain, normed):
    features = tokens[...].astype(F32)
    inverse = lax.rsqrt(jnp.mean(features * features, axis=1, keepdims=True) + 1e-06)
    normed[...] = (features * inverse * gain[...]).astype(BF16)


def norm(tokens, gain):
    return call(
        norm_kernel, [shape(*tokens.shape)], [VMEM] * 2, [VMEM], (tokens, gain[None, :]), flops=4 * tokens.size
    )[0]


def projection_kernel(steps, feats, order, weight, *refs):
    parts, (qkv, kv_up, kv_down, held, sems) = refs[:steps], refs[steps:]
    chunk = held.shape[1]
    moves = [pltpu.make_async_copy(part, held.at[i], sems.at[i]) for i, part in enumerate(parts)]
    for move in moves:
        move.start()
    for i, move in enumerate(moves):
        move.wait()
        at = pl.ds(pl.multiple_of(order[i], 16), chunk)
        for first in range(0, 3 * feats, feats):
            qkv[at, first:first + feats] = nn(held[i], weight[:, first:first + feats]).astype(BF16)
    kv_up[...] = qkv[(BAND_ROWS - HALO) * LONGITUDES:, feats:]
    kv_down[...] = qkv[:HALO * LONGITUDES, feats:]


def projections(order, weight, parts):
    steps, feats = len(parts), weight.shape[1] // 3
    chunk, width = parts[0].shape
    band, halo = BAND_ROWS * LONGITUDES, HALO * LONGITUDES
    return call(
        functools.partial(projection_kernel, steps, feats),
        [shape(band, 3 * feats), shape(halo, 2 * feats), shape(halo, 2 * feats)],
        [SMEM, VMEM] + [HBM] * steps, [VMEM] * 3, (order, weight, *parts),
        flops=2 * band * weight.size,
        scratch=[pltpu.VMEM((steps, chunk, width), BF16), pltpu.SemaphoreType.DMA((steps,))],
    )


def join_kernel(steps, order, own, above, below, *refs):
    parts, (whole, sems) = refs[:steps], refs[steps:]
    chunk = parts[0].shape[0]
    low, high = (BAND_ROWS - HALO) * LONGITUDES, HALO * LONGITUDES
    whole[:low] = (own[:low] + below[:low].astype(F32)).astype(BF16)
    whole[low:high] = (own[low:high] + below[low:].astype(F32) + above[:high - low].astype(F32)).astype(BF16)
    whole[high:] = (own[high:] + above[high - low:].astype(F32)).astype(BF16)
    moves = [
        pltpu.make_async_copy(whole.at[pl.ds(pl.multiple_of(order[i], 16), chunk)], part, sems.at[i])
        for i, part in enumerate(parts)
    ]
    for move in moves:
        move.start()
    for move in moves:
        move.wait()


def joined(order, own, above, below, steps):
    band, feats = own.shape
    return call(
        functools.partial(join_kernel, steps),
        [shape(band // steps, feats)] * steps,
        [SMEM] + [VMEM] * 3, [HBM] * steps, (order, own, above, below), flops=2 * own.size,
        scratch=[pltpu.VMEM((band, feats), BF16), pltpu.SemaphoreType.DMA((steps,))],
    )


def weight_grad_kernel(steps, sides, *refs):
    lefts, refs = refs[:steps], refs[steps:]
    rights, (grad, sums) = [refs[i * steps:(i + 1) * steps] for i in range(sides)], refs[sides * steps:]
    feats = sums.shape[0] // sides
    for side, parts in enumerate(rights):
        at = slice(side * feats, (side + 1) * feats)
        for i, (left, right) in enumerate(zip(lefts, parts)):
            product = lax.dot_general(
                left[:, at], right[...], (((0,), (0,)), ((), ())), preferred_element_type=F32
            )
            if i == 0:
                sums[at, :] = product
            elif i < steps - 1:
                sums[at, :] += product
            else:
                grad[at, :] = (sums[at, :] + product).astype(BF16)


def weight_grad(lefts, *rights):
    steps, width = len(lefts), rights[0][0].shape[1]
    rows = lefts[0].shape[1]
    args = (*lefts, *(part for parts in rights for part in parts))
    return call(
        functools.partial(weight_grad_kernel, steps, len(rights)),
        [shape(rows, width)], [VMEM] * len(args), [VMEM], args,
        flops=2 * steps * lefts[0].size * width,
        scratch=[pltpu.VMEM((rows, width), F32)],
    )[0]


def load_blocks(blocks, held, sems, first):
    rows = held.shape[1]
    moves = [
        pltpu.make_async_copy(block.at[pl.ds(first, rows)], held.at[i], sems.at[i]) for i, block in enumerate(blocks)
    ]
    for move in moves:
        move.start()
    for move in moves:
        move.wait()


def update_kernel(steps, leads, *refs):
    parts, blocks, (out, held, sems) = refs[:steps], refs[steps:2 * steps], refs[2 * steps:]
    feats = held.shape[1]
    load_blocks(blocks, held, sems, 3 * feats)
    out[...] = sum(nn(parts[i][:, :feats], held[leads[i]]) for i in range(steps)).astype(BF16)


def updates(leads, outq_own, blocks):
    steps, (rows, width), chunk = len(blocks), blocks[0].shape, outq_own[0].shape[0]
    return call(
        functools.partial(update_kernel, steps),
        [shape(chunk, width)], [SMEM] + [VMEM] * steps + [HBM] * steps, [VMEM], (leads, *outq_own, *blocks),
        flops=steps * chunk * rows * width // 2,
        scratch=[pltpu.VMEM((steps, rows // 4, width), BF16), pltpu.SemaphoreType.DMA((steps,))],
    )[0]


def grad_input_kernel(steps, leads, tokens, gain, *refs):
    outq, dkv, blocks, (grad, held, sems) = (
        refs[:steps], refs[steps:2 * steps], refs[2 * steps:3 * steps], refs[3 * steps:]
    )
    feats = held.shape[1] // 3
    load_blocks(blocks, held, sems, 0)
    grad_normed = sum(
        nn(outq[i][:, feats:], held[leads[i], :feats, :]) + nn(dkv[i][...], held[leads[i], feats:, :])
        for i in range(steps)
    )
    features = tokens[...].astype(F32)
    inverse = lax.rsqrt(jnp.mean(features * features, axis=1, keepdims=True) + 1e-06)
    centred = features * inverse
    scaled = gain[...] * grad_normed
    grad[...] = (inverse * (scaled - centred * jnp.mean(scaled * centred, axis=1, keepdims=True))).astype(BF16)


def grad_inputs(leads, tokens, gain, outq_own, dkv_own, blocks):
    steps, (rows, width) = len(blocks), blocks[0].shape
    return call(
        functools.partial(grad_input_kernel, steps),
        [shape(*tokens.shape)], [SMEM] + [VMEM] * (2 + 2 * steps) + [HBM] * steps, [VMEM],
        (leads, tokens, gain[None, :], *outq_own, *dkv_own, *blocks),
        flops=steps * tokens.shape[0] * rows * width * 3 // 2,
        scratch=[pltpu.VMEM((steps, rows * 3 // 4, width), BF16), pltpu.SemaphoreType.DMA((steps,))],
    )[0]


from jax.sharding import Mesh, PartitionSpec as P

WIDTH = 1024
GROUP = ("y", "m", "c")


def owners(halves):
    if halves == 2:
        return [
            lambda y, m, c: (c, 1 - m if c == y else m, y),
            lambda y, m, c: (c, 1 - m if c == y else m, 1 - y),
            lambda y, m, c: (c, m if c == y else 1 - m, 1 - y),
            lambda y, m, c: (c, m if c == y else 1 - m, y),
        ]
    return [
        lambda y, m, c, dm=dm, dc=dc: (c, (m + dm) % halves, (y + dc) % 2) for dc in range(2) for dm in range(halves)
    ]


def passed_along(x, by):
    length = lax.axis_size("z") * 2
    pairs = [(i, i + by) for i in range(length) if 0 <= i + by < length]
    return lax.ppermute(x, ("z", "c"), pairs)


def after(x, *others):
    return lax.optimization_barrier((x, *others))[0]


def on_device(tokens, gain, qkv_weight, out_weight, row_cells, upstream):
    heads = qkv_weight.shape[0]
    feats = heads * HEAD_WIDTH
    band_tokens = BAND_ROWS * LONGITUDES
    chunk = tokens.shape[0]
    halves, layers = lax.axis_size("m"), lax.axis_size("z")
    z, y, m, c = (lax.axis_index(axis) for axis in ("z",) + GROUP)
    grad_scale = 4.0 / math.sqrt(band_tokens * layers * 2)
    band_start = (z * 2 + c) * BAND_ROWS
    cells = lax.dynamic_slice_in_dim(jnp.pad(row_cells, (HALO, HALO)), band_start, EXT_ROWS)

    at = lambda y, m, c: (y * halves + m) * 2 + c
    spots = [(y, m, c) for y in range(2) for m in range(halves) for c in range(2)]
    slots = [[owner(*spot) for spot in spots] for owner in owners(halves)]
    here = lambda table: jnp.asarray(table, jnp.int32)[at(y, m, c)]
    order = here([[(slot[i][1] * 2 + slot[i][2]) * chunk for slot in slots] for i in range(len(spots))])

    def lead(slot, spot):
        far = spots[slot.index(spot)]
        return (far[0] - spot[2]) % 2 * halves + (far[1] - spot[1]) % halves

    leads = here([[lead(slot, spot) for slot in slots] for spot in spots])

    def permuted(x, pairs):
        return lax.ppermute(x, GROUP, [(at(*a), at(*b)) for a, b in pairs])

    def send_back(parts):
        return [permuted(x, list(zip(spots, slot))) for x, slot in zip(parts, slots)]

    def gathered(x):
        sent = lambda slot: permuted(x, list(zip(slot, spots)))
        if halves != 2:
            return [sent(slot) for slot in slots]
        first, second = sent(slots[0]), sent(slots[1])
        third = permuted(
            jnp.where(c == y, first, x),
            [(spot, (1 - spot[0], spot[1], spot[0]) if spot[2] == spot[0] else (spot[0], spot[1], spot[0])) for spot in spots],
        )
        fourth = permuted(
            first, [(spot, (spot[0], 1 - spot[1], spot[2])) for spot in spots if spot[2] != spot[0]]
        )
        return [first, second, third, jnp.where(c == y, x, fourth)]

    def from_ahead(x, dm):
        return lax.ppermute(x, "m", [((i + dm) % halves, i) for i in range(halves)])

    def from_sibling(x):
        return lax.ppermute(x, "c", [(0, 1), (1, 0)])

    split = qkv_weight.reshape(heads, 3, HEAD_WIDTH, WIDTH).transpose(1, 0, 2, 3).reshape(3 * feats, WIDTH)
    eighth = jnp.where(jnp.arange(3 * feats) < feats, HEAD_WIDTH ** -0.5, 1.0)[:, None].astype(BF16)
    weight = jnp.concatenate([split * eighth, out_weight.reshape(feats, WIDTH)], axis=0)
    share = 4 * feats // layers
    held = lax.dynamic_slice_in_dim(weight, z * share, share, 0)
    blocks = [weight]
    blocks += [lax.all_gather(from_ahead(held, dm), "z", axis=0, tiled=True) for dm in range(1, halves)]
    blocks += [from_sibling(block) for block in blocks]
    group = jnp.where(c == y, weight, blocks[halves])
    group_qkv, group_out = group[:3 * feats].T, group[3 * feats:]

    *normed_parts, group_qkv, group_out = lax.optimization_barrier(
        (*gathered(norm(tokens, gain)), group_qkv, group_out)
    )
    upstream_parts = gathered(after(upstream, *normed_parts))
    qkv, kv_up, kv_down = projections(order, group_qkv, normed_parts)
    kv_top, kv_bot = passed_along(kv_up, 1), passed_along(kv_down, -1)
    order, *blocks = lax.optimization_barrier((order, *blocks))
    outq_parts, dkv, dkv_top, dkv_bot = attention(cells, order, qkv, kv_top, kv_bot, group_out, upstream_parts)

    from_above, from_below = passed_along(dkv_top, -1), passed_along(dkv_bot, 1)
    outq_own = send_back(outq_parts)
    early = weight_grad(outq_parts, upstream_parts, normed_parts)
    early_sum = lax.psum(early, ("z", "c"))
    dkv_parts = joined(after(order, early), dkv, from_above, from_below, len(slots))
    dkv_own = send_back(dkv_parts)
    late = weight_grad(dkv_parts, normed_parts)
    late_sum = lax.psum(late, ("c", "z"))
    leads, outq_own, dkv_own = lax.optimization_barrier((leads, outq_own, dkv_own))
    update = updates(leads, outq_own, blocks)
    grad_input = grad_inputs(after(leads, late), tokens, gain, outq_own, dkv_own, blocks)

    def spread(grads):
        pairs = [((1 - y, m, 1 - y), (y, m, 1 - y)) for y in range(2) for m in range(halves)]
        return jnp.where(c == y, grads, permuted(grads, pairs)).astype(F32)

    early_sum, grad_input, update = lax.optimization_barrier((early_sum, grad_input, update))
    early, late = spread(early_sum), spread(late_sum) * grad_scale
    by_head = lambda x: x.reshape(heads, HEAD_WIDTH, WIDTH)
    grad_out = by_head(early[:feats] * grad_scale)
    grad_query = early[feats:] * (grad_scale * HEAD_WIDTH ** -0.5)
    grad_qkv = jnp.concatenate([by_head(grad_query), by_head(late[:feats]), by_head(late[feats:])], axis=1)
    return update, grad_input, grad_qkv, grad_out


def solution(mesh):
    devices = mesh.devices.reshape(mesh.shape["lat"] // 2, 2, mesh.shape["mp"] // 2, 2)
    tokens, weights = P(("z", "y", "m", "c"), None), P(("m", "c"), None, None)
    return jax.shard_map(
        on_device,
        mesh=Mesh(devices, ("z", "y", "m", "c")),
        in_specs=(tokens, P(), weights, weights, P(), tokens),
        out_specs=(tokens, tokens, weights, weights),
        check_vma=False,
    )
```

```python
import functools
import math
import jax
import jax.numpy as jnp
from jax import lax
from jax.experimental import pallas as pl
from jax.experimental.pallas import tpu as pltpu

HEAD_WIDTH = 64
LONGITUDES = 256
BAND_ROWS = 8
HALO = 6
EXT_ROWS = BAND_ROWS + 2 * HALO
LANES = 256
QUERY_ROWS = 4
KEY_ROWS = QUERY_ROWS + 2 * HALO
BLOCK = 8
BLOCKS = LONGITUDES // BLOCK
KEYS = KEY_ROWS * BLOCK
MASKED = -1e30


def nn(a, b):
    return lax.dot_general(a, b, (((1,), (0,)), ((), ())), preferred_element_type=jnp.float32)


def nt(a, b):
    return lax.dot_general(a, b, (((1,), (1,)), ((), ())), preferred_element_type=jnp.float32)


def row_cols(row, start, size):
    return pl.ds(pl.multiple_of(row * LONGITUDES + start, 16), size)


def attention_kernel(
    heads, steps,
    cells, order, qkv, kv_top, kv_bot, weight, *refs,
):
    upstream, refs = refs[:steps], refs[steps:]
    outq_parts, refs = refs[:steps], refs[steps:]
    dkv_own, dkv_top, dkv_bot, held, outq, go, k_s, v_s, kt_s, vt_s, dk_s, dv_s, live_s, near_s, sems = refs
    feats = heads * HEAD_WIDTH
    chunk = BAND_ROWS * LONGITUDES // steps
    moves = [
        pltpu.make_async_copy(part, held.at[pl.ds(i * chunk, chunk)], sems.at[i]) for i, part in enumerate(upstream)
    ]
    for move in moves:
        move.start()
    tile_cols = LANES // heads // QUERY_ROWS
    tile_queries = QUERY_ROWS * tile_cols
    window = tile_cols // BLOCK + 2

    def load_pair(p, carry):
        for first, rows_s, turned_s in ((0, k_s, kt_s), (feats, v_s, vt_s)):
            both = jnp.stack(
                [kv_top[row_cols(row, p * 16, 16), first:first + feats] for row in range(HALO)]
                + [qkv[row_cols(row, p * 16, 16), feats + first:2 * feats + first] for row in range(BAND_ROWS)]
                + [kv_bot[row_cols(row, p * 16, 16), first:first + feats] for row in range(HALO)]
            ).astype(jnp.float32)
            for half in range(2):
                block = both[:, 8 * half:8 * half + 8, :].reshape(EXT_ROWS * BLOCK, feats)
                rows_s[2 * p + half] = block.astype(jnp.bfloat16)
                for upper in range(2):
                    low = upper * QUERY_ROWS * BLOCK
                    turned_s[upper, 2 * p + half] = block[low:low + KEYS].T.astype(jnp.bfloat16)
        for half in range(2):
            col = (2 * p + half) * BLOCK + lax.broadcasted_iota(jnp.int32, (BLOCK, 128), 0)
            for row in range(EXT_ROWS):
                live_s[2 * p + half, row * BLOCK:(row + 1) * BLOCK, :] = jnp.where(col < cells[row], 0.0, MASKED)
        return carry

    lax.fori_loop(0, BLOCKS // 2, load_pair, 0)
    dk_s[...] = jnp.zeros_like(dk_s)
    dv_s[...] = jnp.zeros_like(dv_s)

    lane = lax.broadcasted_iota(jnp.int32, (KEYS, LANES), 1) % tile_queries
    query_row = lane // tile_cols
    query_col = lane % tile_cols
    key = lax.broadcasted_iota(jnp.int32, (KEYS, LANES), 0)
    row_gap = key // BLOCK - query_row
    for j in range(window):
        col_gap = (j - 1) * BLOCK + key % BLOCK - query_col
        near = (row_gap >= 0) & (row_gap <= 2 * HALO) & (col_gap >= -HALO) & (col_gap <= HALO)
        near_s[j] = jnp.where(near, 0.0, MASKED)

    own_head = (
        lax.broadcasted_iota(jnp.int32, (LANES, feats), 0) // tile_queries
        == lax.broadcasted_iota(jnp.int32, (LANES, feats), 1) // HEAD_WIDTH
    )
    own_head_turned = (
        lax.broadcasted_iota(jnp.int32, (feats, LANES), 1) // tile_queries
        == lax.broadcasted_iota(jnp.int32, (feats, LANES), 0) // HEAD_WIDTH
    )
    query_lane = lax.broadcasted_iota(jnp.int32, (1, LANES), 1) % tile_queries

    def spread(ref, upper, start):
        tile = jnp.concatenate([
            ref[row_cols(upper * QUERY_ROWS + row, start, tile_cols), :feats] for row in range(QUERY_ROWS)
        ], axis=0)
        if heads == 1:
            return tile
        stacked = jnp.concatenate([tile] * heads, axis=0)
        return jnp.where(own_head, stacked, jnp.zeros_like(stacked))

    def gather(turned):
        if heads == 1:
            tile = turned.T
        else:
            tall = jnp.where(own_head_turned, turned, 0.0).T
            tile = sum(tall[h * tile_queries:(h + 1) * tile_queries] for h in range(heads))
        return tile.astype(jnp.bfloat16)

    def one_tile(upper, tile):
        start = pl.multiple_of(tile * tile_cols, 16)
        keys = pl.ds(upper * QUERY_ROWS * BLOCK, KEYS)
        index = [(tile * (tile_cols // BLOCK) + j + BLOCKS - 1) % BLOCKS for j in range(window)]
        queries = spread(qkv, upper, start)
        grads = spread(go, upper, start)
        scores = [
            nt(k_s[index[j], keys, :], queries)
            + near_s[j]
            + jnp.concatenate([live_s[index[j], keys, :]] * (LANES // 128), axis=1)
            for j in range(window)
        ]
        highest = jnp.max(functools.reduce(jnp.maximum, scores), axis=0, keepdims=True)
        terms = [jnp.exp(score - highest) for score in scores]
        total = jnp.sum(sum(terms), axis=0, keepdims=True)
        query_cells = jnp.zeros((1, LANES), jnp.int32)
        for row in range(QUERY_ROWS):
            cell = cells[HALO + upper * QUERY_ROWS + row]
            query_cells = jnp.where(query_lane // tile_cols == row, cell, query_cells)
        live = start + query_lane % tile_cols < query_cells
        inverse = jnp.where(live, 1.0 / total, 0.0)
        probs = [term * inverse for term in terms]
        grad_probs = [nt(v_s[index[j], keys, :], grads) for j in range(window)]
        delta = jnp.sum(sum(p * g for p, g in zip(probs, grad_probs)), axis=0, keepdims=True)
        weights = [p.astype(jnp.bfloat16) for p in probs]
        grad_scores = [(p * (g - delta)).astype(jnp.bfloat16) for p, g in zip(probs, grad_probs)]
        for j in range(window):
            dv_s[index[j], keys, :] += nn(weights[j], grads)
            dk_s[index[j], keys, :] += nn(grad_scores[j], queries)
        values_turned = jnp.concatenate([vt_s[upper, index[j]] for j in range(window)], axis=1)
        keys_turned = jnp.concatenate([kt_s[upper, index[j]] for j in range(window)], axis=1)
        heads_out = gather(nn(values_turned, jnp.concatenate(weights, axis=0)))
        grad_query = gather(nn(keys_turned, jnp.concatenate(grad_scores, axis=0)))
        for row in range(QUERY_ROWS):
            at = row_cols(upper * QUERY_ROWS + row, start, tile_cols)
            outq[at, :feats] = heads_out[row * tile_cols:(row + 1) * tile_cols]
            outq[at, feats:] = grad_query[row * tile_cols:(row + 1) * tile_cols]

    def tile_pair(tile, carry):
        for upper in range(2):
            one_tile(upper, tile)
        return carry

    for move in moves:
        move.wait()
    grad_heads = nt(held[...], weight[...]).astype(jnp.bfloat16)
    for i in range(steps):
        go[pl.ds(pl.multiple_of(order[i], 16), chunk)] = grad_heads[i * chunk:(i + 1) * chunk]
    lax.fori_loop(0, LONGITUDES // tile_cols, tile_pair, 0)
    moves = [
        pltpu.make_async_copy(outq.at[pl.ds(pl.multiple_of(order[i], 16), chunk)], part, sems.at[i])
        for i, part in enumerate(outq_parts)
    ]
    for move in moves:
        move.start()

    def store_pair(p, carry):
        for first, sums in ((0, dk_s), (feats, dv_s)):
            both = jnp.concatenate(
                [sums[2 * p + half].reshape(EXT_ROWS, BLOCK, feats) for half in range(2)], axis=1
            )
            for row in range(HALO):
                dkv_top[row_cols(row, p * 16, 16), first:first + feats] = both[row].astype(jnp.bfloat16)
                dkv_bot[row_cols(row, p * 16, 16), first:first + feats] = (
                    both[HALO + BAND_ROWS + row].astype(jnp.bfloat16)
                )
            for row in range(BAND_ROWS):
                dkv_own[row_cols(row, p * 16, 16), first:first + feats] = both[HALO + row]
        return carry

    lax.fori_loop(0, BLOCKS // 2, store_pair, 0)
    for move in moves:
        move.wait()


VMEM = pl.BlockSpec(memory_space=pltpu.VMEM)
SMEM = pl.BlockSpec(memory_space=pltpu.SMEM)
HBM = pl.BlockSpec(memory_space=pl.ANY)
BF16, F32 = jnp.bfloat16, jnp.float32


def shape(rows, cols, kind=BF16):
    return jax.ShapeDtypeStruct((rows, cols), kind)


def call(kernel, out_shape, in_specs, out_specs, args, flops, scratch=(), transcendentals=0):
    moved = sum(x.size * x.dtype.itemsize for x in (*args, *out_shape))
    return pl.pallas_call(
        kernel,
        out_shape=tuple(out_shape),
        in_specs=list(in_specs),
        out_specs=tuple(out_specs),
        scratch_shapes=list(scratch),
        compiler_params=pltpu.CompilerParams(vmem_limit_bytes=60 * 2**20),
        cost_estimate=pl.CostEstimate(
            flops=flops, transcendentals=transcendentals, bytes_accessed=moved
        ),
    )(*args)


def attention(cells, order, qkv, kv_top, kv_bot, weight, upstream):
    steps, (feats, width), chunk = len(upstream), weight.shape, upstream[0].shape[0]
    heads = feats // HEAD_WIDTH
    window = LANES // heads // QUERY_ROWS // BLOCK + 2
    band, halo = BAND_ROWS * LONGITUDES, HALO * LONGITUDES
    pairs = band * heads * KEYS * window
    results = call(
        functools.partial(attention_kernel, heads, steps),
        [shape(chunk, 2 * feats)] * steps
        + [shape(band, 2 * feats, F32), shape(halo, 2 * feats), shape(halo, 2 * feats)],
        [SMEM, SMEM, VMEM, VMEM, VMEM, VMEM] + [HBM] * steps,
        [HBM] * steps + [VMEM] * 3,
        (cells, order, qkv, kv_top, kv_bot, weight, *upstream),
        flops=12 * pairs * HEAD_WIDTH * heads + 2 * band * weight.size,
        transcendentals=pairs,
        scratch=[
            pltpu.VMEM((band, width), BF16),
            pltpu.VMEM((band, 2 * feats), BF16),
            pltpu.VMEM((band, feats), BF16),
            pltpu.VMEM((BLOCKS, EXT_ROWS * BLOCK, feats), BF16),
            pltpu.VMEM((BLOCKS, EXT_ROWS * BLOCK, feats), BF16),
            pltpu.VMEM((2, BLOCKS, feats, KEYS), BF16),
            pltpu.VMEM((2, BLOCKS, feats, KEYS), BF16),
            pltpu.VMEM((BLOCKS, EXT_ROWS * BLOCK, feats), F32),
            pltpu.VMEM((BLOCKS, EXT_ROWS * BLOCK, feats), F32),
            pltpu.VMEM((BLOCKS, EXT_ROWS * BLOCK, 128), F32),
            pltpu.VMEM((window, KEYS, LANES), F32),
            pltpu.SemaphoreType.DMA((steps,)),
        ],
    )
    return (results[:steps], *results[steps:])


def norm_kernel(tokens, gain, normed):
    features = tokens[...].astype(F32)
    inverse = lax.rsqrt(jnp.mean(features * features, axis=1, keepdims=True) + 1e-06)
    normed[...] = (features * inverse * gain[...]).astype(BF16)


def norm(tokens, gain):
    return call(
        norm_kernel, [shape(*tokens.shape)], [VMEM] * 2, [VMEM], (tokens, gain[None, :]), flops=4 * tokens.size
    )[0]


def stacked_moves(parts, held, sems, first=0):
    chunk = parts[0].shape[0]
    return [
        pltpu.make_async_copy(part, held.at[pl.ds(i * chunk, chunk)], sems.at[first + i]) for i, part in enumerate(parts)
    ]


def carry_out(moves):
    for move in moves:
        move.start()
    for move in moves:
        move.wait()


def projection_kernel(steps, feats, order, weight, *refs):
    parts, (qkv, kv_up, kv_down, held, sems) = refs[:steps], refs[steps:]
    chunk = parts[0].shape[0]
    carry_out(stacked_moves(parts, held, sems))
    for first in range(0, 3 * feats, feats):
        product = nn(held[...], weight[:, first:first + feats]).astype(BF16)
        for i in range(steps):
            qkv[pl.ds(pl.multiple_of(order[i], 16), chunk), first:first + feats] = product[i * chunk:(i + 1) * chunk]
    kv_up[...] = qkv[(BAND_ROWS - HALO) * LONGITUDES:, feats:]
    kv_down[...] = qkv[:HALO * LONGITUDES, feats:]


def projections(order, weight, parts):
    steps, feats = len(parts), weight.shape[1] // 3
    width = parts[0].shape[1]
    band, halo = BAND_ROWS * LONGITUDES, HALO * LONGITUDES
    return call(
        functools.partial(projection_kernel, steps, feats),
        [shape(band, 3 * feats), shape(halo, 2 * feats), shape(halo, 2 * feats)],
        [SMEM, VMEM] + [HBM] * steps, [VMEM] * 3, (order, weight, *parts),
        flops=2 * band * weight.size,
        scratch=[pltpu.VMEM((band, width), BF16), pltpu.SemaphoreType.DMA((steps,))],
    )


def join_kernel(steps, order, own, above, below, *refs):
    parts, (whole, sems) = refs[:steps], refs[steps:]
    chunk = parts[0].shape[0]
    low, high = (BAND_ROWS - HALO) * LONGITUDES, HALO * LONGITUDES
    whole[:low] = (own[:low] + below[:low].astype(F32)).astype(BF16)
    whole[low:high] = (own[low:high] + below[low:].astype(F32) + above[:high - low].astype(F32)).astype(BF16)
    whole[high:] = (own[high:] + above[high - low:].astype(F32)).astype(BF16)
    moves = [
        pltpu.make_async_copy(whole.at[pl.ds(pl.multiple_of(order[i], 16), chunk)], part, sems.at[i])
        for i, part in enumerate(parts)
    ]
    for move in moves:
        move.start()
    for move in moves:
        move.wait()


def joined(order, own, above, below, steps):
    band, feats = own.shape
    return call(
        functools.partial(join_kernel, steps),
        [shape(band // steps, feats)] * steps,
        [SMEM] + [VMEM] * 3, [HBM] * steps, (order, own, above, below), flops=2 * own.size,
        scratch=[pltpu.VMEM((band, feats), BF16), pltpu.SemaphoreType.DMA((steps,))],
    )


def weight_grad_kernel(steps, sides, *refs):
    lefts, refs = refs[:steps], refs[steps:]
    rights, (grad, left, right, sems) = [refs[i * steps:(i + 1) * steps] for i in range(sides)], refs[sides * steps:]
    feats = left.shape[1] // sides
    moves = stacked_moves(lefts, left, sems)
    for side, parts in enumerate(rights):
        moves += stacked_moves(parts, right.at[side], sems, (side + 1) * steps)
    carry_out(moves)
    for side in range(sides):
        at = slice(side * feats, (side + 1) * feats)
        grad[at, :] = lax.dot_general(
            left[:, at], right[side], (((0,), (0,)), ((), ())), preferred_element_type=F32
        ).astype(BF16)


def weight_grad(lefts, *rights):
    steps, (chunk, rows), width = len(lefts), lefts[0].shape, rights[0][0].shape[1]
    args = (*lefts, *(part for parts in rights for part in parts))
    return call(
        functools.partial(weight_grad_kernel, steps, len(rights)),
        [shape(rows, width)], [HBM] * len(args), [VMEM], args,
        flops=2 * steps * lefts[0].size * width,
        scratch=[
            pltpu.VMEM((steps * chunk, rows), BF16),
            pltpu.VMEM((len(rights), steps * chunk, width), BF16),
            pltpu.SemaphoreType.DMA((len(args),)),
        ],
    )[0]


def update_kernel(steps, leads, *refs):
    parts, blocks, (out, left, right, sems) = refs[:steps], refs[steps:2 * steps], refs[2 * steps:]
    feats = right.shape[0] // steps
    carry_out([
        pltpu.make_async_copy(block.at[pl.ds(3 * feats, feats)], right.at[pl.ds(i * feats, feats)], sems.at[i])
        for i, block in enumerate(blocks)
    ])
    for i, part in enumerate(parts):
        left[leads[i]] = part[:, :feats]
    out[...] = nn(jnp.concatenate([left[i] for i in range(steps)], axis=1), right[...]).astype(BF16)


def updates(leads, outq_own, blocks):
    steps, (rows, width), chunk = len(blocks), blocks[0].shape, outq_own[0].shape[0]
    return call(
        functools.partial(update_kernel, steps),
        [shape(chunk, width)], [SMEM] + [VMEM] * steps + [HBM] * steps, [VMEM], (leads, *outq_own, *blocks),
        flops=steps * chunk * rows * width // 2,
        scratch=[
            pltpu.VMEM((steps, chunk, rows // 4), BF16),
            pltpu.VMEM((steps * rows // 4, width), BF16),
            pltpu.SemaphoreType.DMA((steps,)),
        ],
    )[0]


def grad_input_kernel(steps, leads, tokens, gain, *refs):
    outq, dkv, blocks, (grad, left, right, sems) = (
        refs[:steps], refs[steps:2 * steps], refs[2 * steps:3 * steps], refs[3 * steps:]
    )
    rows = right.shape[0] // steps
    feats = rows // 3
    carry_out([
        pltpu.make_async_copy(block.at[pl.ds(0, rows)], right.at[pl.ds(i * rows, rows)], sems.at[i])
        for i, block in enumerate(blocks)
    ])
    for i in range(steps):
        left[leads[i], :, :feats] = outq[i][:, feats:]
        left[leads[i], :, feats:] = dkv[i][...]
    grad_normed = nn(jnp.concatenate([left[i] for i in range(steps)], axis=1), right[...])
    features = tokens[...].astype(F32)
    inverse = lax.rsqrt(jnp.mean(features * features, axis=1, keepdims=True) + 1e-06)
    centred = features * inverse
    scaled = gain[...] * grad_normed
    grad[...] = (inverse * (scaled - centred * jnp.mean(scaled * centred, axis=1, keepdims=True))).astype(BF16)


def grad_inputs(leads, tokens, gain, outq_own, dkv_own, blocks):
    steps, (rows, width), chunk = len(blocks), blocks[0].shape, tokens.shape[0]
    rows = rows * 3 // 4
    return call(
        functools.partial(grad_input_kernel, steps),
        [shape(*tokens.shape)], [SMEM] + [VMEM] * (2 + 2 * steps) + [HBM] * steps, [VMEM],
        (leads, tokens, gain[None, :], *outq_own, *dkv_own, *blocks),
        flops=2 * steps * chunk * rows * width,
        scratch=[
            pltpu.VMEM((steps, chunk, rows), BF16),
            pltpu.VMEM((steps * rows, width), BF16),
            pltpu.SemaphoreType.DMA((steps,)),
        ],
    )[0]


from jax.sharding import Mesh, PartitionSpec as P

WIDTH = 1024
GROUP = ("y", "m", "c")


def owners(halves):
    if halves == 2:
        return [
            lambda y, m, c: (c, 1 - m if c == y else m, y),
            lambda y, m, c: (c, 1 - m if c == y else m, 1 - y),
            lambda y, m, c: (c, m if c == y else 1 - m, 1 - y),
            lambda y, m, c: (c, m if c == y else 1 - m, y),
        ]
    return [
        lambda y, m, c, dm=dm, dc=dc: (c, (m + dm) % halves, (y + dc) % 2) for dc in range(2) for dm in range(halves)
    ]


def passed_along(x, by):
    length = lax.axis_size("z") * 2
    pairs = [(i, i + by) for i in range(length) if 0 <= i + by < length]
    return lax.ppermute(x, ("z", "c"), pairs)


def after(x, *others):
    return lax.optimization_barrier((x, *others))[0]


def on_device(tokens, gain, qkv_weight, out_weight, row_cells, upstream):
    heads = qkv_weight.shape[0]
    feats = heads * HEAD_WIDTH
    band_tokens = BAND_ROWS * LONGITUDES
    chunk = tokens.shape[0]
    halves, layers = lax.axis_size("m"), lax.axis_size("z")
    z, y, m, c = (lax.axis_index(axis) for axis in ("z",) + GROUP)
    grad_scale = 4.0 / math.sqrt(band_tokens * layers * 2)
    band_start = (z * 2 + c) * BAND_ROWS
    cells = lax.dynamic_slice_in_dim(jnp.pad(row_cells, (HALO, HALO)), band_start, EXT_ROWS)

    at = lambda y, m, c: (y * halves + m) * 2 + c
    spots = [(y, m, c) for y in range(2) for m in range(halves) for c in range(2)]
    slots = [[owner(*spot) for spot in spots] for owner in owners(halves)]
    here = lambda table: jnp.asarray(table, jnp.int32)[at(y, m, c)]
    order = here([[(slot[i][1] * 2 + slot[i][2]) * chunk for slot in slots] for i in range(len(spots))])

    def lead(slot, spot):
        far = spots[slot.index(spot)]
        return (far[0] - spot[2]) % 2 * halves + (far[1] - spot[1]) % halves

    leads = here([[lead(slot, spot) for slot in slots] for spot in spots])

    def permuted(x, pairs):
        return lax.ppermute(x, GROUP, [(at(*a), at(*b)) for a, b in pairs])

    def send_back(parts):
        return [permuted(x, list(zip(spots, slot))) for x, slot in zip(parts, slots)]

    def gathered(x, *others):
        sent = lambda slot: permuted(x, list(zip(slot, spots)))
        if halves != 2:
            return [sent(slot) for slot in slots]
        first, second, *others = lax.optimization_barrier((sent(slots[0]), sent(slots[1]), *others))
        third = permuted(
            jnp.where(c == y, first, x),
            [(spot, (1 - spot[0], spot[1], spot[0]) if spot[2] == spot[0] else (spot[0], spot[1], spot[0])) for spot in spots],
        )
        fourth = permuted(
            first, [(spot, (spot[0], 1 - spot[1], spot[2])) for spot in spots if spot[2] != spot[0]]
        )
        third, fourth = lax.optimization_barrier((third, fourth))
        return [first, second, third, jnp.where(c == y, x, fourth)]

    def from_ahead(x, dm):
        return lax.ppermute(x, "m", [((i + dm) % halves, i) for i in range(halves)])

    def from_sibling(x):
        return lax.ppermute(x, "c", [(0, 1), (1, 0)])

    raw = jnp.concatenate([qkv_weight.reshape(3 * feats, WIDTH), out_weight.reshape(feats, WIDTH)], axis=0)
    share = 4 * feats // layers
    held = lax.dynamic_slice_in_dim(raw, z * share, share, 0)
    shares = [from_ahead(held, dm) for dm in range(1, halves)]

    def split(block):
        qkv = block[:3 * feats].reshape(heads, 3, HEAD_WIDTH, WIDTH)
        eighth = jnp.asarray([HEAD_WIDTH ** -0.5, 1.0, 1.0], BF16)[None, :, None, None]
        qkv = (qkv * eighth).transpose(1, 0, 2, 3).reshape(3 * feats, WIDTH)
        return jnp.concatenate([qkv, block[3 * feats:]], axis=0)

    blocks = [split(raw)]
    sibling = from_sibling(blocks[0])
    group = jnp.where(c == y, blocks[0], sibling)
    group_qkv, group_out = group[:3 * feats].T, group[3 * feats:]

    *normed_parts, group_qkv, group_out = lax.optimization_barrier(
        (*gathered(norm(tokens, gain)), group_qkv, group_out)
    )
    qkv, kv_up, kv_down = projections(order, group_qkv, normed_parts)
    upstream_parts = gathered(after(upstream, *normed_parts), qkv)
    kv_top, kv_bot = passed_along(kv_up, 1), passed_along(kv_down, -1)
    shares = lax.optimization_barrier((shares, normed_parts))[0]
    ahead = [split(lax.all_gather(part, "z", axis=0, tiled=True)) for part in shares]
    order, kv_top, kv_bot, *ahead = lax.optimization_barrier((order, kv_top, kv_bot, *ahead))
    outq_parts, dkv, dkv_top, dkv_bot = attention(cells, order, qkv, kv_top, kv_bot, group_out, upstream_parts)

    blocks += ahead + [sibling] + [from_sibling(after(block, dkv_top)) for block in ahead]
    from_above, from_below = passed_along(dkv_top, -1), passed_along(dkv_bot, 1)
    outq_own = send_back(outq_parts)
    early = weight_grad(outq_parts, upstream_parts, normed_parts)
    dkv_parts = joined(after(order, early), dkv, from_above, from_below, len(slots))
    dkv_own = send_back(dkv_parts)
    late = weight_grad(dkv_parts, normed_parts)
    grads = lax.psum(jnp.concatenate([early, late], axis=0), ("z", "c"))
    update = updates(after(leads, late), outq_own, blocks)
    grad_input = grad_inputs(after(leads, late), tokens, gain, outq_own, dkv_own, blocks)

    def spread(grads):
        pairs = [((1 - y, m, 1 - y), (y, m, 1 - y)) for y in range(2) for m in range(halves)]
        return jnp.where(c == y, grads, permuted(grads, pairs)).astype(F32)

    grads, grad_input, update = lax.optimization_barrier((grads, grad_input, update))
    grads = spread(grads) * grad_scale
    early, late = grads[:2 * feats], grads[2 * feats:]
    by_head = lambda x: x.reshape(heads, HEAD_WIDTH, WIDTH)
    grad_out = by_head(early[:feats])
    grad_query = early[feats:] * HEAD_WIDTH ** -0.5
    grad_qkv = jnp.concatenate([by_head(grad_query), by_head(late[:feats]), by_head(late[feats:])], axis=1)
    return update, grad_input, grad_qkv, grad_out


def solution(mesh):
    devices = mesh.devices.reshape(mesh.shape["lat"] // 2, 2, mesh.shape["mp"] // 2, 2)
    tokens, weights = P(("z", "y", "m", "c"), None), P(("m", "c"), None, None)
    return jax.shard_map(
        on_device,
        mesh=Mesh(devices, ("z", "y", "m", "c")),
        in_specs=(tokens, P(), weights, weights, P(), tokens),
        out_specs=(tokens, tokens, weights, weights),
        check_vma=False,
    )
```

```python
import functools
import math
import jax
import jax.numpy as jnp
from jax import lax
from jax.experimental import pallas as pl
from jax.experimental.pallas import tpu as pltpu

HEAD_WIDTH = 64
LONGITUDES = 256
BAND_ROWS = 8
HALO = 6
EXT_ROWS = BAND_ROWS + 2 * HALO
LANES = 256
QUERY_ROWS = 4
KEY_ROWS = QUERY_ROWS + 2 * HALO
BLOCK = 8
BLOCKS = LONGITUDES // BLOCK
KEYS = KEY_ROWS * BLOCK
MASKED = -1e30


def nn(a, b):
    return lax.dot_general(a, b, (((1,), (0,)), ((), ())), preferred_element_type=jnp.float32)


def nt(a, b):
    return lax.dot_general(a, b, (((1,), (1,)), ((), ())), preferred_element_type=jnp.float32)


def row_cols(row, start, size):
    return pl.ds(pl.multiple_of(row * LONGITUDES + start, 16), size)


def attention_kernel(
    heads, steps,
    cells, order, qkv, kv_top, kv_bot, weight, *refs,
):
    upstream, refs = refs[:steps], refs[steps:]
    outq_parts, refs = refs[:steps], refs[steps:]
    dkv_own, dkv_top, dkv_bot, held, outq, go, k_s, v_s, kt_s, vt_s, dk_s, dv_s, live_s, near_s, sems = refs
    feats = heads * HEAD_WIDTH
    chunk = BAND_ROWS * LONGITUDES // steps
    moves = [
        pltpu.make_async_copy(part, held.at[pl.ds(i * chunk, chunk)], sems.at[i]) for i, part in enumerate(upstream)
    ]
    for move in moves:
        move.start()
    tile_cols = LANES // heads // QUERY_ROWS
    tile_queries = QUERY_ROWS * tile_cols
    window = tile_cols // BLOCK + 2

    def load_pair(p, carry):
        for first, rows_s, turned_s in ((0, k_s, kt_s), (feats, v_s, vt_s)):
            both = jnp.stack(
                [kv_top[row_cols(row, p * 16, 16), first:first + feats] for row in range(HALO)]
                + [qkv[row_cols(row, p * 16, 16), feats + first:2 * feats + first] for row in range(BAND_ROWS)]
                + [kv_bot[row_cols(row, p * 16, 16), first:first + feats] for row in range(HALO)]
            ).astype(jnp.float32)
            for half in range(2):
                block = both[:, 8 * half:8 * half + 8, :].reshape(EXT_ROWS * BLOCK, feats)
                rows_s[2 * p + half] = block.astype(jnp.bfloat16)
                for upper in range(2):
                    low = upper * QUERY_ROWS * BLOCK
                    turned_s[upper, 2 * p + half] = block[low:low + KEYS].T.astype(jnp.bfloat16)
        for half in range(2):
            col = (2 * p + half) * BLOCK + lax.broadcasted_iota(jnp.int32, (BLOCK, 128), 0)
            for row in range(EXT_ROWS):
                live_s[2 * p + half, row * BLOCK:(row + 1) * BLOCK, :] = jnp.where(col < cells[row], 0.0, MASKED)
        return carry

    lax.fori_loop(0, BLOCKS // 2, load_pair, 0)
    dk_s[...] = jnp.zeros_like(dk_s)
    dv_s[...] = jnp.zeros_like(dv_s)

    lane = lax.broadcasted_iota(jnp.int32, (KEYS, LANES), 1) % tile_queries
    query_row = lane // tile_cols
    query_col = lane % tile_cols
    key = lax.broadcasted_iota(jnp.int32, (KEYS, LANES), 0)
    row_gap = key // BLOCK - query_row
    for j in range(window):
        col_gap = (j - 1) * BLOCK + key % BLOCK - query_col
        near = (row_gap >= 0) & (row_gap <= 2 * HALO) & (col_gap >= -HALO) & (col_gap <= HALO)
        near_s[j] = jnp.where(near, 0.0, MASKED)

    own_head = (
        lax.broadcasted_iota(jnp.int32, (LANES, feats), 0) // tile_queries
        == lax.broadcasted_iota(jnp.int32, (LANES, feats), 1) // HEAD_WIDTH
    )
    own_head_turned = (
        lax.broadcasted_iota(jnp.int32, (feats, LANES), 1) // tile_queries
        == lax.broadcasted_iota(jnp.int32, (feats, LANES), 0) // HEAD_WIDTH
    )
    query_lane = lax.broadcasted_iota(jnp.int32, (1, LANES), 1) % tile_queries

    def spread(ref, upper, start):
        tile = jnp.concatenate([
            ref[row_cols(upper * QUERY_ROWS + row, start, tile_cols), :feats] for row in range(QUERY_ROWS)
        ], axis=0)
        if heads == 1:
            return tile
        stacked = jnp.concatenate([tile] * heads, axis=0)
        return jnp.where(own_head, stacked, jnp.zeros_like(stacked))

    def gather(turned):
        if heads == 1:
            tile = turned.T
        else:
            tall = jnp.where(own_head_turned, turned, 0.0).T
            tile = sum(tall[h * tile_queries:(h + 1) * tile_queries] for h in range(heads))
        return tile.astype(jnp.bfloat16)

    def one_tile(upper, tile):
        start = pl.multiple_of(tile * tile_cols, 16)
        keys = pl.ds(upper * QUERY_ROWS * BLOCK, KEYS)
        index = [(tile * (tile_cols // BLOCK) + j + BLOCKS - 1) % BLOCKS for j in range(window)]
        queries = spread(qkv, upper, start)
        grads = spread(go, upper, start)
        scores = [
            nt(k_s[index[j], keys, :], queries)
            + near_s[j]
            + jnp.concatenate([live_s[index[j], keys, :]] * (LANES // 128), axis=1)
            for j in range(window)
        ]
        highest = jnp.max(functools.reduce(jnp.maximum, scores), axis=0, keepdims=True)
        terms = [jnp.exp(score - highest) for score in scores]
        total = jnp.sum(sum(terms), axis=0, keepdims=True)
        query_cells = jnp.zeros((1, LANES), jnp.int32)
        for row in range(QUERY_ROWS):
            cell = cells[HALO + upper * QUERY_ROWS + row]
            query_cells = jnp.where(query_lane // tile_cols == row, cell, query_cells)
        live = start + query_lane % tile_cols < query_cells
        inverse = jnp.where(live, 1.0 / total, 0.0)
        probs = [term * inverse for term in terms]
        grad_probs = [nt(v_s[index[j], keys, :], grads) for j in range(window)]
        delta = jnp.sum(sum(p * g for p, g in zip(probs, grad_probs)), axis=0, keepdims=True)
        weights = [p.astype(jnp.bfloat16) for p in probs]
        grad_scores = [(p * (g - delta)).astype(jnp.bfloat16) for p, g in zip(probs, grad_probs)]
        for j in range(window):
            dv_s[index[j], keys, :] += nn(weights[j], grads)
            dk_s[index[j], keys, :] += nn(grad_scores[j], queries)
        values_turned = jnp.concatenate([vt_s[upper, index[j]] for j in range(window)], axis=1)
        keys_turned = jnp.concatenate([kt_s[upper, index[j]] for j in range(window)], axis=1)
        heads_out = gather(nn(values_turned, jnp.concatenate(weights, axis=0)))
        grad_query = gather(nn(keys_turned, jnp.concatenate(grad_scores, axis=0)))
        for row in range(QUERY_ROWS):
            at = row_cols(upper * QUERY_ROWS + row, start, tile_cols)
            outq[at, :feats] = heads_out[row * tile_cols:(row + 1) * tile_cols]
            outq[at, feats:] = grad_query[row * tile_cols:(row + 1) * tile_cols]

    def tile_pair(tile, carry):
        for upper in range(2):
            one_tile(upper, tile)
        return carry

    for move in moves:
        move.wait()
    grad_heads = nt(held[...], weight[...]).astype(jnp.bfloat16)
    for i in range(steps):
        go[pl.ds(pl.multiple_of(order[i], 16), chunk)] = grad_heads[i * chunk:(i + 1) * chunk]
    lax.fori_loop(0, LONGITUDES // tile_cols, tile_pair, 0)
    moves = [
        pltpu.make_async_copy(outq.at[pl.ds(pl.multiple_of(order[i], 16), chunk)], part, sems.at[i])
        for i, part in enumerate(outq_parts)
    ]
    for move in moves:
        move.start()

    def store_pair(p, carry):
        for first, sums in ((0, dk_s), (feats, dv_s)):
            both = jnp.concatenate(
                [sums[2 * p + half].reshape(EXT_ROWS, BLOCK, feats) for half in range(2)], axis=1
            )
            for row in range(HALO):
                dkv_top[row_cols(row, p * 16, 16), first:first + feats] = both[row].astype(jnp.bfloat16)
                dkv_bot[row_cols(row, p * 16, 16), first:first + feats] = (
                    both[HALO + BAND_ROWS + row].astype(jnp.bfloat16)
                )
            for row in range(BAND_ROWS):
                dkv_own[row_cols(row, p * 16, 16), first:first + feats] = both[HALO + row]
        return carry

    lax.fori_loop(0, BLOCKS // 2, store_pair, 0)
    for move in moves:
        move.wait()


VMEM = pl.BlockSpec(memory_space=pltpu.VMEM)
SMEM = pl.BlockSpec(memory_space=pltpu.SMEM)
HBM = pl.BlockSpec(memory_space=pl.ANY)
BF16, F32 = jnp.bfloat16, jnp.float32


def shape(rows, cols, kind=BF16):
    return jax.ShapeDtypeStruct((rows, cols), kind)


def call(kernel, out_shape, in_specs, out_specs, args, flops, scratch=(), transcendentals=0):
    moved = sum(x.size * x.dtype.itemsize for x in (*args, *out_shape))
    return pl.pallas_call(
        kernel,
        out_shape=tuple(out_shape),
        in_specs=list(in_specs),
        out_specs=tuple(out_specs),
        scratch_shapes=list(scratch),
        compiler_params=pltpu.CompilerParams(vmem_limit_bytes=60 * 2**20),
        cost_estimate=pl.CostEstimate(
            flops=flops, transcendentals=transcendentals, bytes_accessed=moved
        ),
    )(*args)


def attention(cells, order, qkv, kv_top, kv_bot, weight, upstream):
    steps, (feats, width), chunk = len(upstream), weight.shape, upstream[0].shape[0]
    heads = feats // HEAD_WIDTH
    window = LANES // heads // QUERY_ROWS // BLOCK + 2
    band, halo = BAND_ROWS * LONGITUDES, HALO * LONGITUDES
    pairs = band * heads * KEYS * window
    results = call(
        functools.partial(attention_kernel, heads, steps),
        [shape(chunk, 2 * feats)] * steps
        + [shape(band, 2 * feats, F32), shape(halo, 2 * feats), shape(halo, 2 * feats)],
        [SMEM, SMEM, VMEM, VMEM, VMEM, VMEM] + [HBM] * steps,
        [HBM] * steps + [VMEM] * 3,
        (cells, order, qkv, kv_top, kv_bot, weight, *upstream),
        flops=12 * pairs * HEAD_WIDTH * heads + 2 * band * weight.size,
        transcendentals=pairs,
        scratch=[
            pltpu.VMEM((band, width), BF16),
            pltpu.VMEM((band, 2 * feats), BF16),
            pltpu.VMEM((band, feats), BF16),
            pltpu.VMEM((BLOCKS, EXT_ROWS * BLOCK, feats), BF16),
            pltpu.VMEM((BLOCKS, EXT_ROWS * BLOCK, feats), BF16),
            pltpu.VMEM((2, BLOCKS, feats, KEYS), BF16),
            pltpu.VMEM((2, BLOCKS, feats, KEYS), BF16),
            pltpu.VMEM((BLOCKS, EXT_ROWS * BLOCK, feats), F32),
            pltpu.VMEM((BLOCKS, EXT_ROWS * BLOCK, feats), F32),
            pltpu.VMEM((BLOCKS, EXT_ROWS * BLOCK, 128), F32),
            pltpu.VMEM((window, KEYS, LANES), F32),
            pltpu.SemaphoreType.DMA((steps,)),
        ],
    )
    return (results[:steps], *results[steps:])


def norm_kernel(tokens, gain, normed):
    features = tokens[...].astype(F32)
    inverse = lax.rsqrt(jnp.mean(features * features, axis=1, keepdims=True) + 1e-06)
    normed[...] = (features * inverse * gain[...]).astype(BF16)


def norm(tokens, gain):
    return call(
        norm_kernel, [shape(*tokens.shape)], [VMEM] * 2, [VMEM], (tokens, gain[None, :]), flops=4 * tokens.size
    )[0]


def stacked_moves(parts, held, sems, first=0):
    chunk = parts[0].shape[0]
    return [
        pltpu.make_async_copy(part, held.at[pl.ds(i * chunk, chunk)], sems.at[first + i]) for i, part in enumerate(parts)
    ]


def carry_out(moves):
    for move in moves:
        move.start()
    for move in moves:
        move.wait()


def projection_kernel(steps, feats, order, weight, *refs):
    parts, (qkv, kv_up, kv_down, held, sems) = refs[:steps], refs[steps:]
    chunk = parts[0].shape[0]
    carry_out(stacked_moves(parts, held, sems))
    for first in range(0, 3 * feats, feats):
        product = nn(held[...], weight[:, first:first + feats]).astype(BF16)
        for i in range(steps):
            qkv[pl.ds(pl.multiple_of(order[i], 16), chunk), first:first + feats] = product[i * chunk:(i + 1) * chunk]
    kv_up[...] = qkv[(BAND_ROWS - HALO) * LONGITUDES:, feats:]
    kv_down[...] = qkv[:HALO * LONGITUDES, feats:]


def projections(order, weight, parts):
    steps, feats = len(parts), weight.shape[1] // 3
    width = parts[0].shape[1]
    band, halo = BAND_ROWS * LONGITUDES, HALO * LONGITUDES
    return call(
        functools.partial(projection_kernel, steps, feats),
        [shape(band, 3 * feats), shape(halo, 2 * feats), shape(halo, 2 * feats)],
        [SMEM, VMEM] + [HBM] * steps, [VMEM] * 3, (order, weight, *parts),
        flops=2 * band * weight.size,
        scratch=[pltpu.VMEM((band, width), BF16), pltpu.SemaphoreType.DMA((steps,))],
    )


def join_kernel(steps, order, own, above, below, *refs):
    parts, (whole, sems) = refs[:steps], refs[steps:]
    chunk = parts[0].shape[0]
    low, high = (BAND_ROWS - HALO) * LONGITUDES, HALO * LONGITUDES
    whole[:low] = (own[:low] + below[:low].astype(F32)).astype(BF16)
    whole[low:high] = (own[low:high] + below[low:].astype(F32) + above[:high - low].astype(F32)).astype(BF16)
    whole[high:] = (own[high:] + above[high - low:].astype(F32)).astype(BF16)
    moves = [
        pltpu.make_async_copy(whole.at[pl.ds(pl.multiple_of(order[i], 16), chunk)], part, sems.at[i])
        for i, part in enumerate(parts)
    ]
    for move in moves:
        move.start()
    for move in moves:
        move.wait()


def joined(order, own, above, below, steps):
    band, feats = own.shape
    return call(
        functools.partial(join_kernel, steps),
        [shape(band // steps, feats)] * steps,
        [SMEM] + [VMEM] * 3, [HBM] * steps, (order, own, above, below), flops=2 * own.size,
        scratch=[pltpu.VMEM((band, feats), BF16), pltpu.SemaphoreType.DMA((steps,))],
    )


def weight_grad_kernel(steps, sides, *refs):
    lefts, refs = refs[:steps], refs[steps:]
    rights, (grad, left, right, sems) = [refs[i * steps:(i + 1) * steps] for i in range(sides)], refs[sides * steps:]
    feats = left.shape[1] // sides
    moves = stacked_moves(lefts, left, sems)
    for side, parts in enumerate(rights):
        moves += stacked_moves(parts, right.at[side], sems, (side + 1) * steps)
    carry_out(moves)
    for side in range(sides):
        at = slice(side * feats, (side + 1) * feats)
        grad[at, :] = lax.dot_general(
            left[:, at], right[side], (((0,), (0,)), ((), ())), preferred_element_type=F32
        ).astype(BF16)


def weight_grad(lefts, *rights):
    steps, (chunk, rows), width = len(lefts), lefts[0].shape, rights[0][0].shape[1]
    args = (*lefts, *(part for parts in rights for part in parts))
    return call(
        functools.partial(weight_grad_kernel, steps, len(rights)),
        [shape(rows, width)], [HBM] * len(args), [VMEM], args,
        flops=2 * steps * lefts[0].size * width,
        scratch=[
            pltpu.VMEM((steps * chunk, rows), BF16),
            pltpu.VMEM((len(rights), steps * chunk, width), BF16),
            pltpu.SemaphoreType.DMA((len(args),)),
        ],
    )[0]


def update_kernel(steps, leads, *refs):
    parts, blocks, (out, left, right, sems) = refs[:steps], refs[steps:2 * steps], refs[2 * steps:]
    feats = right.shape[0] // steps
    carry_out([
        pltpu.make_async_copy(block.at[pl.ds(3 * feats, feats)], right.at[pl.ds(i * feats, feats)], sems.at[i])
        for i, block in enumerate(blocks)
    ])
    for i, part in enumerate(parts):
        left[leads[i]] = part[:, :feats]
    out[...] = nn(jnp.concatenate([left[i] for i in range(steps)], axis=1), right[...]).astype(BF16)


def updates(leads, outq_own, blocks):
    steps, (rows, width), chunk = len(blocks), blocks[0].shape, outq_own[0].shape[0]
    return call(
        functools.partial(update_kernel, steps),
        [shape(chunk, width)], [SMEM] + [VMEM] * steps + [HBM] * steps, [VMEM], (leads, *outq_own, *blocks),
        flops=steps * chunk * rows * width // 2,
        scratch=[
            pltpu.VMEM((steps, chunk, rows // 4), BF16),
            pltpu.VMEM((steps * rows // 4, width), BF16),
            pltpu.SemaphoreType.DMA((steps,)),
        ],
    )[0]


def grad_input_kernel(steps, leads, tokens, gain, *refs):
    outq, dkv, blocks, (grad, left, right, sems) = (
        refs[:steps], refs[steps:2 * steps], refs[2 * steps:3 * steps], refs[3 * steps:]
    )
    rows = right.shape[0] // steps
    feats = rows // 3
    carry_out([
        pltpu.make_async_copy(block.at[pl.ds(0, rows)], right.at[pl.ds(i * rows, rows)], sems.at[i])
        for i, block in enumerate(blocks)
    ])
    for i in range(steps):
        left[leads[i], :, :feats] = outq[i][:, feats:]
        left[leads[i], :, feats:] = dkv[i][...]
    grad_normed = nn(jnp.concatenate([left[i] for i in range(steps)], axis=1), right[...])
    features = tokens[...].astype(F32)
    inverse = lax.rsqrt(jnp.mean(features * features, axis=1, keepdims=True) + 1e-06)
    centred = features * inverse
    scaled = gain[...] * grad_normed
    grad[...] = (inverse * (scaled - centred * jnp.mean(scaled * centred, axis=1, keepdims=True))).astype(BF16)


def grad_inputs(leads, tokens, gain, outq_own, dkv_own, blocks):
    steps, (rows, width), chunk = len(blocks), blocks[0].shape, tokens.shape[0]
    rows = rows * 3 // 4
    return call(
        functools.partial(grad_input_kernel, steps),
        [shape(*tokens.shape)], [SMEM] + [VMEM] * (2 + 2 * steps) + [HBM] * steps, [VMEM],
        (leads, tokens, gain[None, :], *outq_own, *dkv_own, *blocks),
        flops=2 * steps * chunk * rows * width,
        scratch=[
            pltpu.VMEM((steps, chunk, rows), BF16),
            pltpu.VMEM((steps * rows, width), BF16),
            pltpu.SemaphoreType.DMA((steps,)),
        ],
    )[0]


from jax.sharding import Mesh, PartitionSpec as P

WIDTH = 1024
GROUP = ("y", "m", "c")


def owners(halves):
    if halves == 2:
        return [
            lambda y, m, c: (c, 1 - m if c == y else m, y),
            lambda y, m, c: (c, 1 - m if c == y else m, 1 - y),
            lambda y, m, c: (c, m if c == y else 1 - m, 1 - y),
            lambda y, m, c: (c, m if c == y else 1 - m, y),
        ]
    return [
        lambda y, m, c, dm=dm, dc=dc: (c, (m + dm) % halves, (y + dc) % 2) for dc in range(2) for dm in range(halves)
    ]


def passed_along(x, by):
    length = lax.axis_size("z") * 2
    pairs = [(i, i + by) for i in range(length) if 0 <= i + by < length]
    return lax.ppermute(x, ("z", "c"), pairs)


def after(x, *others):
    return lax.optimization_barrier((x, *others))[0]


def on_device(tokens, gain, qkv_weight, out_weight, row_cells, upstream):
    heads = qkv_weight.shape[0]
    feats = heads * HEAD_WIDTH
    band_tokens = BAND_ROWS * LONGITUDES
    chunk = tokens.shape[0]
    halves, layers = lax.axis_size("m"), lax.axis_size("z")
    z, y, m, c = (lax.axis_index(axis) for axis in ("z",) + GROUP)
    grad_scale = 4.0 / math.sqrt(band_tokens * layers * 2)
    band_start = (z * 2 + c) * BAND_ROWS
    cells = lax.dynamic_slice_in_dim(jnp.pad(row_cells, (HALO, HALO)), band_start, EXT_ROWS)

    at = lambda y, m, c: (y * halves + m) * 2 + c
    spots = [(y, m, c) for y in range(2) for m in range(halves) for c in range(2)]
    slots = [[owner(*spot) for spot in spots] for owner in owners(halves)]
    here = lambda table: jnp.asarray(table, jnp.int32)[at(y, m, c)]
    order = here([[(slot[i][1] * 2 + slot[i][2]) * chunk for slot in slots] for i in range(len(spots))])

    def lead(slot, spot):
        far = spots[slot.index(spot)]
        return (far[0] - spot[2]) % 2 * halves + (far[1] - spot[1]) % halves

    leads = here([[lead(slot, spot) for slot in slots] for spot in spots])

    def permuted(x, pairs):
        return lax.ppermute(x, GROUP, [(at(*a), at(*b)) for a, b in pairs])

    def send_back(parts):
        return [permuted(x, list(zip(spots, slot))) for x, slot in zip(parts, slots)]

    def gathered(x, *others):
        sent = lambda slot: permuted(x, list(zip(slot, spots)))
        if halves != 2:
            parts = [sent(slot) for slot in slots]
            return parts, parts
        first, second = lax.optimization_barrier((sent(slots[0]), sent(slots[1])))
        hop = first, second
        first = after(first, *others)
        third = permuted(
            jnp.where(c == y, first, x),
            [(spot, (1 - spot[0], spot[1], spot[0]) if spot[2] == spot[0] else (spot[0], spot[1], spot[0])) for spot in spots],
        )
        fourth = permuted(
            first, [(spot, (spot[0], 1 - spot[1], spot[2])) for spot in spots if spot[2] != spot[0]]
        )
        third, fourth = lax.optimization_barrier((third, fourth))
        return [first, second, third, jnp.where(c == y, x, fourth)], hop

    def from_ahead(x, dm):
        return lax.ppermute(x, "m", [((i + dm) % halves, i) for i in range(halves)])

    def from_sibling(x):
        return lax.ppermute(x, "c", [(0, 1), (1, 0)])

    rows = 3 * feats // layers, feats // layers
    flat_qkv, flat_out = qkv_weight.reshape(3 * feats, WIDTH), out_weight.reshape(feats, WIDTH)
    held = jnp.concatenate([
        lax.dynamic_slice_in_dim(flat, z * size, size, 0) for flat, size in zip((flat_qkv, flat_out), rows)
    ], axis=0)
    shares = [from_ahead(held, dm) for dm in range(1, halves)]

    def split(qkv, out):
        eighth = jnp.asarray([HEAD_WIDTH ** -0.5, 1.0, 1.0], BF16)[None, :, None, None]
        qkv = (qkv.reshape(heads, 3, HEAD_WIDTH, WIDTH) * eighth).transpose(1, 0, 2, 3)
        return jnp.concatenate([qkv.reshape(3 * feats, WIDTH), out.reshape(feats, WIDTH)], axis=0)

    tokens, *shares = lax.optimization_barrier((tokens, *shares))
    ahead = [lax.all_gather(part, "z") for part in shares]
    blocks = [split(flat_qkv, flat_out)]
    sibling = from_sibling(blocks[0])
    group = jnp.where(c == y, blocks[0], sibling)
    group_qkv, group_out = group[:3 * feats].T, group[3 * feats:]

    normed_parts, hop = gathered(norm(tokens, gain))
    *normed_parts, group_qkv, group_out = lax.optimization_barrier((*normed_parts, group_qkv, group_out))
    qkv, kv_up, kv_down = projections(order, group_qkv, normed_parts)
    upstream_parts, _ = gathered(after(upstream, *hop), qkv)
    kv_top, kv_bot = passed_along(kv_up, 1), passed_along(kv_down, -1)
    order, kv_top, kv_bot, *ahead = lax.optimization_barrier((order, kv_top, kv_bot, *ahead))
    outq_parts, dkv, dkv_top, dkv_bot = attention(cells, order, qkv, kv_top, kv_bot, group_out, upstream_parts)

    ahead = [after(block, dkv_top) for block in ahead]
    ahead = [split(block[:, :rows[0]], block[:, rows[0]:]) for block in ahead]
    blocks += ahead + [sibling] + [from_sibling(block) for block in ahead]
    from_above, from_below = passed_along(dkv_top, -1), passed_along(dkv_bot, 1)
    outq_own = send_back(outq_parts)

    bits = range((layers - 1).bit_length())
    partners = [("c", c, from_sibling)] + [
        ("z", z // 2 ** bit % 2, lambda x, bit=bit: lax.ppermute(x, "z", [(i, i ^ 2 ** bit) for i in range(layers)]))
        for bit in bits
    ]

    def halved(x, partner):
        _, side, swap = partner
        half = x.shape[0] // 2
        keep, give = (lax.dynamic_slice_in_dim(x, at * half, half, 0) for at in (side, 1 - side))
        return (keep.astype(F32) + swap(give).astype(F32)).astype(BF16)

    def in_turn(side, mine, other):
        return jnp.concatenate([jnp.where(side == 0, mine, other), jnp.where(side == 0, other, mine)], axis=1)

    def begun(grads):
        return halved(halved(grads, partners[0]), partners[1])

    early = begun(weight_grad(outq_parts, upstream_parts, normed_parts))
    early, from_above, from_below, *outq_own = lax.optimization_barrier((early, from_above, from_below, *outq_own))
    dkv_parts = joined(order, dkv, from_above, from_below, len(slots))
    dkv_own = send_back(dkv_parts)
    late = begun(weight_grad(dkv_parts, normed_parts))
    update = updates(after(leads, late), outq_own, blocks)
    late, update, *dkv_own = lax.optimization_barrier((late, update, *dkv_own))
    grad_input = grad_inputs(leads, tokens, gain, outq_own, dkv_own, blocks)

    both = jnp.concatenate([early, late], axis=0)
    for partner in partners[2:]:
        both = halved(both, partner)
    for _, side, swap in reversed(partners[2:]):
        other = swap(both)
        both = jnp.concatenate([jnp.where(side == 0, both, other), jnp.where(side == 0, other, both)], axis=0)
    both = both.reshape(2, feats // 2, WIDTH)
    _, side, swap = partners[1]
    over_y = lambda x: lax.ppermute(x, "y", [(0, 1), (1, 0)])
    other, both_y = lax.optimization_barrier((swap(both), over_y(both)))
    own = in_turn(side, both, other)
    far = in_turn(side, both_y, over_y(other))
    own, far, grad_input = lax.optimization_barrier((own, far, grad_input))
    mine, give = jnp.where(c == y, own, far), jnp.where(c == y, far, own)
    early, late = in_turn(c, mine, from_sibling(give)).astype(F32) * grad_scale
    by_head = lambda x: x.reshape(heads, HEAD_WIDTH, WIDTH)
    grad_out = by_head(early[:feats])
    grad_query = early[feats:] * HEAD_WIDTH ** -0.5
    grad_qkv = jnp.concatenate([by_head(grad_query), by_head(late[:feats]), by_head(late[feats:])], axis=1)
    return update, grad_input, grad_qkv, grad_out


def solution(mesh):
    devices = mesh.devices.reshape(mesh.shape["lat"] // 2, 2, mesh.shape["mp"] // 2, 2)
    tokens, weights = P(("z", "y", "m", "c"), None), P(("m", "c"), None, None)
    return jax.shard_map(
        on_device,
        mesh=Mesh(devices, ("z", "y", "m", "c")),
        in_specs=(tokens, P(), weights, weights, P(), tokens),
        out_specs=(tokens, tokens, weights, weights),
        check_vma=False,
    )
```

```python
import functools
import math
import jax
import jax.numpy as jnp
from jax import lax
from jax.experimental import pallas as pl
from jax.experimental.pallas import tpu as pltpu

HEAD_WIDTH = 64
LONGITUDES = 256
BAND_ROWS = 8
HALO = 6
EXT_ROWS = BAND_ROWS + 2 * HALO
LANES = 256
QUERY_ROWS = 4
KEY_ROWS = QUERY_ROWS + 2 * HALO
BLOCK = 8
BLOCKS = LONGITUDES // BLOCK
KEYS = KEY_ROWS * BLOCK
MASKED = -1e30


def nn(a, b):
    return lax.dot_general(a, b, (((1,), (0,)), ((), ())), preferred_element_type=jnp.float32)


def nt(a, b):
    return lax.dot_general(a, b, (((1,), (1,)), ((), ())), preferred_element_type=jnp.float32)


def row_cols(row, start, size):
    return pl.ds(pl.multiple_of(row * LONGITUDES + start, 16), size)


def attention_kernel(
    heads, steps,
    cells, order, qkv, kv_top, kv_bot, weight, *refs,
):
    upstream, refs = refs[:steps], refs[steps:]
    outq_parts, refs = refs[:steps], refs[steps:]
    dkv_own, dkv_top, dkv_bot, held, outq, go, k_s, v_s, kt_s, vt_s, dk_s, dv_s, live_s, near_s, sems = refs
    feats = heads * HEAD_WIDTH
    chunk = BAND_ROWS * LONGITUDES // steps
    moves = [
        pltpu.make_async_copy(part, held.at[pl.ds(i * chunk, chunk)], sems.at[i]) for i, part in enumerate(upstream)
    ]
    for move in moves:
        move.start()
    tile_cols = LANES // heads // QUERY_ROWS
    tile_queries = QUERY_ROWS * tile_cols
    window = tile_cols // BLOCK + 2

    def load_pair(p, carry):
        for first, rows_s, turned_s in ((0, k_s, kt_s), (feats, v_s, vt_s)):
            both = jnp.stack(
                [kv_top[row_cols(row, p * 16, 16), first:first + feats] for row in range(HALO)]
                + [qkv[row_cols(row, p * 16, 16), feats + first:2 * feats + first] for row in range(BAND_ROWS)]
                + [kv_bot[row_cols(row, p * 16, 16), first:first + feats] for row in range(HALO)]
            ).astype(jnp.float32)
            for half in range(2):
                block = both[:, 8 * half:8 * half + 8, :].reshape(EXT_ROWS * BLOCK, feats)
                rows_s[2 * p + half] = block.astype(jnp.bfloat16)
                for upper in range(2):
                    low = upper * QUERY_ROWS * BLOCK
                    turned_s[upper, 2 * p + half] = block[low:low + KEYS].T.astype(jnp.bfloat16)
        for half in range(2):
            col = (2 * p + half) * BLOCK + lax.broadcasted_iota(jnp.int32, (BLOCK, 128), 0)
            for row in range(EXT_ROWS):
                live_s[2 * p + half, row * BLOCK:(row + 1) * BLOCK, :] = jnp.where(col < cells[row], 0.0, MASKED)
        return carry

    lax.fori_loop(0, BLOCKS // 2, load_pair, 0)
    dk_s[...] = jnp.zeros_like(dk_s)
    dv_s[...] = jnp.zeros_like(dv_s)

    lane = lax.broadcasted_iota(jnp.int32, (KEYS, LANES), 1) % tile_queries
    query_row = lane // tile_cols
    query_col = lane % tile_cols
    key = lax.broadcasted_iota(jnp.int32, (KEYS, LANES), 0)
    row_gap = key // BLOCK - query_row
    for j in range(window):
        col_gap = (j - 1) * BLOCK + key % BLOCK - query_col
        near = (row_gap >= 0) & (row_gap <= 2 * HALO) & (col_gap >= -HALO) & (col_gap <= HALO)
        near_s[j] = jnp.where(near, 0.0, MASKED)

    own_head = (
        lax.broadcasted_iota(jnp.int32, (LANES, feats), 0) // tile_queries
        == lax.broadcasted_iota(jnp.int32, (LANES, feats), 1) // HEAD_WIDTH
    )
    own_head_turned = (
        lax.broadcasted_iota(jnp.int32, (feats, LANES), 1) // tile_queries
        == lax.broadcasted_iota(jnp.int32, (feats, LANES), 0) // HEAD_WIDTH
    )
    query_lane = lax.broadcasted_iota(jnp.int32, (1, LANES), 1) % tile_queries

    def spread(ref, upper, start):
        tile = jnp.concatenate([
            ref[row_cols(upper * QUERY_ROWS + row, start, tile_cols), :feats] for row in range(QUERY_ROWS)
        ], axis=0)
        if heads == 1:
            return tile
        stacked = jnp.concatenate([tile] * heads, axis=0)
        return jnp.where(own_head, stacked, jnp.zeros_like(stacked))

    def gather(turned):
        if heads == 1:
            tile = turned.T
        else:
            tall = jnp.where(own_head_turned, turned, 0.0).T
            tile = sum(tall[h * tile_queries:(h + 1) * tile_queries] for h in range(heads))
        return tile.astype(jnp.bfloat16)

    def one_tile(upper, tile):
        start = pl.multiple_of(tile * tile_cols, 16)
        keys = pl.ds(upper * QUERY_ROWS * BLOCK, KEYS)
        index = [(tile * (tile_cols // BLOCK) + j + BLOCKS - 1) % BLOCKS for j in range(window)]
        queries = spread(qkv, upper, start)
        grads = spread(go, upper, start)
        scores = [
            nt(k_s[index[j], keys, :], queries)
            + near_s[j]
            + jnp.concatenate([live_s[index[j], keys, :]] * (LANES // 128), axis=1)
            for j in range(window)
        ]
        highest = jnp.max(functools.reduce(jnp.maximum, scores), axis=0, keepdims=True)
        terms = [jnp.exp(score - highest) for score in scores]
        total = jnp.sum(sum(terms), axis=0, keepdims=True)
        query_cells = jnp.zeros((1, LANES), jnp.int32)
        for row in range(QUERY_ROWS):
            cell = cells[HALO + upper * QUERY_ROWS + row]
            query_cells = jnp.where(query_lane // tile_cols == row, cell, query_cells)
        live = start + query_lane % tile_cols < query_cells
        inverse = jnp.where(live, 1.0 / total, 0.0)
        probs = [term * inverse for term in terms]
        grad_probs = [nt(v_s[index[j], keys, :], grads) for j in range(window)]
        delta = jnp.sum(sum(p * g for p, g in zip(probs, grad_probs)), axis=0, keepdims=True)
        weights = [p.astype(jnp.bfloat16) for p in probs]
        grad_scores = [(p * (g - delta)).astype(jnp.bfloat16) for p, g in zip(probs, grad_probs)]
        for j in range(window):
            dv_s[index[j], keys, :] += nn(weights[j], grads)
            dk_s[index[j], keys, :] += nn(grad_scores[j], queries)
        values_turned = jnp.concatenate([vt_s[upper, index[j]] for j in range(window)], axis=1)
        keys_turned = jnp.concatenate([kt_s[upper, index[j]] for j in range(window)], axis=1)
        heads_out = gather(nn(values_turned, jnp.concatenate(weights, axis=0)))
        grad_query = gather(nn(keys_turned, jnp.concatenate(grad_scores, axis=0)))
        for row in range(QUERY_ROWS):
            at = row_cols(upper * QUERY_ROWS + row, start, tile_cols)
            outq[at, :feats] = heads_out[row * tile_cols:(row + 1) * tile_cols]
            outq[at, feats:] = grad_query[row * tile_cols:(row + 1) * tile_cols]

    def tile_pair(tile, carry):
        for upper in range(2):
            one_tile(upper, tile)
        return carry

    for move in moves:
        move.wait()
    grad_heads = nt(held[...], weight[...]).astype(jnp.bfloat16)
    for i in range(steps):
        go[pl.ds(pl.multiple_of(order[i], 16), chunk)] = grad_heads[i * chunk:(i + 1) * chunk]
    lax.fori_loop(0, LONGITUDES // tile_cols, tile_pair, 0)
    moves = [
        pltpu.make_async_copy(outq.at[pl.ds(pl.multiple_of(order[i], 16), chunk)], part, sems.at[i])
        for i, part in enumerate(outq_parts)
    ]
    for move in moves:
        move.start()

    def store_pair(p, carry):
        for first, sums in ((0, dk_s), (feats, dv_s)):
            both = jnp.concatenate(
                [sums[2 * p + half].reshape(EXT_ROWS, BLOCK, feats) for half in range(2)], axis=1
            )
            for row in range(HALO):
                dkv_top[row_cols(row, p * 16, 16), first:first + feats] = both[row].astype(jnp.bfloat16)
                dkv_bot[row_cols(row, p * 16, 16), first:first + feats] = (
                    both[HALO + BAND_ROWS + row].astype(jnp.bfloat16)
                )
            for row in range(BAND_ROWS):
                dkv_own[row_cols(row, p * 16, 16), first:first + feats] = both[HALO + row]
        return carry

    lax.fori_loop(0, BLOCKS // 2, store_pair, 0)
    for move in moves:
        move.wait()


VMEM = pl.BlockSpec(memory_space=pltpu.VMEM)
SMEM = pl.BlockSpec(memory_space=pltpu.SMEM)
HBM = pl.BlockSpec(memory_space=pl.ANY)
BF16, F32 = jnp.bfloat16, jnp.float32


def shape(rows, cols, kind=BF16):
    return jax.ShapeDtypeStruct((rows, cols), kind)


def call(kernel, out_shape, in_specs, out_specs, args, flops, scratch=(), transcendentals=0):
    moved = sum(x.size * x.dtype.itemsize for x in (*args, *out_shape))
    return pl.pallas_call(
        kernel,
        out_shape=tuple(out_shape),
        in_specs=list(in_specs),
        out_specs=tuple(out_specs),
        scratch_shapes=list(scratch),
        compiler_params=pltpu.CompilerParams(vmem_limit_bytes=60 * 2**20),
        cost_estimate=pl.CostEstimate(
            flops=flops, transcendentals=transcendentals, bytes_accessed=moved
        ),
    )(*args)


def attention(cells, order, qkv, kv_top, kv_bot, weight, upstream):
    steps, (feats, width), chunk = len(upstream), weight.shape, upstream[0].shape[0]
    heads = feats // HEAD_WIDTH
    window = LANES // heads // QUERY_ROWS // BLOCK + 2
    band, halo = BAND_ROWS * LONGITUDES, HALO * LONGITUDES
    pairs = band * heads * KEYS * window
    results = call(
        functools.partial(attention_kernel, heads, steps),
        [shape(chunk, 2 * feats)] * steps
        + [shape(band, 2 * feats, F32), shape(halo, 2 * feats), shape(halo, 2 * feats)],
        [SMEM, SMEM, VMEM, VMEM, VMEM, VMEM] + [HBM] * steps,
        [HBM] * steps + [VMEM] * 3,
        (cells, order, qkv, kv_top, kv_bot, weight, *upstream),
        flops=12 * pairs * HEAD_WIDTH * heads + 2 * band * weight.size,
        transcendentals=pairs,
        scratch=[
            pltpu.VMEM((band, width), BF16),
            pltpu.VMEM((band, 2 * feats), BF16),
            pltpu.VMEM((band, feats), BF16),
            pltpu.VMEM((BLOCKS, EXT_ROWS * BLOCK, feats), BF16),
            pltpu.VMEM((BLOCKS, EXT_ROWS * BLOCK, feats), BF16),
            pltpu.VMEM((2, BLOCKS, feats, KEYS), BF16),
            pltpu.VMEM((2, BLOCKS, feats, KEYS), BF16),
            pltpu.VMEM((BLOCKS, EXT_ROWS * BLOCK, feats), F32),
            pltpu.VMEM((BLOCKS, EXT_ROWS * BLOCK, feats), F32),
            pltpu.VMEM((BLOCKS, EXT_ROWS * BLOCK, 128), F32),
            pltpu.VMEM((window, KEYS, LANES), F32),
            pltpu.SemaphoreType.DMA((steps,)),
        ],
    )
    return (results[:steps], *results[steps:])


def norm_kernel(tokens, gain, normed):
    features = tokens[...].astype(F32)
    inverse = lax.rsqrt(jnp.mean(features * features, axis=1, keepdims=True) + 1e-06)
    normed[...] = (features * inverse * gain[...]).astype(BF16)


def norm(tokens, gain):
    return call(
        norm_kernel, [shape(*tokens.shape)], [VMEM] * 2, [VMEM], (tokens, gain[None, :]), flops=4 * tokens.size
    )[0]


def stacked_moves(parts, held, sems, first=0):
    chunk = parts[0].shape[0]
    return [
        pltpu.make_async_copy(part, held.at[pl.ds(i * chunk, chunk)], sems.at[first + i]) for i, part in enumerate(parts)
    ]


def carry_out(moves):
    for move in moves:
        move.start()
    for move in moves:
        move.wait()


def halo_kernel(steps, order, *refs):
    parts, (up, down, held, sems) = refs[:steps], refs[steps:]
    chunk = parts[0].shape[0]
    carry_out([
        pltpu.make_async_copy(part, held.at[pl.ds(pl.multiple_of(order[i], 16), chunk)], sems.at[i])
        for i, part in enumerate(parts)
    ])
    halo, rest = HALO * LONGITUDES, (BAND_ROWS - HALO) * LONGITUDES
    carry_out([
        pltpu.make_async_copy(held.at[pl.ds(rest, halo)], up, sems.at[0]),
        pltpu.make_async_copy(held.at[pl.ds(0, halo)], down, sems.at[1]),
    ])


def halo_rows(order, parts):
    steps, width = len(parts), parts[0].shape[1]
    halo = shape(HALO * LONGITUDES, width)
    return call(
        functools.partial(halo_kernel, steps), [halo, halo], [SMEM] + [HBM] * steps, [HBM] * 2, (order, *parts), flops=0,
        scratch=[pltpu.VMEM((BAND_ROWS * LONGITUDES, width), BF16), pltpu.SemaphoreType.DMA((steps,))],
    )


def projection_kernel(steps, feats, order, weight, *refs):
    parts, (qkv, held, sems) = refs[:steps], refs[steps:]
    chunk = parts[0].shape[0]
    carry_out(stacked_moves(parts, held, sems))
    for first in range(0, 3 * feats, feats):
        product = nn(held[...], weight[:, first:first + feats]).astype(BF16)
        for i in range(steps):
            qkv[pl.ds(pl.multiple_of(order[i], 16), chunk), first:first + feats] = product[i * chunk:(i + 1) * chunk]


def projections(order, weight, parts):
    steps, feats, width = len(parts), weight.shape[1] // 3, parts[0].shape[1]
    band = BAND_ROWS * LONGITUDES
    return call(
        functools.partial(projection_kernel, steps, feats),
        [shape(band, 3 * feats)], [SMEM, VMEM] + [HBM] * steps, [VMEM], (order, weight, *parts),
        flops=2 * band * weight.size,
        scratch=[pltpu.VMEM((band, width), BF16), pltpu.SemaphoreType.DMA((steps,))],
    )[0]


def join_kernel(steps, order, own, above, below, *refs):
    parts, (whole, sems) = refs[:steps], refs[steps:]
    chunk = parts[0].shape[0]
    low, high = (BAND_ROWS - HALO) * LONGITUDES, HALO * LONGITUDES
    whole[:low] = (own[:low] + below[:low].astype(F32)).astype(BF16)
    whole[low:high] = (own[low:high] + below[low:].astype(F32) + above[:high - low].astype(F32)).astype(BF16)
    whole[high:] = (own[high:] + above[high - low:].astype(F32)).astype(BF16)
    moves = [
        pltpu.make_async_copy(whole.at[pl.ds(pl.multiple_of(order[i], 16), chunk)], part, sems.at[i])
        for i, part in enumerate(parts)
    ]
    for move in moves:
        move.start()
    for move in moves:
        move.wait()


def joined(order, own, above, below, steps):
    band, feats = own.shape
    return call(
        functools.partial(join_kernel, steps),
        [shape(band // steps, feats)] * steps,
        [SMEM] + [VMEM] * 3, [HBM] * steps, (order, own, above, below), flops=2 * own.size,
        scratch=[pltpu.VMEM((band, feats), BF16), pltpu.SemaphoreType.DMA((steps,))],
    )


def weight_grad_kernel(steps, order, *refs):
    (outq_parts, upstream, normed), refs = [refs[i * steps:(i + 1) * steps] for i in range(3)], refs[3 * steps:]
    dkv, dkv_top, dkv_bot, normed_top, normed_bot, grad, outq, up, own, sems = refs
    feats, chunk = outq.shape[1] // 2, outq_parts[0].shape[0]
    groups = [
        [
            pltpu.make_async_copy(part, held.at[pl.ds(pl.multiple_of(order[i], 16), chunk)], sems.at[group, i])
            for i, part in enumerate(parts)
        ]
        for group, (parts, held) in enumerate(((outq_parts, outq), (normed, own), (upstream, up)))
    ]
    for moves in groups:
        for move in moves:
            move.start()

    def product(left, right):
        return lax.dot_general(left, right, (((0,), (0,)), ((), ())), preferred_element_type=F32)

    keyval = product(dkv_top[...], normed_top[...]) + product(dkv_bot[...], normed_bot[...])
    for moves in groups[:2]:
        for move in moves:
            move.wait()
    grad[2 * feats:, :] = (keyval + product(dkv[...].astype(BF16), own[...])).astype(BF16)
    grad[feats:2 * feats, :] = product(outq[:, feats:], own[...]).astype(BF16)
    for move in groups[2]:
        move.wait()
    grad[:feats, :] = product(outq[:, :feats], up[...]).astype(BF16)


def weight_grads(order, outq_parts, upstream, normed, dkv, dkv_halos, normed_halos):
    steps, (chunk, rows), width = len(normed), outq_parts[0].shape, normed[0].shape[1]
    band = steps * chunk
    return call(
        functools.partial(weight_grad_kernel, steps),
        [shape(2 * rows, width)], [SMEM] + [HBM] * (3 * steps) + [VMEM] * 5, [VMEM],
        (order, *outq_parts, *upstream, *normed, dkv, *dkv_halos, *normed_halos),
        flops=2 * width * rows * (2 * band + 2 * HALO * LONGITUDES),
        scratch=[
            pltpu.VMEM((band, rows), BF16), pltpu.VMEM((band, width), BF16), pltpu.VMEM((band, width), BF16),
            pltpu.SemaphoreType.DMA((3, steps)),
        ],
    )[0]


def update_kernel(steps, leads, *refs):
    parts, blocks, (out, left, right, sems) = refs[:steps], refs[steps:2 * steps], refs[2 * steps:]
    feats = right.shape[0] // steps
    carry_out([
        pltpu.make_async_copy(block.at[pl.ds(3 * feats, feats)], right.at[pl.ds(i * feats, feats)], sems.at[i])
        for i, block in enumerate(blocks)
    ])
    for i, part in enumerate(parts):
        left[leads[i]] = part[:, :feats]
    out[...] = nn(jnp.concatenate([left[i] for i in range(steps)], axis=1), right[...]).astype(BF16)


def updates(leads, outq_own, blocks):
    steps, (rows, width), chunk = len(blocks), blocks[0].shape, outq_own[0].shape[0]
    return call(
        functools.partial(update_kernel, steps),
        [shape(chunk, width)], [SMEM] + [VMEM] * steps + [HBM] * steps, [VMEM], (leads, *outq_own, *blocks),
        flops=steps * chunk * rows * width // 2,
        scratch=[
            pltpu.VMEM((steps, chunk, rows // 4), BF16),
            pltpu.VMEM((steps * rows // 4, width), BF16),
            pltpu.SemaphoreType.DMA((steps,)),
        ],
    )[0]


def grad_input_kernel(steps, leads, tokens, gain, *refs):
    outq, dkv, blocks, (grad, left, right, sems) = (
        refs[:steps], refs[steps:2 * steps], refs[2 * steps:3 * steps], refs[3 * steps:]
    )
    rows = right.shape[0] // steps
    feats = rows // 3
    carry_out([
        pltpu.make_async_copy(block.at[pl.ds(0, rows)], right.at[pl.ds(i * rows, rows)], sems.at[i])
        for i, block in enumerate(blocks)
    ])
    for i in range(steps):
        left[leads[i], :, :feats] = outq[i][:, feats:]
        left[leads[i], :, feats:] = dkv[i][...]
    grad_normed = nn(jnp.concatenate([left[i] for i in range(steps)], axis=1), right[...])
    features = tokens[...].astype(F32)
    inverse = lax.rsqrt(jnp.mean(features * features, axis=1, keepdims=True) + 1e-06)
    centred = features * inverse
    scaled = gain[...] * grad_normed
    grad[...] = (inverse * (scaled - centred * jnp.mean(scaled * centred, axis=1, keepdims=True))).astype(BF16)


def grad_inputs(leads, tokens, gain, outq_own, dkv_own, blocks):
    steps, (rows, width), chunk = len(blocks), blocks[0].shape, tokens.shape[0]
    rows = rows * 3 // 4
    return call(
        functools.partial(grad_input_kernel, steps),
        [shape(*tokens.shape)], [SMEM] + [VMEM] * (2 + 2 * steps) + [HBM] * steps, [VMEM],
        (leads, tokens, gain[None, :], *outq_own, *dkv_own, *blocks),
        flops=2 * steps * chunk * rows * width,
        scratch=[
            pltpu.VMEM((steps, chunk, rows), BF16),
            pltpu.VMEM((steps * rows, width), BF16),
            pltpu.SemaphoreType.DMA((steps,)),
        ],
    )[0]


from jax.sharding import Mesh, PartitionSpec as P

WIDTH = 1024
GROUP = ("y", "m", "c")


def owners(halves):
    if halves == 2:
        return [
            lambda y, m, c: (c, 1 - m if c == y else m, y),
            lambda y, m, c: (c, 1 - m if c == y else m, 1 - y),
            lambda y, m, c: (c, m if c == y else 1 - m, 1 - y),
            lambda y, m, c: (c, m if c == y else 1 - m, y),
        ]
    return [
        lambda y, m, c, dm=dm, dc=dc: (c, (m + dm) % halves, (y + dc) % 2) for dc in range(2) for dm in range(halves)
    ]


def passed_along(x, by):
    length = lax.axis_size("z") * 2
    pairs = [(i, i + by) for i in range(length) if 0 <= i + by < length]
    return lax.ppermute(x, ("z", "c"), pairs)


def after(x, *others):
    return lax.optimization_barrier((x, *others))[0]


def on_device(tokens, gain, qkv_weight, out_weight, row_cells, upstream):
    heads = qkv_weight.shape[0]
    feats = heads * HEAD_WIDTH
    band_tokens = BAND_ROWS * LONGITUDES
    chunk = tokens.shape[0]
    halves, layers = lax.axis_size("m"), lax.axis_size("z")
    z, y, m, c = (lax.axis_index(axis) for axis in ("z",) + GROUP)
    grad_scale = 4.0 / math.sqrt(band_tokens * layers * 2)
    band_start = (z * 2 + c) * BAND_ROWS
    cells = lax.dynamic_slice_in_dim(jnp.pad(row_cells, (HALO, HALO)), band_start, EXT_ROWS)

    at = lambda y, m, c: (y * halves + m) * 2 + c
    spots = [(y, m, c) for y in range(2) for m in range(halves) for c in range(2)]
    slots = [[owner(*spot) for spot in spots] for owner in owners(halves)]
    here = lambda table: jnp.asarray(table, jnp.int32)[at(y, m, c)]
    order = here([[(slot[i][1] * 2 + slot[i][2]) * chunk for slot in slots] for i in range(len(spots))])

    def lead(slot, spot):
        far = spots[slot.index(spot)]
        return (far[0] - spot[2]) % 2 * halves + (far[1] - spot[1]) % halves

    leads = here([[lead(slot, spot) for slot in slots] for spot in spots])

    def permuted(x, pairs):
        return lax.ppermute(x, GROUP, [(at(*a), at(*b)) for a, b in pairs])

    def send_back(parts):
        return [permuted(x, list(zip(spots, slot))) for x, slot in zip(parts, slots)]

    def gathered(x, *others):
        sent = lambda slot: permuted(x, list(zip(slot, spots)))
        if halves != 2:
            parts = [sent(slot) for slot in slots]
            return parts, parts
        first, second = lax.optimization_barrier((sent(slots[0]), sent(slots[1])))
        hop = first, second
        first = after(first, *others)
        third = permuted(
            jnp.where(c == y, first, x),
            [(spot, (1 - spot[0], spot[1], spot[0]) if spot[2] == spot[0] else (spot[0], spot[1], spot[0])) for spot in spots],
        )
        fourth = permuted(
            first, [(spot, (spot[0], 1 - spot[1], spot[2])) for spot in spots if spot[2] != spot[0]]
        )
        third, fourth = lax.optimization_barrier((third, fourth))
        return [first, second, third, jnp.where(c == y, x, fourth)], hop

    def from_ahead(x, dm):
        return lax.ppermute(x, "m", [((i + dm) % halves, i) for i in range(halves)])

    def from_sibling(x):
        return lax.ppermute(x, "c", [(0, 1), (1, 0)])

    rows = 3 * feats // layers, feats // layers
    flat_qkv, flat_out = qkv_weight.reshape(3 * feats, WIDTH), out_weight.reshape(feats, WIDTH)
    held = jnp.concatenate([
        lax.dynamic_slice_in_dim(flat, z * size, size, 0) for flat, size in zip((flat_qkv, flat_out), rows)
    ], axis=0)

    def split(qkv, out):
        eighth = jnp.asarray([HEAD_WIDTH ** -0.5, 1.0, 1.0], BF16)[None, :, None, None]
        qkv = (qkv.reshape(heads, 3, HEAD_WIDTH, WIDTH) * eighth).transpose(1, 0, 2, 3)
        return jnp.concatenate([qkv.reshape(3 * feats, WIDTH), out.reshape(feats, WIDTH)], axis=0)

    blocks = [split(flat_qkv, flat_out)]
    sibling = from_sibling(blocks[0])
    group = jnp.where(c == y, blocks[0], sibling)
    group_qkv, group_out = group[:3 * feats].T, group[3 * feats:]

    normed_parts, hop = gathered(norm(tokens, gain))
    *normed_parts, group_qkv, group_out = lax.optimization_barrier((*normed_parts, group_qkv, group_out))
    normed_up, normed_down = halo_rows(order, normed_parts)
    normed_halos = passed_along(normed_up, 1), passed_along(normed_down, -1)
    qkv = projections(order, group_qkv, normed_parts)
    shares = [from_ahead(after(held, qkv), dm) for dm in range(1, halves)]
    upstream_parts, _ = gathered(after(upstream, *normed_parts), qkv)
    kv_top, kv_bot = (nn(x, group_qkv[:, feats:]).astype(BF16) for x in normed_halos)
    order, kv_top, kv_bot, *shares = lax.optimization_barrier((order, kv_top, kv_bot, *shares))
    ahead = [lax.all_gather(part, "z") for part in shares]
    outq_parts, dkv, dkv_top, dkv_bot = attention(cells, order, qkv, kv_top, kv_bot, group_out, upstream_parts)

    ahead = [after(block, dkv_top) for block in ahead]
    ahead = [split(block[:, :rows[0]], block[:, rows[0]:]) for block in ahead]
    blocks += ahead + [sibling] + [from_sibling(block) for block in ahead]
    from_above, from_below = passed_along(dkv_top, -1), passed_along(dkv_bot, 1)
    outq_own = send_back(outq_parts)

    grads = weight_grads(order, outq_parts, upstream_parts, normed_parts, dkv, (dkv_top, dkv_bot), normed_halos)
    grads = lax.psum(grads, ("z", "c"))
    dkv_parts = joined(order, dkv, from_above, from_below, len(slots))
    dkv_own = send_back(dkv_parts)
    update = updates(leads, outq_own, blocks)
    grad_input = grad_inputs(leads, tokens, gain, outq_own, dkv_own, blocks)
    grads, grad_input, update = lax.optimization_barrier((grads, grad_input, update))
    pairs = [((1 - y, m, 1 - y), (y, m, 1 - y)) for y in range(2) for m in range(halves)]
    grads = jnp.where(c == y, grads, permuted(grads, pairs)).astype(F32) * grad_scale
    early, late = grads[:2 * feats], grads[2 * feats:]
    by_head = lambda x: x.reshape(heads, HEAD_WIDTH, WIDTH)
    grad_out = by_head(early[:feats])
    grad_query = early[feats:] * HEAD_WIDTH ** -0.5
    grad_qkv = jnp.concatenate([by_head(grad_query), by_head(late[:feats]), by_head(late[feats:])], axis=1)
    return update, grad_input, grad_qkv, grad_out


def solution(mesh):
    devices = mesh.devices.reshape(mesh.shape["lat"] // 2, 2, mesh.shape["mp"] // 2, 2)
    tokens, weights = P(("z", "y", "m", "c"), None), P(("m", "c"), None, None)
    return jax.shard_map(
        on_device,
        mesh=Mesh(devices, ("z", "y", "m", "c")),
        in_specs=(tokens, P(), weights, weights, P(), tokens),
        out_specs=(tokens, tokens, weights, weights),
        check_vma=False,
    )
```

```python
import functools
import math
import jax
import jax.numpy as jnp
from jax import lax
from jax.experimental import pallas as pl
from jax.experimental.pallas import tpu as pltpu

HEAD_WIDTH = 64
LONGITUDES = 256
BAND_ROWS = 8
HALO = 6
EXT_ROWS = BAND_ROWS + 2 * HALO
LANES = 256
QUERY_ROWS = 4
KEY_ROWS = QUERY_ROWS + 2 * HALO
BLOCK = 8
BLOCKS = LONGITUDES // BLOCK
KEYS = KEY_ROWS * BLOCK
MASKED = -1e30


def nn(a, b):
    return lax.dot_general(a, b, (((1,), (0,)), ((), ())), preferred_element_type=jnp.float32)


def nt(a, b):
    return lax.dot_general(a, b, (((1,), (1,)), ((), ())), preferred_element_type=jnp.float32)


def row_cols(row, start, size):
    return pl.ds(pl.multiple_of(row * LONGITUDES + start, 16), size)


def attention_kernel(
    heads, steps,
    cells, order, qkv, kv_top, kv_bot, weight, *refs,
):
    upstream, refs = refs[:steps], refs[steps:]
    outq_parts, refs = refs[:steps], refs[steps:]
    dkv_own, dkv_top, dkv_bot, held, outq, go, k_s, v_s, kt_s, vt_s, dk_s, dv_s, live_s, near_s, sems = refs
    feats = heads * HEAD_WIDTH
    chunk = BAND_ROWS * LONGITUDES // steps
    moves = [
        pltpu.make_async_copy(part, held.at[pl.ds(i * chunk, chunk)], sems.at[i]) for i, part in enumerate(upstream)
    ]
    for move in moves:
        move.start()
    tile_cols = LANES // heads // QUERY_ROWS
    tile_queries = QUERY_ROWS * tile_cols
    window = tile_cols // BLOCK + 2

    def load_pair(p, carry):
        for first, rows_s, turned_s in ((0, k_s, kt_s), (feats, v_s, vt_s)):
            both = jnp.stack(
                [kv_top[row_cols(row, p * 16, 16), first:first + feats] for row in range(HALO)]
                + [qkv[row_cols(row, p * 16, 16), feats + first:2 * feats + first] for row in range(BAND_ROWS)]
                + [kv_bot[row_cols(row, p * 16, 16), first:first + feats] for row in range(HALO)]
            ).astype(jnp.float32)
            for half in range(2):
                block = both[:, 8 * half:8 * half + 8, :].reshape(EXT_ROWS * BLOCK, feats)
                rows_s[2 * p + half] = block.astype(jnp.bfloat16)
                for upper in range(2):
                    low = upper * QUERY_ROWS * BLOCK
                    turned_s[upper, 2 * p + half] = block[low:low + KEYS].T.astype(jnp.bfloat16)
        for half in range(2):
            col = (2 * p + half) * BLOCK + lax.broadcasted_iota(jnp.int32, (BLOCK, 128), 0)
            for row in range(EXT_ROWS):
                live_s[2 * p + half, row * BLOCK:(row + 1) * BLOCK, :] = jnp.where(col < cells[row], 0.0, MASKED)
        return carry

    lax.fori_loop(0, BLOCKS // 2, load_pair, 0)
    dk_s[...] = jnp.zeros_like(dk_s)
    dv_s[...] = jnp.zeros_like(dv_s)

    lane = lax.broadcasted_iota(jnp.int32, (KEYS, LANES), 1) % tile_queries
    query_row = lane // tile_cols
    query_col = lane % tile_cols
    key = lax.broadcasted_iota(jnp.int32, (KEYS, LANES), 0)
    row_gap = key // BLOCK - query_row
    for j in range(window):
        col_gap = (j - 1) * BLOCK + key % BLOCK - query_col
        near = (row_gap >= 0) & (row_gap <= 2 * HALO) & (col_gap >= -HALO) & (col_gap <= HALO)
        near_s[j] = jnp.where(near, 0.0, MASKED)

    own_head = (
        lax.broadcasted_iota(jnp.int32, (LANES, feats), 0) // tile_queries
        == lax.broadcasted_iota(jnp.int32, (LANES, feats), 1) // HEAD_WIDTH
    )
    own_head_turned = (
        lax.broadcasted_iota(jnp.int32, (feats, LANES), 1) // tile_queries
        == lax.broadcasted_iota(jnp.int32, (feats, LANES), 0) // HEAD_WIDTH
    )
    query_lane = lax.broadcasted_iota(jnp.int32, (1, LANES), 1) % tile_queries

    def spread(ref, upper, start):
        tile = jnp.concatenate([
            ref[row_cols(upper * QUERY_ROWS + row, start, tile_cols), :feats] for row in range(QUERY_ROWS)
        ], axis=0)
        if heads == 1:
            return tile
        stacked = jnp.concatenate([tile] * heads, axis=0)
        return jnp.where(own_head, stacked, jnp.zeros_like(stacked))

    def gather(turned):
        if heads == 1:
            tile = turned.T
        else:
            tall = jnp.where(own_head_turned, turned, 0.0).T
            tile = sum(tall[h * tile_queries:(h + 1) * tile_queries] for h in range(heads))
        return tile.astype(jnp.bfloat16)

    def one_tile(upper, tile):
        start = pl.multiple_of(tile * tile_cols, 16)
        keys = pl.ds(upper * QUERY_ROWS * BLOCK, KEYS)
        index = [(tile * (tile_cols // BLOCK) + j + BLOCKS - 1) % BLOCKS for j in range(window)]
        queries = spread(qkv, upper, start)
        grads = spread(go, upper, start)
        scores = [
            nt(k_s[index[j], keys, :], queries)
            + near_s[j]
            + jnp.concatenate([live_s[index[j], keys, :]] * (LANES // 128), axis=1)
            for j in range(window)
        ]
        highest = jnp.max(functools.reduce(jnp.maximum, scores), axis=0, keepdims=True)
        terms = [jnp.exp(score - highest) for score in scores]
        total = jnp.sum(sum(terms), axis=0, keepdims=True)
        query_cells = jnp.zeros((1, LANES), jnp.int32)
        for row in range(QUERY_ROWS):
            cell = cells[HALO + upper * QUERY_ROWS + row]
            query_cells = jnp.where(query_lane // tile_cols == row, cell, query_cells)
        live = start + query_lane % tile_cols < query_cells
        inverse = jnp.where(live, 1.0 / total, 0.0)
        probs = [term * inverse for term in terms]
        grad_probs = [nt(v_s[index[j], keys, :], grads) for j in range(window)]
        delta = jnp.sum(sum(p * g for p, g in zip(probs, grad_probs)), axis=0, keepdims=True)
        weights = [p.astype(jnp.bfloat16) for p in probs]
        grad_scores = [(p * (g - delta)).astype(jnp.bfloat16) for p, g in zip(probs, grad_probs)]
        for j in range(window):
            dv_s[index[j], keys, :] += nn(weights[j], grads)
            dk_s[index[j], keys, :] += nn(grad_scores[j], queries)
        values_turned = jnp.concatenate([vt_s[upper, index[j]] for j in range(window)], axis=1)
        keys_turned = jnp.concatenate([kt_s[upper, index[j]] for j in range(window)], axis=1)
        heads_out = gather(nn(values_turned, jnp.concatenate(weights, axis=0)))
        grad_query = gather(nn(keys_turned, jnp.concatenate(grad_scores, axis=0)))
        for row in range(QUERY_ROWS):
            at = row_cols(upper * QUERY_ROWS + row, start, tile_cols)
            outq[at, :feats] = heads_out[row * tile_cols:(row + 1) * tile_cols]
            outq[at, feats:] = grad_query[row * tile_cols:(row + 1) * tile_cols]

    def tile_pair(tile, carry):
        for upper in range(2):
            one_tile(upper, tile)
        return carry

    for move in moves:
        move.wait()
    grad_heads = nt(held[...], weight[...]).astype(jnp.bfloat16)
    for i in range(steps):
        go[pl.ds(pl.multiple_of(order[i], 16), chunk)] = grad_heads[i * chunk:(i + 1) * chunk]
    lax.fori_loop(0, LONGITUDES // tile_cols, tile_pair, 0)
    moves = [
        pltpu.make_async_copy(outq.at[pl.ds(pl.multiple_of(order[i], 16), chunk)], part, sems.at[i])
        for i, part in enumerate(outq_parts)
    ]
    for move in moves:
        move.start()

    def store_pair(p, carry):
        for first, sums in ((0, dk_s), (feats, dv_s)):
            both = jnp.concatenate(
                [sums[2 * p + half].reshape(EXT_ROWS, BLOCK, feats) for half in range(2)], axis=1
            )
            for row in range(HALO):
                dkv_top[row_cols(row, p * 16, 16), first:first + feats] = both[row].astype(jnp.bfloat16)
                dkv_bot[row_cols(row, p * 16, 16), first:first + feats] = (
                    both[HALO + BAND_ROWS + row].astype(jnp.bfloat16)
                )
            for row in range(BAND_ROWS):
                dkv_own[row_cols(row, p * 16, 16), first:first + feats] = both[HALO + row]
        return carry

    lax.fori_loop(0, BLOCKS // 2, store_pair, 0)
    for move in moves:
        move.wait()


VMEM = pl.BlockSpec(memory_space=pltpu.VMEM)
SMEM = pl.BlockSpec(memory_space=pltpu.SMEM)
HBM = pl.BlockSpec(memory_space=pl.ANY)
BF16, F32 = jnp.bfloat16, jnp.float32


def shape(rows, cols, kind=BF16):
    return jax.ShapeDtypeStruct((rows, cols), kind)


def call(kernel, out_shape, in_specs, out_specs, args, flops, scratch=(), transcendentals=0):
    moved = sum(x.size * x.dtype.itemsize for x in (*args, *out_shape)) if flops else 0
    return pl.pallas_call(
        kernel,
        out_shape=tuple(out_shape),
        in_specs=list(in_specs),
        out_specs=tuple(out_specs),
        scratch_shapes=list(scratch),
        compiler_params=pltpu.CompilerParams(vmem_limit_bytes=60 * 2**20),
        cost_estimate=pl.CostEstimate(
            flops=flops, transcendentals=transcendentals, bytes_accessed=moved
        ),
    )(*args)


def attention(cells, order, qkv, kv_top, kv_bot, weight, upstream):
    steps, (feats, width), chunk = len(upstream), weight.shape, upstream[0].shape[0]
    heads = feats // HEAD_WIDTH
    window = LANES // heads // QUERY_ROWS // BLOCK + 2
    band, halo = BAND_ROWS * LONGITUDES, HALO * LONGITUDES
    pairs = band * heads * KEYS * window
    results = call(
        functools.partial(attention_kernel, heads, steps),
        [shape(chunk, 2 * feats)] * steps
        + [shape(band, 2 * feats, F32), shape(halo, 2 * feats), shape(halo, 2 * feats)],
        [SMEM, SMEM, VMEM, VMEM, VMEM, VMEM] + [HBM] * steps,
        [HBM] * steps + [VMEM] * 3,
        (cells, order, qkv, kv_top, kv_bot, weight, *upstream),
        flops=12 * pairs * HEAD_WIDTH * heads + 2 * band * weight.size,
        transcendentals=pairs,
        scratch=[
            pltpu.VMEM((band, width), BF16),
            pltpu.VMEM((band, 2 * feats), BF16),
            pltpu.VMEM((band, feats), BF16),
            pltpu.VMEM((BLOCKS, EXT_ROWS * BLOCK, feats), BF16),
            pltpu.VMEM((BLOCKS, EXT_ROWS * BLOCK, feats), BF16),
            pltpu.VMEM((2, BLOCKS, feats, KEYS), BF16),
            pltpu.VMEM((2, BLOCKS, feats, KEYS), BF16),
            pltpu.VMEM((BLOCKS, EXT_ROWS * BLOCK, feats), F32),
            pltpu.VMEM((BLOCKS, EXT_ROWS * BLOCK, feats), F32),
            pltpu.VMEM((BLOCKS, EXT_ROWS * BLOCK, 128), F32),
            pltpu.VMEM((window, KEYS, LANES), F32),
            pltpu.SemaphoreType.DMA((steps,)),
        ],
    )
    return (results[:steps], *results[steps:])


def norm_kernel(tokens, gain, normed):
    features = tokens[...].astype(F32)
    inverse = lax.rsqrt(jnp.mean(features * features, axis=1, keepdims=True) + 1e-06)
    normed[...] = (features * inverse * gain[...]).astype(BF16)


def norm(tokens, gain):
    return call(
        norm_kernel, [shape(*tokens.shape)], [VMEM] * 2, [VMEM], (tokens, gain[None, :]), flops=4 * tokens.size
    )[0]


def stacked_moves(parts, held, sems, first=0):
    chunk = parts[0].shape[0]
    return [
        pltpu.make_async_copy(part, held.at[pl.ds(i * chunk, chunk)], sems.at[first + i]) for i, part in enumerate(parts)
    ]


def carry_out(moves):
    for move in moves:
        move.start()
    for move in moves:
        move.wait()


def halo_kernel(steps, order, *refs):
    parts, (up, down, held, sems) = refs[:steps], refs[steps:]
    chunk = parts[0].shape[0]
    carry_out([
        pltpu.make_async_copy(part, held.at[pl.ds(pl.multiple_of(order[i], 16), chunk)], sems.at[i])
        for i, part in enumerate(parts)
    ])
    halo, rest = HALO * LONGITUDES, (BAND_ROWS - HALO) * LONGITUDES
    carry_out([
        pltpu.make_async_copy(held.at[pl.ds(rest, halo)], up, sems.at[0]),
        pltpu.make_async_copy(held.at[pl.ds(0, halo)], down, sems.at[1]),
    ])


def halo_rows(order, parts):
    steps, width = len(parts), parts[0].shape[1]
    halo = shape(HALO * LONGITUDES, width)
    return call(
        functools.partial(halo_kernel, steps), [halo, halo], [SMEM] + [HBM] * steps, [HBM] * 2, (order, *parts), flops=0,
        scratch=[pltpu.VMEM((BAND_ROWS * LONGITUDES, width), BF16), pltpu.SemaphoreType.DMA((steps,))],
    )


def projection_kernel(steps, feats, order, weight, *refs):
    parts, (qkv, held, sems) = refs[:steps], refs[steps:]
    chunk = parts[0].shape[0]
    carry_out(stacked_moves(parts, held, sems))
    for first in range(0, 3 * feats, feats):
        product = nn(held[...], weight[:, first:first + feats]).astype(BF16)
        for i in range(steps):
            qkv[pl.ds(pl.multiple_of(order[i], 16), chunk), first:first + feats] = product[i * chunk:(i + 1) * chunk]


def projections(order, weight, parts):
    steps, feats, width = len(parts), weight.shape[1] // 3, parts[0].shape[1]
    band = BAND_ROWS * LONGITUDES
    return call(
        functools.partial(projection_kernel, steps, feats),
        [shape(band, 3 * feats)], [SMEM, VMEM] + [HBM] * steps, [VMEM], (order, weight, *parts),
        flops=2 * band * weight.size,
        scratch=[pltpu.VMEM((band, width), BF16), pltpu.SemaphoreType.DMA((steps,))],
    )[0]


def halo_projection_kernel(weight, top, bot, kv_top, kv_bot):
    for halo, out in ((top, kv_top), (bot, kv_bot)):
        out[...] = nn(halo[...], weight[...]).astype(BF16)


def halo_projections(weight, top, bot):
    out = shape(top.shape[0], weight.shape[1])
    return call(
        halo_projection_kernel, [out, out], [VMEM] * 3, [VMEM] * 2, (weight, top, bot),
        flops=4 * top.shape[0] * weight.size,
    )


def join_kernel(steps, order, own, above, below, *refs):
    outq_parts, parts, (whole, sems) = refs[:steps], refs[steps:2 * steps], refs[2 * steps:]
    chunk, feats = outq_parts[0].shape
    moves = [
        pltpu.make_async_copy(outq, part.at[:, pl.ds(0, feats)], sems.at[steps + i])
        for i, (outq, part) in enumerate(zip(outq_parts, parts))
    ]
    for move in moves:
        move.start()
    low, high = (BAND_ROWS - HALO) * LONGITUDES, HALO * LONGITUDES
    whole[:low] = (own[:low] + below[:low].astype(F32)).astype(BF16)
    whole[low:high] = (own[low:high] + below[low:].astype(F32) + above[:high - low].astype(F32)).astype(BF16)
    whole[high:] = (own[high:] + above[high - low:].astype(F32)).astype(BF16)
    carry_out([
        pltpu.make_async_copy(
            whole.at[pl.ds(pl.multiple_of(order[i], 16), chunk)], part.at[:, pl.ds(feats, feats)], sems.at[i]
        )
        for i, part in enumerate(parts)
    ])
    for move in moves:
        move.wait()


def joined(order, own, above, below, outq_parts):
    steps, (chunk, feats) = len(outq_parts), outq_parts[0].shape
    return call(
        functools.partial(join_kernel, steps),
        [shape(chunk, 2 * feats)] * steps,
        [SMEM] + [VMEM] * 3 + [HBM] * steps, [HBM] * steps, (order, own, above, below, *outq_parts), flops=0,
        scratch=[pltpu.VMEM((steps * chunk, feats), BF16), pltpu.SemaphoreType.DMA((2 * steps,))],
    )


def weight_grad_kernel(steps, order, *refs):
    (outq_parts, upstream, normed), refs = [refs[i * steps:(i + 1) * steps] for i in range(3)], refs[3 * steps:]
    dkv, dkv_top, dkv_bot, normed_top, normed_bot, grad, outq, up, own, sems = refs
    feats, chunk = outq.shape[1] // 2, outq_parts[0].shape[0]
    groups = [
        [
            pltpu.make_async_copy(part, held.at[pl.ds(pl.multiple_of(order[i], 16), chunk)], sems.at[group, i])
            for i, part in enumerate(parts)
        ]
        for group, (parts, held) in enumerate(((outq_parts, outq), (normed, own), (upstream, up)))
    ]
    for moves in groups:
        for move in moves:
            move.start()

    def product(left, right):
        return lax.dot_general(left, right, (((0,), (0,)), ((), ())), preferred_element_type=F32)

    keyval = product(dkv_top[...], normed_top[...]) + product(dkv_bot[...], normed_bot[...])
    for moves in groups[:2]:
        for move in moves:
            move.wait()
    grad[2 * feats:, :] = (keyval + product(dkv[...].astype(BF16), own[...])).astype(BF16)
    grad[feats:2 * feats, :] = product(outq[:, feats:], own[...]).astype(BF16)
    for move in groups[2]:
        move.wait()
    grad[:feats, :] = product(outq[:, :feats], up[...]).astype(BF16)


def weight_grads(order, outq_parts, upstream, normed, dkv, dkv_halos, normed_halos):
    steps, (chunk, rows), width = len(normed), outq_parts[0].shape, normed[0].shape[1]
    band = steps * chunk
    return call(
        functools.partial(weight_grad_kernel, steps),
        [shape(2 * rows, width)], [SMEM] + [HBM] * (3 * steps) + [VMEM] * 5, [VMEM],
        (order, *outq_parts, *upstream, *normed, dkv, *dkv_halos, *normed_halos),
        flops=2 * width * rows * (2 * band + 2 * HALO * LONGITUDES),
        scratch=[
            pltpu.VMEM((band, rows), BF16), pltpu.VMEM((band, width), BF16), pltpu.VMEM((band, width), BF16),
            pltpu.SemaphoreType.DMA((3, steps)),
        ],
    )[0]


def token_kernel(steps, leads, tokens, gain, *refs):
    parts, blocks, (update, grad, left, qkv, out, sems) = refs[:steps], refs[steps:2 * steps], refs[2 * steps:]
    feats = out.shape[0] // steps
    carry_out([
        move for i, block in enumerate(blocks) for move in (
            pltpu.make_async_copy(block.at[pl.ds(0, 3 * feats)], qkv.at[pl.ds(3 * i * feats, 3 * feats)], sems.at[i]),
            pltpu.make_async_copy(block.at[pl.ds(3 * feats, feats)], out.at[pl.ds(i * feats, feats)], sems.at[steps + i]),
        )
    ])
    for i, part in enumerate(parts):
        left[leads[i]] = part[...]
    side_by_side = lambda cut: jnp.concatenate([left[i, :, cut] for i in range(steps)], axis=1)
    update[...] = nn(side_by_side(slice(0, feats)), out[...]).astype(BF16)
    grad_normed = nn(side_by_side(slice(feats, None)), qkv[...])
    features = tokens[...].astype(F32)
    inverse = lax.rsqrt(jnp.mean(features * features, axis=1, keepdims=True) + 1e-06)
    centred = features * inverse
    scaled = gain[...] * grad_normed
    grad[...] = (inverse * (scaled - centred * jnp.mean(scaled * centred, axis=1, keepdims=True))).astype(BF16)


def token_outputs(leads, tokens, gain, parts, blocks):
    steps, (rows, width), chunk = len(blocks), blocks[0].shape, tokens.shape[0]
    feats = rows // 4
    return call(
        functools.partial(token_kernel, steps),
        [shape(chunk, width)] * 2, [SMEM] + [VMEM] * (2 + steps) + [HBM] * steps, [VMEM] * 2,
        (leads, tokens, gain[None, :], *parts, *blocks), flops=2 * steps * chunk * rows * width,
        scratch=[
            pltpu.VMEM((steps, chunk, rows), BF16),
            pltpu.VMEM((3 * steps * feats, width), BF16),
            pltpu.VMEM((steps * feats, width), BF16),
            pltpu.SemaphoreType.DMA((2 * steps,)),
        ],
    )


def finish_kernel(scale, flag, mine, other, grad_qkv, grad_out):
    heads = grad_out.shape[0]
    for h in range(heads):
        for i in range(4):
            at = pl.ds((i * heads + h) * HEAD_WIDTH, HEAD_WIDTH)
            part = jnp.where(flag[0] == 1, mine[at, :], other[at, :]).astype(F32)
            if i == 0:
                grad_out[h] = part * scale
            else:
                factor = scale * HEAD_WIDTH ** -0.5 if i == 1 else scale
                grad_qkv[h, (i - 1) * HEAD_WIDTH:i * HEAD_WIDTH, :] = part * factor


def finished(scale, flag, mine, other):
    heads, width = mine.shape[0] // (4 * HEAD_WIDTH), mine.shape[1]
    return call(
        functools.partial(finish_kernel, scale),
        [jax.ShapeDtypeStruct((heads, 3 * HEAD_WIDTH, width), F32), jax.ShapeDtypeStruct((heads, HEAD_WIDTH, width), F32)],
        [SMEM, VMEM, VMEM], [VMEM] * 2, (flag, mine, other), flops=mine.size,
    )


from jax.sharding import Mesh, PartitionSpec as P

WIDTH = 1024
GROUP = ("y", "m", "c")


def owners(halves):
    if halves == 2:
        return [
            lambda y, m, c: (c, 1 - m if c == y else m, y),
            lambda y, m, c: (c, 1 - m if c == y else m, 1 - y),
            lambda y, m, c: (c, m if c == y else 1 - m, 1 - y),
            lambda y, m, c: (c, m if c == y else 1 - m, y),
        ]
    return [
        lambda y, m, c, dm=dm, dc=dc: (c, (m + dm) % halves, (y + dc) % 2) for dc in range(2) for dm in range(halves)
    ]


def passed_along(x, by):
    length = lax.axis_size("z") * 2
    pairs = [(i, i + by) for i in range(length) if 0 <= i + by < length]
    return lax.ppermute(x, ("z", "c"), pairs)


def after(x, *others):
    return lax.optimization_barrier((x, *others))[0]


def on_device(tokens, gain, qkv_weight, out_weight, row_cells, upstream):
    heads = qkv_weight.shape[0]
    feats = heads * HEAD_WIDTH
    band_tokens = BAND_ROWS * LONGITUDES
    chunk = tokens.shape[0]
    halves, layers = lax.axis_size("m"), lax.axis_size("z")
    z, y, m, c = (lax.axis_index(axis) for axis in ("z",) + GROUP)
    grad_scale = 4.0 / math.sqrt(band_tokens * layers * 2)
    band_start = (z * 2 + c) * BAND_ROWS
    cells = lax.dynamic_slice_in_dim(jnp.pad(row_cells, (HALO, HALO)), band_start, EXT_ROWS)

    at = lambda y, m, c: (y * halves + m) * 2 + c
    spots = [(y, m, c) for y in range(2) for m in range(halves) for c in range(2)]
    slots = [[owner(*spot) for spot in spots] for owner in owners(halves)]
    here = lambda table: jnp.asarray(table, jnp.int32)[at(y, m, c)]
    order = here([[(slot[i][1] * 2 + slot[i][2]) * chunk for slot in slots] for i in range(len(spots))])

    def lead(slot, spot):
        far = spots[slot.index(spot)]
        return (far[0] - spot[2]) % 2 * halves + (far[1] - spot[1]) % halves

    leads = here([[lead(slot, spot) for slot in slots] for spot in spots])

    def permuted(x, pairs):
        return lax.ppermute(x, GROUP, [(at(*a), at(*b)) for a, b in pairs])

    def send_back(parts):
        return [permuted(x, list(zip(spots, slot))) for x, slot in zip(parts, slots)]

    def gathered(x, *others):
        sent = lambda slot: permuted(x, list(zip(slot, spots)))
        if halves != 2:
            parts = [sent(slot) for slot in slots]
            return parts, parts
        first, second = lax.optimization_barrier((sent(slots[0]), sent(slots[1])))
        hop = first, second
        first = after(first, *others)
        third = permuted(
            jnp.where(c == y, first, x),
            [(spot, (1 - spot[0], spot[1], spot[0]) if spot[2] == spot[0] else (spot[0], spot[1], spot[0])) for spot in spots],
        )
        fourth = permuted(
            first, [(spot, (spot[0], 1 - spot[1], spot[2])) for spot in spots if spot[2] != spot[0]]
        )
        third, fourth = lax.optimization_barrier((third, fourth))
        return [first, second, third, jnp.where(c == y, x, fourth)], hop

    def from_ahead(x, dm):
        return lax.ppermute(x, "m", [((i + dm) % halves, i) for i in range(halves)])

    def from_sibling(x):
        return lax.ppermute(x, "c", [(0, 1), (1, 0)])

    rows = 3 * feats // layers, feats // layers
    flat_qkv, flat_out = qkv_weight.reshape(3 * feats, WIDTH), out_weight.reshape(feats, WIDTH)
    held = jnp.concatenate([
        lax.dynamic_slice_in_dim(flat, z * size, size, 0) for flat, size in zip((flat_qkv, flat_out), rows)
    ], axis=0)

    def split(qkv, out):
        eighth = jnp.asarray([HEAD_WIDTH ** -0.5, 1.0, 1.0], BF16)[None, :, None, None]
        qkv = (qkv.reshape(heads, 3, HEAD_WIDTH, WIDTH) * eighth).transpose(1, 0, 2, 3)
        return jnp.concatenate([qkv.reshape(3 * feats, WIDTH), out.reshape(feats, WIDTH)], axis=0)

    blocks = [split(flat_qkv, flat_out)]
    sibling = from_sibling(blocks[0])
    group = jnp.where(c == y, blocks[0], sibling)
    group_qkv, group_out = group[:3 * feats].T, group[3 * feats:]

    normed_parts, hop = gathered(norm(tokens, gain))
    *normed_parts, group_qkv, group_out = lax.optimization_barrier((*normed_parts, group_qkv, group_out))
    normed_up, normed_down = halo_rows(order, normed_parts)
    normed_halos = passed_along(normed_up, 1), passed_along(normed_down, -1)
    qkv = projections(order, group_qkv, normed_parts)
    shares = [from_ahead(after(held, qkv), dm) for dm in range(1, halves)]
    upstream_parts, _ = gathered(after(upstream, *normed_parts), qkv)
    kv_top, kv_bot = halo_projections(group_qkv[:, feats:], *normed_halos)
    kv_top, kv_bot, *upstream_parts = lax.optimization_barrier((kv_top, kv_bot, *upstream_parts))
    order, *shares = lax.optimization_barrier((order, *shares))
    ahead = [lax.all_gather(part, "z") for part in shares]
    outq_parts, dkv, dkv_top, dkv_bot = attention(cells, order, qkv, kv_top, kv_bot, group_out, upstream_parts)

    from_above, from_below = passed_along(dkv_top, -1), passed_along(dkv_bot, 1)
    grads = weight_grads(
        after(order, ahead), outq_parts, upstream_parts, normed_parts, dkv, (dkv_top, dkv_bot), normed_halos
    )
    grads_sum = lax.psum(grads, ("z", "c"))
    parts = joined(after(order, grads), dkv, from_above, from_below, outq_parts)
    parts, ahead = lax.optimization_barrier((parts, ahead))
    parts_own = send_back(parts)
    ahead = [split(block[:, :rows[0]], block[:, rows[0]:]) for block in ahead]
    blocks += ahead + [sibling] + [from_sibling(block) for block in ahead]
    update, grad_input = token_outputs(leads, tokens, gain, parts_own, blocks)
    grads = after(grads_sum, *parts_own)
    pairs = [((1 - y, m, 1 - y), (y, m, 1 - y)) for y in range(2) for m in range(halves)]
    flag = after(jnp.reshape(c == y, (1,)).astype(jnp.int32), grad_input, update)
    grad_qkv, grad_out = finished(grad_scale, flag, grads, permuted(grads, pairs))
    return update, grad_input, grad_qkv, grad_out


def solution(mesh):
    devices = mesh.devices.reshape(mesh.shape["lat"] // 2, 2, mesh.shape["mp"] // 2, 2)
    tokens, weights = P(("z", "y", "m", "c"), None), P(("m", "c"), None, None)
    return jax.shard_map(
        on_device,
        mesh=Mesh(devices, ("z", "y", "m", "c")),
        in_specs=(tokens, P(), weights, weights, P(), tokens),
        out_specs=(tokens, tokens, weights, weights),
        check_vma=False,
    )
```

```python
import functools
import math
import jax
import jax.numpy as jnp
from jax import lax
from jax.experimental import pallas as pl
from jax.experimental.pallas import tpu as pltpu

HEAD_WIDTH = 64
LONGITUDES = 256
BAND_ROWS = 8
HALO = 6
EXT_ROWS = BAND_ROWS + 2 * HALO
LANES = 256
QUERY_ROWS = 4
KEY_ROWS = QUERY_ROWS + 2 * HALO
BLOCK = 8
BLOCKS = LONGITUDES // BLOCK
KEYS = KEY_ROWS * BLOCK
MASKED = -1e30


def nn(a, b):
    return lax.dot_general(a, b, (((1,), (0,)), ((), ())), preferred_element_type=jnp.float32)


def nt(a, b):
    return lax.dot_general(a, b, (((1,), (1,)), ((), ())), preferred_element_type=jnp.float32)


def row_cols(row, start, size):
    return pl.ds(pl.multiple_of(row * LONGITUDES + start, 16), size)


def attention_kernel(
    heads, steps,
    cells, order, qkv, kv_top, kv_bot, weight, *refs,
):
    upstream, refs = refs[:steps], refs[steps:]
    outq_parts, refs = refs[:steps], refs[steps:]
    dkv_own, dkv_top, dkv_bot, held, outq, go, k_s, v_s, kt_s, vt_s, dk_s, dv_s, live_s, near_s, sems = refs
    feats = heads * HEAD_WIDTH
    chunk = BAND_ROWS * LONGITUDES // steps
    moves = [
        pltpu.make_async_copy(part, held.at[pl.ds(i * chunk, chunk)], sems.at[i]) for i, part in enumerate(upstream)
    ]
    for move in moves:
        move.start()
    tile_cols = LANES // heads // QUERY_ROWS
    tile_queries = QUERY_ROWS * tile_cols
    window = tile_cols // BLOCK + 2

    def load_pair(p, carry):
        for first, rows_s, turned_s in ((0, k_s, kt_s), (feats, v_s, vt_s)):
            both = jnp.stack(
                [kv_top[row_cols(row, p * 16, 16), first:first + feats] for row in range(HALO)]
                + [qkv[row_cols(row, p * 16, 16), feats + first:2 * feats + first] for row in range(BAND_ROWS)]
                + [kv_bot[row_cols(row, p * 16, 16), first:first + feats] for row in range(HALO)]
            ).astype(jnp.float32)
            for half in range(2):
                block = both[:, 8 * half:8 * half + 8, :].reshape(EXT_ROWS * BLOCK, feats)
                rows_s[2 * p + half] = block.astype(jnp.bfloat16)
                for upper in range(2):
                    low = upper * QUERY_ROWS * BLOCK
                    turned_s[upper, 2 * p + half] = block[low:low + KEYS].T.astype(jnp.bfloat16)
        for half in range(2):
            col = (2 * p + half) * BLOCK + lax.broadcasted_iota(jnp.int32, (BLOCK, 128), 0)
            for row in range(EXT_ROWS):
                live_s[2 * p + half, row * BLOCK:(row + 1) * BLOCK, :] = jnp.where(col < cells[row], 0.0, MASKED)
        return carry

    lax.fori_loop(0, BLOCKS // 2, load_pair, 0)
    dk_s[...] = jnp.zeros_like(dk_s)
    dv_s[...] = jnp.zeros_like(dv_s)

    lane = lax.broadcasted_iota(jnp.int32, (KEYS, LANES), 1) % tile_queries
    query_row = lane // tile_cols
    query_col = lane % tile_cols
    key = lax.broadcasted_iota(jnp.int32, (KEYS, LANES), 0)
    row_gap = key // BLOCK - query_row
    for j in range(window):
        col_gap = (j - 1) * BLOCK + key % BLOCK - query_col
        near = (row_gap >= 0) & (row_gap <= 2 * HALO) & (col_gap >= -HALO) & (col_gap <= HALO)
        near_s[j] = jnp.where(near, 0.0, MASKED)

    own_head = (
        lax.broadcasted_iota(jnp.int32, (LANES, feats), 0) // tile_queries
        == lax.broadcasted_iota(jnp.int32, (LANES, feats), 1) // HEAD_WIDTH
    )
    own_head_turned = (
        lax.broadcasted_iota(jnp.int32, (feats, LANES), 1) // tile_queries
        == lax.broadcasted_iota(jnp.int32, (feats, LANES), 0) // HEAD_WIDTH
    )
    query_lane = lax.broadcasted_iota(jnp.int32, (1, LANES), 1) % tile_queries

    def spread(ref, upper, start):
        tile = jnp.concatenate([
            ref[row_cols(upper * QUERY_ROWS + row, start, tile_cols), :feats] for row in range(QUERY_ROWS)
        ], axis=0)
        if heads == 1:
            return tile
        stacked = jnp.concatenate([tile] * heads, axis=0)
        return jnp.where(own_head, stacked, jnp.zeros_like(stacked))

    def gather(turned):
        if heads == 1:
            tile = turned.T
        else:
            tall = jnp.where(own_head_turned, turned, 0.0).T
            tile = sum(tall[h * tile_queries:(h + 1) * tile_queries] for h in range(heads))
        return tile.astype(jnp.bfloat16)

    def one_tile(upper, tile):
        start = pl.multiple_of(tile * tile_cols, 16)
        keys = pl.ds(upper * QUERY_ROWS * BLOCK, KEYS)
        index = [(tile * (tile_cols // BLOCK) + j + BLOCKS - 1) % BLOCKS for j in range(window)]
        queries = spread(qkv, upper, start)
        grads = spread(go, upper, start)
        scores = [
            nt(k_s[index[j], keys, :], queries)
            + near_s[j]
            + jnp.concatenate([live_s[index[j], keys, :]] * (LANES // 128), axis=1)
            for j in range(window)
        ]
        highest = jnp.max(functools.reduce(jnp.maximum, scores), axis=0, keepdims=True)
        terms = [jnp.exp(score - highest) for score in scores]
        total = jnp.sum(sum(terms), axis=0, keepdims=True)
        query_cells = jnp.zeros((1, LANES), jnp.int32)
        for row in range(QUERY_ROWS):
            cell = cells[HALO + upper * QUERY_ROWS + row]
            query_cells = jnp.where(query_lane // tile_cols == row, cell, query_cells)
        live = start + query_lane % tile_cols < query_cells
        inverse = jnp.where(live, 1.0 / total, 0.0)
        probs = [term * inverse for term in terms]
        grad_probs = [nt(v_s[index[j], keys, :], grads) for j in range(window)]
        delta = jnp.sum(sum(p * g for p, g in zip(probs, grad_probs)), axis=0, keepdims=True)
        weights = [p.astype(jnp.bfloat16) for p in probs]
        grad_scores = [(p * (g - delta)).astype(jnp.bfloat16) for p, g in zip(probs, grad_probs)]
        for j in range(window):
            dv_s[index[j], keys, :] += nn(weights[j], grads)
            dk_s[index[j], keys, :] += nn(grad_scores[j], queries)
        values_turned = jnp.concatenate([vt_s[upper, index[j]] for j in range(window)], axis=1)
        keys_turned = jnp.concatenate([kt_s[upper, index[j]] for j in range(window)], axis=1)
        heads_out = gather(nn(values_turned, jnp.concatenate(weights, axis=0)))
        grad_query = gather(nn(keys_turned, jnp.concatenate(grad_scores, axis=0)))
        for row in range(QUERY_ROWS):
            at = row_cols(upper * QUERY_ROWS + row, start, tile_cols)
            outq[at, :feats] = heads_out[row * tile_cols:(row + 1) * tile_cols]
            outq[at, feats:] = grad_query[row * tile_cols:(row + 1) * tile_cols]

    def tile_pair(tile, carry):
        for upper in range(2):
            one_tile(upper, tile)
        return carry

    for move in moves:
        move.wait()
    grad_heads = nt(held[...], weight[...]).astype(jnp.bfloat16)
    for i in range(steps):
        go[pl.ds(pl.multiple_of(order[i], 16), chunk)] = grad_heads[i * chunk:(i + 1) * chunk]
    lax.fori_loop(0, LONGITUDES // tile_cols, tile_pair, 0)
    moves = [
        pltpu.make_async_copy(outq.at[pl.ds(pl.multiple_of(order[i], 16), chunk)], part, sems.at[i])
        for i, part in enumerate(outq_parts)
    ]
    for move in moves:
        move.start()

    def store_pair(p, carry):
        for first, sums in ((0, dk_s), (feats, dv_s)):
            both = jnp.concatenate(
                [sums[2 * p + half].reshape(EXT_ROWS, BLOCK, feats) for half in range(2)], axis=1
            )
            for row in range(HALO):
                dkv_top[row_cols(row, p * 16, 16), first:first + feats] = both[row].astype(jnp.bfloat16)
                dkv_bot[row_cols(row, p * 16, 16), first:first + feats] = (
                    both[HALO + BAND_ROWS + row].astype(jnp.bfloat16)
                )
            for row in range(BAND_ROWS):
                dkv_own[row_cols(row, p * 16, 16), first:first + feats] = both[HALO + row]
        return carry

    lax.fori_loop(0, BLOCKS // 2, store_pair, 0)
    for move in moves:
        move.wait()


VMEM = pl.BlockSpec(memory_space=pltpu.VMEM)
SMEM = pl.BlockSpec(memory_space=pltpu.SMEM)
HBM = pl.BlockSpec(memory_space=pl.ANY)
BF16, F32 = jnp.bfloat16, jnp.float32


def shape(rows, cols, kind=BF16):
    return jax.ShapeDtypeStruct((rows, cols), kind)


def call(kernel, out_shape, in_specs, out_specs, args, flops, scratch=(), transcendentals=0):
    moved = sum(x.size * x.dtype.itemsize for x in (*args, *out_shape)) if flops else 0
    return pl.pallas_call(
        kernel,
        out_shape=tuple(out_shape),
        in_specs=list(in_specs),
        out_specs=tuple(out_specs),
        scratch_shapes=list(scratch),
        compiler_params=pltpu.CompilerParams(vmem_limit_bytes=60 * 2**20),
        cost_estimate=pl.CostEstimate(
            flops=flops, transcendentals=transcendentals, bytes_accessed=moved
        ),
    )(*args)


def attention(cells, order, qkv, kv_top, kv_bot, weight, upstream):
    steps, (feats, width), chunk = len(upstream), weight.shape, upstream[0].shape[0]
    heads = feats // HEAD_WIDTH
    window = LANES // heads // QUERY_ROWS // BLOCK + 2
    band, halo = BAND_ROWS * LONGITUDES, HALO * LONGITUDES
    pairs = band * heads * KEYS * window
    results = call(
        functools.partial(attention_kernel, heads, steps),
        [shape(chunk, 2 * feats)] * steps
        + [shape(band, 2 * feats, F32), shape(halo, 2 * feats), shape(halo, 2 * feats)],
        [SMEM, SMEM, VMEM, VMEM, VMEM, VMEM] + [HBM] * steps,
        [HBM] * steps + [VMEM] * 3,
        (cells, order, qkv, kv_top, kv_bot, weight, *upstream),
        flops=12 * pairs * HEAD_WIDTH * heads + 2 * band * weight.size,
        transcendentals=pairs,
        scratch=[
            pltpu.VMEM((band, width), BF16),
            pltpu.VMEM((band, 2 * feats), BF16),
            pltpu.VMEM((band, feats), BF16),
            pltpu.VMEM((BLOCKS, EXT_ROWS * BLOCK, feats), BF16),
            pltpu.VMEM((BLOCKS, EXT_ROWS * BLOCK, feats), BF16),
            pltpu.VMEM((2, BLOCKS, feats, KEYS), BF16),
            pltpu.VMEM((2, BLOCKS, feats, KEYS), BF16),
            pltpu.VMEM((BLOCKS, EXT_ROWS * BLOCK, feats), F32),
            pltpu.VMEM((BLOCKS, EXT_ROWS * BLOCK, feats), F32),
            pltpu.VMEM((BLOCKS, EXT_ROWS * BLOCK, 128), F32),
            pltpu.VMEM((window, KEYS, LANES), F32),
            pltpu.SemaphoreType.DMA((steps,)),
        ],
    )
    return (results[:steps], *results[steps:])


def norm_kernel(tokens, gain, normed):
    features = tokens[...].astype(F32)
    inverse = lax.rsqrt(jnp.mean(features * features, axis=1, keepdims=True) + 1e-06)
    normed[...] = (features * inverse * gain[...]).astype(BF16)


def norm(tokens, gain):
    return call(
        norm_kernel, [shape(*tokens.shape)], [VMEM] * 2, [VMEM], (tokens, gain[None, :]), flops=4 * tokens.size
    )[0]


def stacked_moves(parts, held, sems, first=0):
    chunk = parts[0].shape[0]
    return [
        pltpu.make_async_copy(part, held.at[pl.ds(i * chunk, chunk)], sems.at[first + i]) for i, part in enumerate(parts)
    ]


def carry_out(moves):
    for move in moves:
        move.start()
    for move in moves:
        move.wait()


def halo_kernel(steps, order, *refs):
    parts, (up, down, held, sems) = refs[:steps], refs[steps:]
    chunk = parts[0].shape[0]
    carry_out([
        pltpu.make_async_copy(part, held.at[pl.ds(pl.multiple_of(order[i], 16), chunk)], sems.at[i])
        for i, part in enumerate(parts)
    ])
    halo, rest = HALO * LONGITUDES, (BAND_ROWS - HALO) * LONGITUDES
    carry_out([
        pltpu.make_async_copy(held.at[pl.ds(rest, halo)], up, sems.at[0]),
        pltpu.make_async_copy(held.at[pl.ds(0, halo)], down, sems.at[1]),
    ])


def halo_rows(order, parts):
    steps, width = len(parts), parts[0].shape[1]
    halo = shape(HALO * LONGITUDES, width)
    return call(
        functools.partial(halo_kernel, steps), [halo, halo], [SMEM] + [HBM] * steps, [HBM] * 2, (order, *parts), flops=0,
        scratch=[pltpu.VMEM((BAND_ROWS * LONGITUDES, width), BF16), pltpu.SemaphoreType.DMA((steps,))],
    )


def projection_kernel(steps, feats, order, weight, *refs):
    parts, (qkv, held, sems) = refs[:steps], refs[steps:]
    chunk = parts[0].shape[0]
    carry_out(stacked_moves(parts, held, sems))
    for first in range(0, 3 * feats, feats):
        product = nn(held[...], weight[:, first:first + feats]).astype(BF16)
        for i in range(steps):
            qkv[pl.ds(pl.multiple_of(order[i], 16), chunk), first:first + feats] = product[i * chunk:(i + 1) * chunk]


def projections(order, weight, parts):
    steps, feats, width = len(parts), weight.shape[1] // 3, parts[0].shape[1]
    band = BAND_ROWS * LONGITUDES
    return call(
        functools.partial(projection_kernel, steps, feats),
        [shape(band, 3 * feats)], [SMEM, VMEM] + [HBM] * steps, [VMEM], (order, weight, *parts),
        flops=2 * band * weight.size,
        scratch=[pltpu.VMEM((band, width), BF16), pltpu.SemaphoreType.DMA((steps,))],
    )[0]


def halo_projection_kernel(weight, top, bot, kv_top, kv_bot):
    for halo, out in ((top, kv_top), (bot, kv_bot)):
        out[...] = nn(halo[...], weight[...]).astype(BF16)


def halo_projections(weight, top, bot):
    out = shape(top.shape[0], weight.shape[1])
    return call(
        halo_projection_kernel, [out, out], [VMEM] * 3, [VMEM] * 2, (weight, top, bot),
        flops=4 * top.shape[0] * weight.size,
    )


def join_kernel(steps, order, own, above, below, *refs):
    outq_parts, parts, whole = refs[:steps], refs[steps:2 * steps], refs[-1]
    chunk, feats = outq_parts[0].shape
    low, high = (BAND_ROWS - HALO) * LONGITUDES, HALO * LONGITUDES
    for outq, part in zip(outq_parts, parts):
        part[:, :feats] = outq[...]
    whole[:low] = (own[:low] + below[:low].astype(F32)).astype(BF16)
    whole[low:high] = (own[low:high] + below[low:].astype(F32) + above[:high - low].astype(F32)).astype(BF16)
    whole[high:] = (own[high:] + above[high - low:].astype(F32)).astype(BF16)
    for i, part in enumerate(parts):
        part[:, feats:] = whole[pl.ds(pl.multiple_of(order[i], 16), chunk), :]


def joined(order, own, above, below, outq_parts):
    steps, (chunk, feats) = len(outq_parts), outq_parts[0].shape
    return call(
        functools.partial(join_kernel, steps),
        [shape(chunk, 2 * feats)] * steps,
        [SMEM] + [VMEM] * (3 + steps), [VMEM] * steps, (order, own, above, below, *outq_parts), flops=0,
        scratch=[pltpu.VMEM((steps * chunk, feats), BF16)],
    )


def weight_grad_kernel(steps, order, *refs):
    (outq_parts, upstream, normed), refs = [refs[i * steps:(i + 1) * steps] for i in range(3)], refs[3 * steps:]
    dkv, dkv_top, dkv_bot, normed_top, normed_bot, grad, outq, up, own, sems = refs
    feats, chunk = outq.shape[1] // 2, outq_parts[0].shape[0]
    groups = [
        [
            pltpu.make_async_copy(part, held.at[pl.ds(pl.multiple_of(order[i], 16), chunk)], sems.at[group, i])
            for i, part in enumerate(parts)
        ]
        for group, (parts, held) in enumerate(((outq_parts, outq), (normed, own), (upstream, up)))
    ]
    for moves in groups:
        for move in moves:
            move.start()

    def product(left, right):
        return lax.dot_general(left, right, (((0,), (0,)), ((), ())), preferred_element_type=F32)

    keyval = product(dkv_top[...], normed_top[...]) + product(dkv_bot[...], normed_bot[...])
    for moves in groups[:2]:
        for move in moves:
            move.wait()
    grad[2 * feats:, :] = (keyval + product(dkv[...].astype(BF16), own[...])).astype(BF16)
    grad[feats:2 * feats, :] = product(outq[:, feats:], own[...]).astype(BF16)
    for move in groups[2]:
        move.wait()
    grad[:feats, :] = product(outq[:, :feats], up[...]).astype(BF16)


def weight_grads(order, outq_parts, upstream, normed, dkv, dkv_halos, normed_halos):
    steps, (chunk, rows), width = len(normed), outq_parts[0].shape, normed[0].shape[1]
    band = steps * chunk
    return call(
        functools.partial(weight_grad_kernel, steps),
        [shape(2 * rows, width)], [SMEM] + [HBM] * (3 * steps) + [VMEM] * 5, [VMEM],
        (order, *outq_parts, *upstream, *normed, dkv, *dkv_halos, *normed_halos),
        flops=2 * width * rows * (2 * band + 2 * HALO * LONGITUDES),
        scratch=[
            pltpu.VMEM((band, rows), BF16), pltpu.VMEM((band, width), BF16), pltpu.VMEM((band, width), BF16),
            pltpu.SemaphoreType.DMA((3, steps)),
        ],
    )[0]


def token_kernel(steps, leads, tokens, gain, *refs):
    parts, blocks, (update, grad, left, qkv, out, sems) = refs[:steps], refs[steps:2 * steps], refs[2 * steps:]
    feats = out.shape[0] // steps
    carry_out([
        move for i, block in enumerate(blocks) for move in (
            pltpu.make_async_copy(block.at[pl.ds(0, 3 * feats)], qkv.at[pl.ds(3 * i * feats, 3 * feats)], sems.at[i]),
            pltpu.make_async_copy(block.at[pl.ds(3 * feats, feats)], out.at[pl.ds(i * feats, feats)], sems.at[steps + i]),
        )
    ])
    for i, part in enumerate(parts):
        left[leads[i]] = part[...]
    side_by_side = lambda cut: jnp.concatenate([left[i, :, cut] for i in range(steps)], axis=1)
    update[...] = nn(side_by_side(slice(0, feats)), out[...]).astype(BF16)
    grad_normed = nn(side_by_side(slice(feats, None)), qkv[...])
    features = tokens[...].astype(F32)
    inverse = lax.rsqrt(jnp.mean(features * features, axis=1, keepdims=True) + 1e-06)
    centred = features * inverse
    scaled = gain[...] * grad_normed
    grad[...] = (inverse * (scaled - centred * jnp.mean(scaled * centred, axis=1, keepdims=True))).astype(BF16)


def token_outputs(leads, tokens, gain, parts, blocks):
    steps, (rows, width), chunk = len(blocks), blocks[0].shape, tokens.shape[0]
    feats = rows // 4
    return call(
        functools.partial(token_kernel, steps),
        [shape(chunk, width)] * 2, [SMEM] + [VMEM] * (2 + steps) + [HBM] * steps, [VMEM] * 2,
        (leads, tokens, gain[None, :], *parts, *blocks), flops=2 * steps * chunk * rows * width,
        scratch=[
            pltpu.VMEM((steps, chunk, rows), BF16),
            pltpu.VMEM((3 * steps * feats, width), BF16),
            pltpu.VMEM((steps * feats, width), BF16),
            pltpu.SemaphoreType.DMA((2 * steps,)),
        ],
    )


def finish_kernel(scale, flag, mine, other, grad_qkv, grad_out):
    heads = grad_out.shape[0]
    for h in range(heads):
        for i in range(4):
            at = pl.ds((i * heads + h) * HEAD_WIDTH, HEAD_WIDTH)
            part = jnp.where(flag[0] == 1, mine[at, :], other[at, :]).astype(F32)
            if i == 0:
                grad_out[h] = part * scale
            else:
                factor = scale * HEAD_WIDTH ** -0.5 if i == 1 else scale
                grad_qkv[h, (i - 1) * HEAD_WIDTH:i * HEAD_WIDTH, :] = part * factor


def finished(scale, flag, mine, other):
    heads, width = mine.shape[0] // (4 * HEAD_WIDTH), mine.shape[1]
    return call(
        functools.partial(finish_kernel, scale),
        [jax.ShapeDtypeStruct((heads, 3 * HEAD_WIDTH, width), F32), jax.ShapeDtypeStruct((heads, HEAD_WIDTH, width), F32)],
        [SMEM, VMEM, VMEM], [VMEM] * 2, (flag, mine, other), flops=mine.size,
    )


from jax.sharding import Mesh, PartitionSpec as P

WIDTH = 1024
GROUP = ("y", "m", "c")


def owners(halves):
    if halves == 2:
        return [
            lambda y, m, c: (c, 1 - m if c == y else m, y),
            lambda y, m, c: (c, 1 - m if c == y else m, 1 - y),
            lambda y, m, c: (c, m if c == y else 1 - m, 1 - y),
            lambda y, m, c: (c, m if c == y else 1 - m, y),
        ]
    return [
        lambda y, m, c, dm=dm, dc=dc: (c, (m + dm) % halves, (y + dc) % 2) for dc in range(2) for dm in range(halves)
    ]


def passed_along(x, by):
    length = lax.axis_size("z") * 2
    pairs = [(i, i + by) for i in range(length) if 0 <= i + by < length]
    return lax.ppermute(x, ("z", "c"), pairs)


def after(x, *others):
    return lax.optimization_barrier((x, *others))[0]


def on_device(tokens, gain, qkv_weight, out_weight, row_cells, upstream):
    heads = qkv_weight.shape[0]
    feats = heads * HEAD_WIDTH
    band_tokens = BAND_ROWS * LONGITUDES
    chunk = tokens.shape[0]
    halves, layers = lax.axis_size("m"), lax.axis_size("z")
    z, y, m, c = (lax.axis_index(axis) for axis in ("z",) + GROUP)
    grad_scale = 4.0 / math.sqrt(band_tokens * layers * 2)
    band_start = (z * 2 + c) * BAND_ROWS
    cells = lax.dynamic_slice_in_dim(jnp.pad(row_cells, (HALO, HALO)), band_start, EXT_ROWS)

    at = lambda y, m, c: (y * halves + m) * 2 + c
    spots = [(y, m, c) for y in range(2) for m in range(halves) for c in range(2)]
    slots = [[owner(*spot) for spot in spots] for owner in owners(halves)]
    here = lambda table: jnp.asarray(table, jnp.int32)[at(y, m, c)]
    order = here([[(slot[i][1] * 2 + slot[i][2]) * chunk for slot in slots] for i in range(len(spots))])

    def lead(slot, spot):
        far = spots[slot.index(spot)]
        return (far[0] - spot[2]) % 2 * halves + (far[1] - spot[1]) % halves

    leads = here([[lead(slot, spot) for slot in slots] for spot in spots])

    def permuted(x, pairs):
        return lax.ppermute(x, GROUP, [(at(*a), at(*b)) for a, b in pairs])

    def send_back(parts):
        return [permuted(x, list(zip(spots, slot))) for x, slot in zip(parts, slots)]

    def gathered(x, *others):
        sent = lambda slot: permuted(x, list(zip(slot, spots)))
        if halves != 2:
            parts = [sent(slot) for slot in slots]
            return parts, parts
        first, second = lax.optimization_barrier((sent(slots[0]), sent(slots[1])))
        hop = first, second
        first = after(first, *others)
        third = permuted(
            jnp.where(c == y, first, x),
            [(spot, (1 - spot[0], spot[1], spot[0]) if spot[2] == spot[0] else (spot[0], spot[1], spot[0])) for spot in spots],
        )
        fourth = permuted(
            first, [(spot, (spot[0], 1 - spot[1], spot[2])) for spot in spots if spot[2] != spot[0]]
        )
        third, fourth = lax.optimization_barrier((third, fourth))
        return [first, second, third, jnp.where(c == y, x, fourth)], hop

    def from_ahead(x, dm):
        return lax.ppermute(x, "m", [((i + dm) % halves, i) for i in range(halves)])

    def from_sibling(x):
        return lax.ppermute(x, "c", [(0, 1), (1, 0)])

    def split(qkv, out):
        eighth = jnp.asarray([HEAD_WIDTH ** -0.5, 1.0, 1.0], BF16)[None, :, None, None]
        qkv = (qkv.reshape(heads, 3, HEAD_WIDTH, WIDTH) * eighth).transpose(1, 0, 2, 3)
        return jnp.concatenate([qkv.reshape(3 * feats, WIDTH), out.reshape(feats, WIDTH)], axis=0)

    blocks = [split(qkv_weight, out_weight)]
    sibling = from_sibling(blocks[0])
    group = jnp.where(c == y, blocks[0], sibling)
    group_qkv, group_out = group[:3 * feats].T, group[3 * feats:]

    normed_parts, hop = gathered(norm(tokens, gain))
    *normed_parts, group_qkv, group_out = lax.optimization_barrier((*normed_parts, group_qkv, group_out))
    normed_up, normed_down = halo_rows(order, normed_parts)
    normed_halos = passed_along(normed_up, 1), passed_along(normed_down, -1)
    qkv = projections(order, group_qkv, normed_parts)
    upstream_parts, _ = gathered(after(upstream, *normed_parts), qkv)
    kv_top, kv_bot = halo_projections(group_qkv[:, feats:], *normed_halos)
    kv_top, kv_bot, *upstream_parts = lax.optimization_barrier((kv_top, kv_bot, *upstream_parts))
    ahead = [from_ahead(after(blocks[0], *upstream_parts), dm) for dm in range(1, halves)]
    outq_parts, dkv, dkv_top, dkv_bot = attention(cells, order, qkv, kv_top, kv_bot, group_out, upstream_parts)

    from_above, from_below = passed_along(dkv_top, -1), passed_along(dkv_bot, 1)
    grads = weight_grads(
        order, outq_parts, upstream_parts, normed_parts, dkv, (dkv_top, dkv_bot), normed_halos
    )
    grads_sum = lax.psum(grads, ("z", "c"))
    parts = joined(after(order, grads), dkv, from_above, from_below, outq_parts)
    parts, ahead = lax.optimization_barrier((parts, ahead))
    parts_own = send_back(parts)
    blocks += ahead + [sibling] + [from_sibling(block) for block in ahead]
    update, grad_input = token_outputs(leads, tokens, gain, parts_own, blocks)
    grads = after(grads_sum, *parts_own)
    pairs = [((1 - y, m, 1 - y), (y, m, 1 - y)) for y in range(2) for m in range(halves)]
    flag = after(jnp.reshape(c == y, (1,)).astype(jnp.int32), grad_input, update)
    grad_qkv, grad_out = finished(grad_scale, flag, grads, permuted(grads, pairs))
    return update, grad_input, grad_qkv, grad_out


def solution(mesh):
    devices = mesh.devices.reshape(mesh.shape["lat"] // 2, 2, mesh.shape["mp"] // 2, 2)
    tokens, weights = P(("z", "y", "m", "c"), None), P(("m", "c"), None, None)
    return jax.shard_map(
        on_device,
        mesh=Mesh(devices, ("z", "y", "m", "c")),
        in_specs=(tokens, P(), weights, weights, P(), tokens),
        out_specs=(tokens, tokens, weights, weights),
        check_vma=False,
    )
```

```python
import functools
import math
import jax
import jax.numpy as jnp
from jax import lax
from jax.experimental import pallas as pl
from jax.experimental.pallas import tpu as pltpu

HEAD_WIDTH = 64
LONGITUDES = 256
BAND_ROWS = 8
HALO = 6
EXT_ROWS = BAND_ROWS + 2 * HALO
LANES = 256
QUERY_ROWS = 4
KEY_ROWS = QUERY_ROWS + 2 * HALO
BLOCK = 8
BLOCKS = LONGITUDES // BLOCK
KEYS = KEY_ROWS * BLOCK
MASKED = -1e30


def nn(a, b):
    return lax.dot_general(a, b, (((1,), (0,)), ((), ())), preferred_element_type=jnp.float32)


def nt(a, b):
    return lax.dot_general(a, b, (((1,), (1,)), ((), ())), preferred_element_type=jnp.float32)


def row_cols(row, start, size):
    return pl.ds(pl.multiple_of(row * LONGITUDES + start, 16), size)


def attention_kernel(
    heads, steps,
    cells, order, qkv, kv_top, kv_bot, weight, *refs,
):
    upstream, refs = refs[:steps], refs[steps:]
    outq_parts, refs = refs[:steps], refs[steps:]
    dkv_own, dkv_top, dkv_bot, held, outq, go, k_s, v_s, kt_s, vt_s, dk_s, dv_s, live_s, near_s, sems = refs
    feats = heads * HEAD_WIDTH
    chunk = BAND_ROWS * LONGITUDES // steps
    moves = [
        pltpu.make_async_copy(part, held.at[pl.ds(i * chunk, chunk)], sems.at[i]) for i, part in enumerate(upstream)
    ]
    for move in moves:
        move.start()
    tile_cols = LANES // heads // QUERY_ROWS
    tile_queries = QUERY_ROWS * tile_cols
    window = tile_cols // BLOCK + 2

    def load_pair(p, carry):
        for first, rows_s, turned_s in ((0, k_s, kt_s), (feats, v_s, vt_s)):
            both = jnp.stack(
                [kv_top[row_cols(row, p * 16, 16), first:first + feats] for row in range(HALO)]
                + [qkv[row_cols(row, p * 16, 16), feats + first:2 * feats + first] for row in range(BAND_ROWS)]
                + [kv_bot[row_cols(row, p * 16, 16), first:first + feats] for row in range(HALO)]
            ).astype(jnp.float32)
            for half in range(2):
                block = both[:, 8 * half:8 * half + 8, :].reshape(EXT_ROWS * BLOCK, feats)
                rows_s[2 * p + half] = block.astype(jnp.bfloat16)
                for upper in range(2):
                    low = upper * QUERY_ROWS * BLOCK
                    turned_s[upper, 2 * p + half] = block[low:low + KEYS].T.astype(jnp.bfloat16)
        for half in range(2):
            col = (2 * p + half) * BLOCK + lax.broadcasted_iota(jnp.int32, (BLOCK, 128), 0)
            for row in range(EXT_ROWS):
                live_s[2 * p + half, row * BLOCK:(row + 1) * BLOCK, :] = jnp.where(col < cells[row], 0.0, MASKED)
        return carry

    lax.fori_loop(0, BLOCKS // 2, load_pair, 0)
    dk_s[...] = jnp.zeros_like(dk_s)
    dv_s[...] = jnp.zeros_like(dv_s)

    lane = lax.broadcasted_iota(jnp.int32, (KEYS, LANES), 1) % tile_queries
    query_row = lane // tile_cols
    query_col = lane % tile_cols
    key = lax.broadcasted_iota(jnp.int32, (KEYS, LANES), 0)
    row_gap = key // BLOCK - query_row
    for j in range(window):
        col_gap = (j - 1) * BLOCK + key % BLOCK - query_col
        near = (row_gap >= 0) & (row_gap <= 2 * HALO) & (col_gap >= -HALO) & (col_gap <= HALO)
        near_s[j] = jnp.where(near, 0.0, MASKED)

    own_head = (
        lax.broadcasted_iota(jnp.int32, (LANES, feats), 0) // tile_queries
        == lax.broadcasted_iota(jnp.int32, (LANES, feats), 1) // HEAD_WIDTH
    )
    own_head_turned = (
        lax.broadcasted_iota(jnp.int32, (feats, LANES), 1) // tile_queries
        == lax.broadcasted_iota(jnp.int32, (feats, LANES), 0) // HEAD_WIDTH
    )
    query_lane = lax.broadcasted_iota(jnp.int32, (1, LANES), 1) % tile_queries

    def spread(ref, upper, start):
        tile = jnp.concatenate([
            ref[row_cols(upper * QUERY_ROWS + row, start, tile_cols), :feats] for row in range(QUERY_ROWS)
        ], axis=0)
        if heads == 1:
            return tile
        stacked = jnp.concatenate([tile] * heads, axis=0)
        return jnp.where(own_head, stacked, jnp.zeros_like(stacked))

    def gather(turned):
        if heads == 1:
            tile = turned.T
        else:
            tall = jnp.where(own_head_turned, turned, 0.0).T
            tile = sum(tall[h * tile_queries:(h + 1) * tile_queries] for h in range(heads))
        return tile.astype(jnp.bfloat16)

    def one_tile(upper, tile):
        start = pl.multiple_of(tile * tile_cols, 16)
        keys = pl.ds(upper * QUERY_ROWS * BLOCK, KEYS)
        index = [(tile * (tile_cols // BLOCK) + j + BLOCKS - 1) % BLOCKS for j in range(window)]
        queries = spread(qkv, upper, start)
        grads = spread(go, upper, start)
        scores = [
            nt(k_s[index[j], keys, :], queries)
            + near_s[j]
            + jnp.concatenate([live_s[index[j], keys, :]] * (LANES // 128), axis=1)
            for j in range(window)
        ]
        highest = jnp.max(functools.reduce(jnp.maximum, scores), axis=0, keepdims=True)
        terms = [jnp.exp(score - highest) for score in scores]
        total = jnp.sum(sum(terms), axis=0, keepdims=True)
        query_cells = jnp.zeros((1, LANES), jnp.int32)
        for row in range(QUERY_ROWS):
            cell = cells[HALO + upper * QUERY_ROWS + row]
            query_cells = jnp.where(query_lane // tile_cols == row, cell, query_cells)
        live = start + query_lane % tile_cols < query_cells
        inverse = jnp.where(live, 1.0 / total, 0.0)
        probs = [term * inverse for term in terms]
        grad_probs = [nt(v_s[index[j], keys, :], grads) for j in range(window)]
        delta = jnp.sum(sum(p * g for p, g in zip(probs, grad_probs)), axis=0, keepdims=True)
        weights = [p.astype(jnp.bfloat16) for p in probs]
        grad_scores = [(p * (g - delta)).astype(jnp.bfloat16) for p, g in zip(probs, grad_probs)]
        for j in range(window):
            dv_s[index[j], keys, :] += nn(weights[j], grads)
            dk_s[index[j], keys, :] += nn(grad_scores[j], queries)
        values_turned = jnp.concatenate([vt_s[upper, index[j]] for j in range(window)], axis=1)
        keys_turned = jnp.concatenate([kt_s[upper, index[j]] for j in range(window)], axis=1)
        heads_out = gather(nn(values_turned, jnp.concatenate(weights, axis=0)))
        grad_query = gather(nn(keys_turned, jnp.concatenate(grad_scores, axis=0)))
        for row in range(QUERY_ROWS):
            at = row_cols(upper * QUERY_ROWS + row, start, tile_cols)
            outq[at, :feats] = heads_out[row * tile_cols:(row + 1) * tile_cols]
            outq[at, feats:] = grad_query[row * tile_cols:(row + 1) * tile_cols]

    def tile_pair(tile, carry):
        for upper in range(2):
            one_tile(upper, tile)
        return carry

    for move in moves:
        move.wait()
    grad_heads = nt(held[...], weight[...]).astype(jnp.bfloat16)
    for i in range(steps):
        go[pl.ds(pl.multiple_of(order[i], 16), chunk)] = grad_heads[i * chunk:(i + 1) * chunk]
    lax.fori_loop(0, LONGITUDES // tile_cols, tile_pair, 0)
    moves = [
        pltpu.make_async_copy(outq.at[pl.ds(pl.multiple_of(order[i], 16), chunk)], part, sems.at[i])
        for i, part in enumerate(outq_parts)
    ]
    for move in moves:
        move.start()

    def store_pair(p, carry):
        for first, sums in ((0, dk_s), (feats, dv_s)):
            both = jnp.concatenate(
                [sums[2 * p + half].reshape(EXT_ROWS, BLOCK, feats) for half in range(2)], axis=1
            )
            for row in range(HALO):
                dkv_top[row_cols(row, p * 16, 16), first:first + feats] = both[row].astype(jnp.bfloat16)
                dkv_bot[row_cols(row, p * 16, 16), first:first + feats] = (
                    both[HALO + BAND_ROWS + row].astype(jnp.bfloat16)
                )
            for row in range(BAND_ROWS):
                dkv_own[row_cols(row, p * 16, 16), first:first + feats] = both[HALO + row]
        return carry

    lax.fori_loop(0, BLOCKS // 2, store_pair, 0)
    for move in moves:
        move.wait()


VMEM = pl.BlockSpec(memory_space=pltpu.VMEM)
SMEM = pl.BlockSpec(memory_space=pltpu.SMEM)
HBM = pl.BlockSpec(memory_space=pl.ANY)
BF16, F32 = jnp.bfloat16, jnp.float32


def shape(rows, cols, kind=BF16):
    return jax.ShapeDtypeStruct((rows, cols), kind)


def call(kernel, out_shape, in_specs, out_specs, args, flops, scratch=(), transcendentals=0):
    moved = sum(x.size * x.dtype.itemsize for x in (*args, *out_shape)) if flops else 0
    return pl.pallas_call(
        kernel,
        out_shape=tuple(out_shape),
        in_specs=list(in_specs),
        out_specs=tuple(out_specs),
        scratch_shapes=list(scratch),
        compiler_params=pltpu.CompilerParams(vmem_limit_bytes=60 * 2**20),
        cost_estimate=pl.CostEstimate(
            flops=flops, transcendentals=transcendentals, bytes_accessed=moved
        ),
    )(*args)


def attention(cells, order, qkv, kv_top, kv_bot, weight, upstream):
    steps, (feats, width), chunk = len(upstream), weight.shape, upstream[0].shape[0]
    heads = feats // HEAD_WIDTH
    window = LANES // heads // QUERY_ROWS // BLOCK + 2
    band, halo = BAND_ROWS * LONGITUDES, HALO * LONGITUDES
    pairs = band * heads * KEYS * window
    results = call(
        functools.partial(attention_kernel, heads, steps),
        [shape(chunk, 2 * feats)] * steps
        + [shape(band, 2 * feats, F32), shape(halo, 2 * feats), shape(halo, 2 * feats)],
        [SMEM, SMEM, VMEM, VMEM, VMEM, VMEM] + [HBM] * steps,
        [HBM] * steps + [VMEM] * 3,
        (cells, order, qkv, kv_top, kv_bot, weight, *upstream),
        flops=12 * pairs * HEAD_WIDTH * heads + 2 * band * weight.size,
        transcendentals=pairs,
        scratch=[
            pltpu.VMEM((band, width), BF16),
            pltpu.VMEM((band, 2 * feats), BF16),
            pltpu.VMEM((band, feats), BF16),
            pltpu.VMEM((BLOCKS, EXT_ROWS * BLOCK, feats), BF16),
            pltpu.VMEM((BLOCKS, EXT_ROWS * BLOCK, feats), BF16),
            pltpu.VMEM((2, BLOCKS, feats, KEYS), BF16),
            pltpu.VMEM((2, BLOCKS, feats, KEYS), BF16),
            pltpu.VMEM((BLOCKS, EXT_ROWS * BLOCK, feats), F32),
            pltpu.VMEM((BLOCKS, EXT_ROWS * BLOCK, feats), F32),
            pltpu.VMEM((BLOCKS, EXT_ROWS * BLOCK, 128), F32),
            pltpu.VMEM((window, KEYS, LANES), F32),
            pltpu.SemaphoreType.DMA((steps,)),
        ],
    )
    return (results[:steps], *results[steps:])


def norm_kernel(tokens, gain, normed):
    features = tokens[...].astype(F32)
    inverse = lax.rsqrt(jnp.mean(features * features, axis=1, keepdims=True) + 1e-06)
    normed[...] = (features * inverse * gain[...]).astype(BF16)


def norm(tokens, gain):
    return call(
        norm_kernel, [shape(*tokens.shape)], [VMEM] * 2, [VMEM], (tokens, gain[None, :]), flops=4 * tokens.size
    )[0]


def stacked_moves(parts, held, sems, first=0):
    chunk = parts[0].shape[0]
    return [
        pltpu.make_async_copy(part, held.at[pl.ds(i * chunk, chunk)], sems.at[first + i]) for i, part in enumerate(parts)
    ]


def carry_out(moves):
    for move in moves:
        move.start()
    for move in moves:
        move.wait()


def projection_kernel(steps, feats, order, weight, *refs):
    parts, (qkv, kv_up, kv_down, normed_up, normed_down, held, sems) = refs[:steps], refs[steps:]
    chunk = parts[0].shape[0]
    halo, rest = HALO * LONGITUDES, (BAND_ROWS - HALO) * LONGITUDES
    carry_out([
        pltpu.make_async_copy(part, held.at[pl.ds(pl.multiple_of(order[i], 16), chunk)], sems.at[i])
        for i, part in enumerate(parts)
    ])
    moves = [
        pltpu.make_async_copy(held.at[pl.ds(rest, halo)], normed_up, sems.at[0]),
        pltpu.make_async_copy(held.at[pl.ds(0, halo)], normed_down, sems.at[1]),
    ]
    for move in moves:
        move.start()
    for i in range(3):
        product = nn(held[...], weight[:, i * feats:(i + 1) * feats]).astype(BF16)
        qkv[:, i * feats:(i + 1) * feats] = product
        if i:
            kv_up[:, (i - 1) * feats:i * feats] = product[rest:]
            kv_down[:, (i - 1) * feats:i * feats] = product[:halo]
    for move in moves:
        move.wait()


def projections(order, weight, parts):
    steps, feats, width = len(parts), weight.shape[1] // 3, parts[0].shape[1]
    band, halo = BAND_ROWS * LONGITUDES, HALO * LONGITUDES
    return call(
        functools.partial(projection_kernel, steps, feats),
        [shape(band, 3 * feats)] + [shape(halo, 2 * feats)] * 2 + [shape(halo, width)] * 2,
        [SMEM, VMEM] + [HBM] * steps, [VMEM] * 3 + [HBM] * 2, (order, weight, *parts),
        flops=2 * band * weight.size,
        scratch=[pltpu.VMEM((band, width), BF16), pltpu.SemaphoreType.DMA((steps,))],
    )


def join_kernel(steps, order, own, above, below, *refs):
    outq_parts, parts, whole = refs[:steps], refs[steps:2 * steps], refs[-1]
    chunk, feats = outq_parts[0].shape
    low, high = (BAND_ROWS - HALO) * LONGITUDES, HALO * LONGITUDES
    for outq, part in zip(outq_parts, parts):
        part[:, :feats] = outq[...]
    whole[:low] = (own[:low] + below[:low].astype(F32)).astype(BF16)
    whole[low:high] = (own[low:high] + below[low:].astype(F32) + above[:high - low].astype(F32)).astype(BF16)
    whole[high:] = (own[high:] + above[high - low:].astype(F32)).astype(BF16)
    for i, part in enumerate(parts):
        part[:, feats:] = whole[pl.ds(pl.multiple_of(order[i], 16), chunk), :]


def joined(order, own, above, below, outq_parts):
    steps, (chunk, feats) = len(outq_parts), outq_parts[0].shape
    return call(
        functools.partial(join_kernel, steps),
        [shape(chunk, 2 * feats)] * steps,
        [SMEM] + [VMEM] * (3 + steps), [VMEM] * steps, (order, own, above, below, *outq_parts), flops=0,
        scratch=[pltpu.VMEM((steps * chunk, feats), BF16)],
    )


def weight_grad_kernel(steps, order, *refs):
    (outq_parts, upstream, normed), refs = [refs[i * steps:(i + 1) * steps] for i in range(3)], refs[3 * steps:]
    dkv, dkv_top, dkv_bot, normed_top, normed_bot, grad, outq, up, own, sems = refs
    feats, chunk = outq.shape[1] // 2, outq_parts[0].shape[0]
    groups = [
        [
            pltpu.make_async_copy(part, held.at[pl.ds(pl.multiple_of(order[i], 16), chunk)], sems.at[group, i])
            for i, part in enumerate(parts)
        ]
        for group, (parts, held) in enumerate(((outq_parts, outq), (normed, own), (upstream, up)))
    ]
    for moves in groups:
        for move in moves:
            move.start()

    def product(left, right):
        return lax.dot_general(left, right, (((0,), (0,)), ((), ())), preferred_element_type=F32)

    keyval = product(dkv_top[...], normed_top[...]) + product(dkv_bot[...], normed_bot[...])
    for moves in groups[:2]:
        for move in moves:
            move.wait()
    grad[2 * feats:, :] = (keyval + product(dkv[...].astype(BF16), own[...])).astype(BF16)
    grad[feats:2 * feats, :] = product(outq[:, feats:], own[...]).astype(BF16)
    for move in groups[2]:
        move.wait()
    grad[:feats, :] = product(outq[:, :feats], up[...]).astype(BF16)


def weight_grads(order, outq_parts, upstream, normed, dkv, dkv_halos, normed_halos):
    steps, (chunk, rows), width = len(normed), outq_parts[0].shape, normed[0].shape[1]
    band = steps * chunk
    return call(
        functools.partial(weight_grad_kernel, steps),
        [shape(2 * rows, width)], [SMEM] + [HBM] * (3 * steps) + [VMEM] * 5, [VMEM],
        (order, *outq_parts, *upstream, *normed, dkv, *dkv_halos, *normed_halos),
        flops=2 * width * rows * (2 * band + 2 * HALO * LONGITUDES),
        scratch=[
            pltpu.VMEM((band, rows), BF16), pltpu.VMEM((band, width), BF16), pltpu.VMEM((band, width), BF16),
            pltpu.SemaphoreType.DMA((3, steps)),
        ],
    )[0]


def token_kernel(steps, leads, tokens, gain, *refs):
    parts, blocks, (update, grad, left, qkv, out, sems) = refs[:steps], refs[steps:2 * steps], refs[2 * steps:]
    feats = out.shape[0] // steps
    carry_out([
        move for i, block in enumerate(blocks) for move in (
            pltpu.make_async_copy(block.at[pl.ds(0, 3 * feats)], qkv.at[pl.ds(3 * i * feats, 3 * feats)], sems.at[i]),
            pltpu.make_async_copy(block.at[pl.ds(3 * feats, feats)], out.at[pl.ds(i * feats, feats)], sems.at[steps + i]),
        )
    ])
    for i, part in enumerate(parts):
        left[leads[i]] = part[...]
    side_by_side = lambda cut: jnp.concatenate([left[i, :, cut] for i in range(steps)], axis=1)
    update[...] = nn(side_by_side(slice(0, feats)), out[...]).astype(BF16)
    grad_normed = nn(side_by_side(slice(feats, None)), qkv[...])
    features = tokens[...].astype(F32)
    inverse = lax.rsqrt(jnp.mean(features * features, axis=1, keepdims=True) + 1e-06)
    centred = features * inverse
    scaled = gain[...] * grad_normed
    grad[...] = (inverse * (scaled - centred * jnp.mean(scaled * centred, axis=1, keepdims=True))).astype(BF16)


def token_outputs(leads, tokens, gain, parts, blocks):
    steps, (rows, width), chunk = len(blocks), blocks[0].shape, tokens.shape[0]
    feats = rows // 4
    return call(
        functools.partial(token_kernel, steps),
        [shape(chunk, width)] * 2, [SMEM] + [VMEM] * (2 + steps) + [HBM] * steps, [VMEM] * 2,
        (leads, tokens, gain[None, :], *parts, *blocks), flops=2 * steps * chunk * rows * width,
        scratch=[
            pltpu.VMEM((steps, chunk, rows), BF16),
            pltpu.VMEM((3 * steps * feats, width), BF16),
            pltpu.VMEM((steps * feats, width), BF16),
            pltpu.SemaphoreType.DMA((2 * steps,)),
        ],
    )


def finish_kernel(scale, flag, mine, other, grad_qkv, grad_out):
    heads = grad_out.shape[0]
    for h in range(heads):
        for i in range(4):
            at = pl.ds((i * heads + h) * HEAD_WIDTH, HEAD_WIDTH)
            part = jnp.where(flag[0] == 1, mine[at, :], other[at, :]).astype(F32)
            if i == 0:
                grad_out[h] = part * scale
            else:
                factor = scale * HEAD_WIDTH ** -0.5 if i == 1 else scale
                grad_qkv[h, (i - 1) * HEAD_WIDTH:i * HEAD_WIDTH, :] = part * factor


def finished(scale, flag, mine, other):
    heads, width = mine.shape[0] // (4 * HEAD_WIDTH), mine.shape[1]
    return call(
        functools.partial(finish_kernel, scale),
        [jax.ShapeDtypeStruct((heads, 3 * HEAD_WIDTH, width), F32), jax.ShapeDtypeStruct((heads, HEAD_WIDTH, width), F32)],
        [SMEM, VMEM, VMEM], [VMEM] * 2, (flag, mine, other), flops=mine.size,
    )


from jax.sharding import Mesh, PartitionSpec as P

WIDTH = 1024
GROUP = ("y", "m", "c")


def owners(halves):
    if halves == 2:
        return [
            lambda y, m, c: (c, 1 - m if c == y else m, y),
            lambda y, m, c: (c, 1 - m if c == y else m, 1 - y),
            lambda y, m, c: (c, m if c == y else 1 - m, 1 - y),
            lambda y, m, c: (c, m if c == y else 1 - m, y),
        ]
    return [
        lambda y, m, c, dm=dm, dc=dc: (c, (m + dm) % halves, (y + dc) % 2) for dc in range(2) for dm in range(halves)
    ]


def passed_along(x, by):
    length = lax.axis_size("z") * 2
    pairs = [(i, i + by) for i in range(length) if 0 <= i + by < length]
    return lax.ppermute(x, ("z", "c"), pairs)


def after(x, *others):
    return lax.optimization_barrier((x, *others))[0]


def on_device(tokens, gain, qkv_weight, out_weight, row_cells, upstream):
    heads = qkv_weight.shape[0]
    feats = heads * HEAD_WIDTH
    band_tokens = BAND_ROWS * LONGITUDES
    chunk = tokens.shape[0]
    halves, layers = lax.axis_size("m"), lax.axis_size("z")
    z, y, m, c = (lax.axis_index(axis) for axis in ("z",) + GROUP)
    grad_scale = 4.0 / math.sqrt(band_tokens * layers * 2)
    band_start = (z * 2 + c) * BAND_ROWS
    cells = lax.dynamic_slice_in_dim(jnp.pad(row_cells, (HALO, HALO)), band_start, EXT_ROWS)

    at = lambda y, m, c: (y * halves + m) * 2 + c
    spots = [(y, m, c) for y in range(2) for m in range(halves) for c in range(2)]
    slots = [[owner(*spot) for spot in spots] for owner in owners(halves)]
    here = lambda table: jnp.asarray(table, jnp.int32)[at(y, m, c)]
    order = here([[(slot[i][1] * 2 + slot[i][2]) * chunk for slot in slots] for i in range(len(spots))])

    def lead(slot, spot):
        far = spots[slot.index(spot)]
        return (far[0] - spot[2]) % 2 * halves + (far[1] - spot[1]) % halves

    leads = here([[lead(slot, spot) for slot in slots] for spot in spots])

    def permuted(x, pairs):
        return lax.ppermute(x, GROUP, [(at(*a), at(*b)) for a, b in pairs])

    def send_back(parts):
        return [permuted(x, list(zip(spots, slot))) for x, slot in zip(parts, slots)]

    def gathered(x, *others):
        sent = lambda slot: permuted(x, list(zip(slot, spots)))
        if halves != 2:
            parts = [sent(slot) for slot in slots]
            return parts, parts
        first, second = lax.optimization_barrier((sent(slots[0]), sent(slots[1])))
        hop = first, second
        first = after(first, *others)
        third = permuted(
            jnp.where(c == y, first, x),
            [(spot, (1 - spot[0], spot[1], spot[0]) if spot[2] == spot[0] else (spot[0], spot[1], spot[0])) for spot in spots],
        )
        fourth = permuted(
            first, [(spot, (spot[0], 1 - spot[1], spot[2])) for spot in spots if spot[2] != spot[0]]
        )
        third, fourth = lax.optimization_barrier((third, fourth))
        return [first, second, third, jnp.where(c == y, x, fourth)], hop

    def from_ahead(x, dm):
        return lax.ppermute(x, "m", [((i + dm) % halves, i) for i in range(halves)])

    def from_sibling(x):
        return lax.ppermute(x, "c", [(0, 1), (1, 0)])

    def split(qkv, out):
        eighth = jnp.asarray([HEAD_WIDTH ** -0.5, 1.0, 1.0], BF16)[None, :, None, None]
        qkv = (qkv.reshape(heads, 3, HEAD_WIDTH, WIDTH) * eighth).transpose(1, 0, 2, 3)
        return jnp.concatenate([qkv.reshape(3 * feats, WIDTH), out.reshape(feats, WIDTH)], axis=0)

    blocks = [split(qkv_weight, out_weight)]
    sibling = from_sibling(blocks[0])
    group = jnp.where(c == y, blocks[0], sibling)
    group_qkv, group_out = group[:3 * feats].T, group[3 * feats:]

    normed_parts, hop = gathered(norm(tokens, gain))
    *normed_parts, group_qkv, group_out = lax.optimization_barrier((*normed_parts, group_qkv, group_out))
    qkv, kv_up, kv_down, normed_up, normed_down = projections(order, group_qkv, normed_parts)
    kv_top, kv_bot = passed_along(kv_up, 1), passed_along(kv_down, -1)
    upstream_parts, _ = gathered(after(upstream, *hop), qkv)

    kv_top, kv_bot, normed_up, normed_down, *upstream_parts = lax.optimization_barrier(
        (kv_top, kv_bot, normed_up, normed_down, *upstream_parts)
    )
    normed_halos = passed_along(normed_up, 1), passed_along(normed_down, -1)
    ahead = [from_ahead(after(blocks[0], *upstream_parts), dm) for dm in range(1, halves)]
    outq_parts, dkv, dkv_top, dkv_bot = attention(cells, order, qkv, kv_top, kv_bot, group_out, upstream_parts)

    from_above, from_below = passed_along(dkv_top, -1), passed_along(dkv_bot, 1)
    grads = weight_grads(
        order, outq_parts, upstream_parts, normed_parts, dkv, (dkv_top, dkv_bot), normed_halos
    )
    grads_sum = lax.psum(grads, ("z", "c"))
    parts = joined(after(order, grads), dkv, from_above, from_below, outq_parts)
    parts, ahead = lax.optimization_barrier((parts, ahead))
    parts_own = send_back(parts)
    blocks += ahead + [sibling] + [from_sibling(block) for block in ahead]
    update, grad_input = token_outputs(leads, tokens, gain, parts_own, blocks)
    grads = after(grads_sum, *parts_own)
    pairs = [((1 - y, m, 1 - y), (y, m, 1 - y)) for y in range(2) for m in range(halves)]
    flag = after(jnp.reshape(c == y, (1,)).astype(jnp.int32), grad_input, update)
    grad_qkv, grad_out = finished(grad_scale, flag, grads, permuted(grads, pairs))
    return update, grad_input, grad_qkv, grad_out


def solution(mesh):
    devices = mesh.devices.reshape(mesh.shape["lat"] // 2, 2, mesh.shape["mp"] // 2, 2)
    tokens, weights = P(("z", "y", "m", "c"), None), P(("m", "c"), None, None)
    return jax.shard_map(
        on_device,
        mesh=Mesh(devices, ("z", "y", "m", "c")),
        in_specs=(tokens, P(), weights, weights, P(), tokens),
        out_specs=(tokens, tokens, weights, weights),
        check_vma=False,
    )
```

```python
import functools
import math
import jax
import jax.numpy as jnp
from jax import lax
from jax.experimental import pallas as pl
from jax.experimental.pallas import tpu as pltpu

HEAD_WIDTH = 64
LONGITUDES = 256
BAND_ROWS = 8
HALO = 6
EXT_ROWS = BAND_ROWS + 2 * HALO
LANES = 256
QUERY_ROWS = 4
KEY_ROWS = QUERY_ROWS + 2 * HALO
BLOCK = 8
BLOCKS = LONGITUDES // BLOCK
KEYS = KEY_ROWS * BLOCK
MASKED = -1e30


def nn(a, b):
    return lax.dot_general(a, b, (((1,), (0,)), ((), ())), preferred_element_type=jnp.float32)


def nt(a, b):
    return lax.dot_general(a, b, (((1,), (1,)), ((), ())), preferred_element_type=jnp.float32)


def row_cols(row, start, size):
    return pl.ds(pl.multiple_of(row * LONGITUDES + start, 16), size)


def attention_kernel(
    heads, steps,
    cells, order, qkv, kv_top, kv_bot, weight, *refs,
):
    upstream, refs = refs[:steps], refs[steps:]
    outq_parts, refs = refs[:steps], refs[steps:]
    dkv_own, dkv_top, dkv_bot, held, outq, go, k_s, v_s, kt_s, vt_s, dk_s, dv_s, live_s, near_s, sems = refs
    feats = heads * HEAD_WIDTH
    chunk = BAND_ROWS * LONGITUDES // steps
    moves = [
        pltpu.make_async_copy(part, held.at[pl.ds(i * chunk, chunk)], sems.at[i]) for i, part in enumerate(upstream)
    ]
    for move in moves:
        move.start()
    tile_cols = LANES // heads // QUERY_ROWS
    tile_queries = QUERY_ROWS * tile_cols
    window = tile_cols // BLOCK + 2

    def load_pair(p, carry):
        for first, rows_s, turned_s in ((0, k_s, kt_s), (feats, v_s, vt_s)):
            both = jnp.stack(
                [kv_top[row_cols(row, p * 16, 16), first:first + feats] for row in range(HALO)]
                + [qkv[row_cols(row, p * 16, 16), feats + first:2 * feats + first] for row in range(BAND_ROWS)]
                + [kv_bot[row_cols(row, p * 16, 16), first:first + feats] for row in range(HALO)]
            ).astype(jnp.float32)
            for half in range(2):
                block = both[:, 8 * half:8 * half + 8, :].reshape(EXT_ROWS * BLOCK, feats)
                rows_s[2 * p + half] = block.astype(jnp.bfloat16)
                for upper in range(2):
                    low = upper * QUERY_ROWS * BLOCK
                    turned_s[upper, 2 * p + half] = block[low:low + KEYS].T.astype(jnp.bfloat16)
        for half in range(2):
            col = (2 * p + half) * BLOCK + lax.broadcasted_iota(jnp.int32, (BLOCK, 128), 0)
            for row in range(EXT_ROWS):
                live_s[2 * p + half, row * BLOCK:(row + 1) * BLOCK, :] = jnp.where(col < cells[row], 0.0, MASKED)
        return carry

    lax.fori_loop(0, BLOCKS // 2, load_pair, 0)
    dk_s[...] = jnp.zeros_like(dk_s)
    dv_s[...] = jnp.zeros_like(dv_s)

    lane = lax.broadcasted_iota(jnp.int32, (KEYS, LANES), 1) % tile_queries
    query_row = lane // tile_cols
    query_col = lane % tile_cols
    key = lax.broadcasted_iota(jnp.int32, (KEYS, LANES), 0)
    row_gap = key // BLOCK - query_row
    for j in range(window):
        col_gap = (j - 1) * BLOCK + key % BLOCK - query_col
        near = (row_gap >= 0) & (row_gap <= 2 * HALO) & (col_gap >= -HALO) & (col_gap <= HALO)
        near_s[j] = jnp.where(near, 0.0, MASKED)

    own_head = (
        lax.broadcasted_iota(jnp.int32, (LANES, feats), 0) // tile_queries
        == lax.broadcasted_iota(jnp.int32, (LANES, feats), 1) // HEAD_WIDTH
    )
    own_head_turned = (
        lax.broadcasted_iota(jnp.int32, (feats, LANES), 1) // tile_queries
        == lax.broadcasted_iota(jnp.int32, (feats, LANES), 0) // HEAD_WIDTH
    )
    query_lane = lax.broadcasted_iota(jnp.int32, (1, LANES), 1) % tile_queries

    def spread(ref, upper, start):
        tile = jnp.concatenate([
            ref[row_cols(upper * QUERY_ROWS + row, start, tile_cols), :feats] for row in range(QUERY_ROWS)
        ], axis=0)
        if heads == 1:
            return tile
        stacked = jnp.concatenate([tile] * heads, axis=0)
        return jnp.where(own_head, stacked, jnp.zeros_like(stacked))

    def gather(turned):
        if heads == 1:
            tile = turned.T
        else:
            tall = jnp.where(own_head_turned, turned, 0.0).T
            tile = sum(tall[h * tile_queries:(h + 1) * tile_queries] for h in range(heads))
        return tile.astype(jnp.bfloat16)

    def one_tile(upper, tile):
        start = pl.multiple_of(tile * tile_cols, 16)
        keys = pl.ds(upper * QUERY_ROWS * BLOCK, KEYS)
        index = [(tile * (tile_cols // BLOCK) + j + BLOCKS - 1) % BLOCKS for j in range(window)]
        queries = spread(qkv, upper, start)
        grads = spread(go, upper, start)
        scores = [
            nt(k_s[index[j], keys, :], queries)
            + near_s[j]
            + jnp.concatenate([live_s[index[j], keys, :]] * (LANES // 128), axis=1)
            for j in range(window)
        ]
        highest = jnp.max(functools.reduce(jnp.maximum, scores), axis=0, keepdims=True)
        terms = [jnp.exp(score - highest) for score in scores]
        total = jnp.sum(sum(terms), axis=0, keepdims=True)
        query_cells = jnp.zeros((1, LANES), jnp.int32)
        for row in range(QUERY_ROWS):
            cell = cells[HALO + upper * QUERY_ROWS + row]
            query_cells = jnp.where(query_lane // tile_cols == row, cell, query_cells)
        live = start + query_lane % tile_cols < query_cells
        inverse = jnp.where(live, 1.0 / total, 0.0)
        probs = [term * inverse for term in terms]
        grad_probs = [nt(v_s[index[j], keys, :], grads) for j in range(window)]
        delta = jnp.sum(sum(p * g for p, g in zip(probs, grad_probs)), axis=0, keepdims=True)
        weights = [p.astype(jnp.bfloat16) for p in probs]
        grad_scores = [(p * (g - delta)).astype(jnp.bfloat16) for p, g in zip(probs, grad_probs)]
        for j in range(window):
            dv_s[index[j], keys, :] += nn(weights[j], grads)
            dk_s[index[j], keys, :] += nn(grad_scores[j], queries)
        values_turned = jnp.concatenate([vt_s[upper, index[j]] for j in range(window)], axis=1)
        keys_turned = jnp.concatenate([kt_s[upper, index[j]] for j in range(window)], axis=1)
        heads_out = gather(nn(values_turned, jnp.concatenate(weights, axis=0)))
        grad_query = gather(nn(keys_turned, jnp.concatenate(grad_scores, axis=0)))
        for row in range(QUERY_ROWS):
            at = row_cols(upper * QUERY_ROWS + row, start, tile_cols)
            outq[at, :feats] = heads_out[row * tile_cols:(row + 1) * tile_cols]
            outq[at, feats:] = grad_query[row * tile_cols:(row + 1) * tile_cols]

    def tile_pair(tile, carry):
        for upper in range(2):
            one_tile(upper, tile)
        return carry

    for move in moves:
        move.wait()
    grad_heads = nt(held[...], weight[...]).astype(jnp.bfloat16)
    for i in range(steps):
        go[pl.ds(pl.multiple_of(order[i], 16), chunk)] = grad_heads[i * chunk:(i + 1) * chunk]
    lax.fori_loop(0, LONGITUDES // tile_cols, tile_pair, 0)
    moves = [
        pltpu.make_async_copy(outq.at[pl.ds(pl.multiple_of(order[i], 16), chunk)], part, sems.at[i])
        for i, part in enumerate(outq_parts)
    ]
    for move in moves:
        move.start()

    def store_pair(p, carry):
        for first, sums in ((0, dk_s), (feats, dv_s)):
            both = jnp.concatenate(
                [sums[2 * p + half].reshape(EXT_ROWS, BLOCK, feats) for half in range(2)], axis=1
            )
            for row in range(HALO):
                dkv_top[row_cols(row, p * 16, 16), first:first + feats] = both[row].astype(jnp.bfloat16)
                dkv_bot[row_cols(row, p * 16, 16), first:first + feats] = (
                    both[HALO + BAND_ROWS + row].astype(jnp.bfloat16)
                )
            for row in range(BAND_ROWS):
                dkv_own[row_cols(row, p * 16, 16), first:first + feats] = both[HALO + row]
        return carry

    lax.fori_loop(0, BLOCKS // 2, store_pair, 0)
    for move in moves:
        move.wait()


VMEM = pl.BlockSpec(memory_space=pltpu.VMEM)
SMEM = pl.BlockSpec(memory_space=pltpu.SMEM)
HBM = pl.BlockSpec(memory_space=pl.ANY)
BF16, F32 = jnp.bfloat16, jnp.float32


def shape(rows, cols, kind=BF16):
    return jax.ShapeDtypeStruct((rows, cols), kind)


def call(kernel, out_shape, in_specs, out_specs, args, flops, scratch=(), transcendentals=0):
    moved = sum(x.size * x.dtype.itemsize for x in (*args, *out_shape)) if flops else 0
    return pl.pallas_call(
        kernel,
        out_shape=tuple(out_shape),
        in_specs=list(in_specs),
        out_specs=tuple(out_specs),
        scratch_shapes=list(scratch),
        compiler_params=pltpu.CompilerParams(vmem_limit_bytes=60 * 2**20),
        cost_estimate=pl.CostEstimate(
            flops=flops, transcendentals=transcendentals, bytes_accessed=moved
        ),
    )(*args)


def attention(cells, order, qkv, kv_top, kv_bot, weight, upstream):
    steps, (feats, width), chunk = len(upstream), weight.shape, upstream[0].shape[0]
    heads = feats // HEAD_WIDTH
    window = LANES // heads // QUERY_ROWS // BLOCK + 2
    band, halo = BAND_ROWS * LONGITUDES, HALO * LONGITUDES
    pairs = band * heads * KEYS * window
    results = call(
        functools.partial(attention_kernel, heads, steps),
        [shape(chunk, 2 * feats)] * steps
        + [shape(band, 2 * feats, F32), shape(halo, 2 * feats), shape(halo, 2 * feats)],
        [SMEM, SMEM, VMEM, VMEM, VMEM, VMEM] + [HBM] * steps,
        [HBM] * steps + [VMEM] * 3,
        (cells, order, qkv, kv_top, kv_bot, weight, *upstream),
        flops=12 * pairs * HEAD_WIDTH * heads + 2 * band * weight.size,
        transcendentals=pairs,
        scratch=[
            pltpu.VMEM((band, width), BF16),
            pltpu.VMEM((band, 2 * feats), BF16),
            pltpu.VMEM((band, feats), BF16),
            pltpu.VMEM((BLOCKS, EXT_ROWS * BLOCK, feats), BF16),
            pltpu.VMEM((BLOCKS, EXT_ROWS * BLOCK, feats), BF16),
            pltpu.VMEM((2, BLOCKS, feats, KEYS), BF16),
            pltpu.VMEM((2, BLOCKS, feats, KEYS), BF16),
            pltpu.VMEM((BLOCKS, EXT_ROWS * BLOCK, feats), F32),
            pltpu.VMEM((BLOCKS, EXT_ROWS * BLOCK, feats), F32),
            pltpu.VMEM((BLOCKS, EXT_ROWS * BLOCK, 128), F32),
            pltpu.VMEM((window, KEYS, LANES), F32),
            pltpu.SemaphoreType.DMA((steps,)),
        ],
    )
    return (results[:steps], *results[steps:])


def norm_kernel(tokens, gain, normed):
    features = tokens[...].astype(F32)
    inverse = lax.rsqrt(jnp.mean(features * features, axis=1, keepdims=True) + 1e-06)
    normed[...] = (features * inverse * gain[...]).astype(BF16)


def norm(tokens, gain):
    return call(
        norm_kernel, [shape(*tokens.shape)], [VMEM] * 2, [VMEM], (tokens, gain[None, :]), flops=4 * tokens.size
    )[0]


def stacked_moves(parts, held, sems, first=0):
    chunk = parts[0].shape[0]
    return [
        pltpu.make_async_copy(part, held.at[pl.ds(i * chunk, chunk)], sems.at[first + i]) for i, part in enumerate(parts)
    ]


def carry_out(moves):
    for move in moves:
        move.start()
    for move in moves:
        move.wait()


def projection_kernel(steps, feats, order, weight, *refs):
    parts, (qkv, kv_up, kv_down, normed_up, normed_down, held, sems) = refs[:steps], refs[steps:]
    chunk = parts[0].shape[0]
    halo, rest = HALO * LONGITUDES, (BAND_ROWS - HALO) * LONGITUDES
    carry_out([
        pltpu.make_async_copy(part, held.at[pl.ds(pl.multiple_of(order[i], 16), chunk)], sems.at[i])
        for i, part in enumerate(parts)
    ])
    moves = [
        pltpu.make_async_copy(held.at[pl.ds(rest, halo)], normed_up, sems.at[0]),
        pltpu.make_async_copy(held.at[pl.ds(0, halo)], normed_down, sems.at[1]),
    ]
    for move in moves:
        move.start()
    for i in range(3):
        product = nn(held[...], weight[:, i * feats:(i + 1) * feats]).astype(BF16)
        qkv[:, i * feats:(i + 1) * feats] = product
        if i:
            kv_up[:, (i - 1) * feats:i * feats] = product[rest:]
            kv_down[:, (i - 1) * feats:i * feats] = product[:halo]
    for move in moves:
        move.wait()


def projections(order, weight, parts):
    steps, feats, width = len(parts), weight.shape[1] // 3, parts[0].shape[1]
    band, halo = BAND_ROWS * LONGITUDES, HALO * LONGITUDES
    return call(
        functools.partial(projection_kernel, steps, feats),
        [shape(band, 3 * feats)] + [shape(halo, 2 * feats)] * 2 + [shape(halo, width)] * 2,
        [SMEM, VMEM] + [HBM] * steps, [VMEM] * 3 + [HBM] * 2, (order, weight, *parts),
        flops=2 * band * weight.size,
        scratch=[pltpu.VMEM((band, width), BF16), pltpu.SemaphoreType.DMA((steps,))],
    )


def join_kernel(steps, order, own, above, below, *refs):
    outq_parts, parts, whole = refs[:steps], refs[steps:2 * steps], refs[-1]
    chunk, feats = outq_parts[0].shape
    low, high = (BAND_ROWS - HALO) * LONGITUDES, HALO * LONGITUDES
    for outq, part in zip(outq_parts, parts):
        part[:, :feats] = outq[...]
    whole[:low] = (own[:low] + below[:low].astype(F32)).astype(BF16)
    whole[low:high] = (own[low:high] + below[low:].astype(F32) + above[:high - low].astype(F32)).astype(BF16)
    whole[high:] = (own[high:] + above[high - low:].astype(F32)).astype(BF16)
    for i, part in enumerate(parts):
        part[:, feats:] = whole[pl.ds(pl.multiple_of(order[i], 16), chunk), :]


def joined(order, own, above, below, outq_parts):
    steps, (chunk, feats) = len(outq_parts), outq_parts[0].shape
    return call(
        functools.partial(join_kernel, steps),
        [shape(chunk, 2 * feats)] * steps,
        [SMEM] + [VMEM] * (3 + steps), [VMEM] * steps, (order, own, above, below, *outq_parts), flops=0,
        scratch=[pltpu.VMEM((steps * chunk, feats), BF16)],
    )


def weight_grad_kernel(steps, order, *refs):
    (outq_parts, upstream, normed), refs = [refs[i * steps:(i + 1) * steps] for i in range(3)], refs[3 * steps:]
    dkv, dkv_top, dkv_bot, normed_top, normed_bot, grad, outq, up, own, sems = refs
    feats, chunk = outq.shape[1] // 2, outq_parts[0].shape[0]
    groups = [
        [
            pltpu.make_async_copy(part, held.at[pl.ds(pl.multiple_of(order[i], 16), chunk)], sems.at[group, i])
            for i, part in enumerate(parts)
        ]
        for group, (parts, held) in enumerate(((outq_parts, outq), (normed, own), (upstream, up)))
    ]
    for moves in groups:
        for move in moves:
            move.start()

    def product(left, right):
        return lax.dot_general(left, right, (((0,), (0,)), ((), ())), preferred_element_type=F32)

    keyval = product(dkv_top[...], normed_top[...]) + product(dkv_bot[...], normed_bot[...])
    for moves in groups[:2]:
        for move in moves:
            move.wait()
    grad[2 * feats:, :] = (keyval + product(dkv[...].astype(BF16), own[...])).astype(BF16)
    grad[feats:2 * feats, :] = product(outq[:, feats:], own[...]).astype(BF16)
    for move in groups[2]:
        move.wait()
    grad[:feats, :] = product(outq[:, :feats], up[...]).astype(BF16)


def weight_grads(order, outq_parts, upstream, normed, dkv, dkv_halos, normed_halos):
    steps, (chunk, rows), width = len(normed), outq_parts[0].shape, normed[0].shape[1]
    band = steps * chunk
    return call(
        functools.partial(weight_grad_kernel, steps),
        [shape(2 * rows, width)], [SMEM] + [HBM] * (3 * steps) + [VMEM] * 5, [VMEM],
        (order, *outq_parts, *upstream, *normed, dkv, *dkv_halos, *normed_halos),
        flops=2 * width * rows * (2 * band + 2 * HALO * LONGITUDES),
        scratch=[
            pltpu.VMEM((band, rows), BF16), pltpu.VMEM((band, width), BF16), pltpu.VMEM((band, width), BF16),
            pltpu.SemaphoreType.DMA((3, steps)),
        ],
    )[0]


def token_kernel(steps, leads, tokens, gain, *refs):
    parts, blocks, (update, grad, left, qkv, out, sems) = refs[:steps], refs[steps:2 * steps], refs[2 * steps:]
    feats = out.shape[0] // steps
    carry_out([
        move for i, block in enumerate(blocks) for move in (
            pltpu.make_async_copy(block.at[pl.ds(0, 3 * feats)], qkv.at[pl.ds(3 * i * feats, 3 * feats)], sems.at[i]),
            pltpu.make_async_copy(block.at[pl.ds(3 * feats, feats)], out.at[pl.ds(i * feats, feats)], sems.at[steps + i]),
        )
    ])
    for i, part in enumerate(parts):
        left[leads[i]] = part[...]
    side_by_side = lambda cut: jnp.concatenate([left[i, :, cut] for i in range(steps)], axis=1)
    update[...] = nn(side_by_side(slice(0, feats)), out[...]).astype(BF16)
    grad_normed = nn(side_by_side(slice(feats, None)), qkv[...])
    features = tokens[...].astype(F32)
    inverse = lax.rsqrt(jnp.mean(features * features, axis=1, keepdims=True) + 1e-06)
    centred = features * inverse
    scaled = gain[...] * grad_normed
    grad[...] = (inverse * (scaled - centred * jnp.mean(scaled * centred, axis=1, keepdims=True))).astype(BF16)


def token_outputs(leads, tokens, gain, parts, blocks):
    steps, (rows, width), chunk = len(blocks), blocks[0].shape, tokens.shape[0]
    feats = rows // 4
    return call(
        functools.partial(token_kernel, steps),
        [shape(chunk, width)] * 2, [SMEM] + [VMEM] * (2 + steps) + [HBM] * steps, [VMEM] * 2,
        (leads, tokens, gain[None, :], *parts, *blocks), flops=2 * steps * chunk * rows * width,
        scratch=[
            pltpu.VMEM((steps, chunk, rows), BF16),
            pltpu.VMEM((3 * steps * feats, width), BF16),
            pltpu.VMEM((steps * feats, width), BF16),
            pltpu.SemaphoreType.DMA((2 * steps,)),
        ],
    )


def finish_kernel(scale, flag, mine, other, grad_qkv, grad_out):
    heads = grad_out.shape[0]
    for h in range(heads):
        for i in range(4):
            at = pl.ds((i * heads + h) * HEAD_WIDTH, HEAD_WIDTH)
            part = jnp.where(flag[0] == 1, mine[at, :], other[at, :]).astype(F32)
            if i == 0:
                grad_out[h] = part * scale
            else:
                factor = scale * HEAD_WIDTH ** -0.5 if i == 1 else scale
                grad_qkv[h, (i - 1) * HEAD_WIDTH:i * HEAD_WIDTH, :] = part * factor


def finished(scale, flag, mine, other):
    heads, width = mine.shape[0] // (4 * HEAD_WIDTH), mine.shape[1]
    return call(
        functools.partial(finish_kernel, scale),
        [jax.ShapeDtypeStruct((heads, 3 * HEAD_WIDTH, width), F32), jax.ShapeDtypeStruct((heads, HEAD_WIDTH, width), F32)],
        [SMEM, VMEM, VMEM], [VMEM] * 2, (flag, mine, other), flops=mine.size,
    )


from jax.sharding import Mesh, PartitionSpec as P

WIDTH = 1024
GROUP = ("y", "m", "c")


def owners(halves):
    if halves == 2:
        return [
            lambda y, m, c: (c, 1 - m if c == y else m, y),
            lambda y, m, c: (c, 1 - m if c == y else m, 1 - y),
            lambda y, m, c: (c, m if c == y else 1 - m, 1 - y),
            lambda y, m, c: (c, m if c == y else 1 - m, y),
        ]
    return [
        lambda y, m, c, dm=dm, dc=dc: (c, (m + dm) % halves, (y + dc) % 2) for dc in range(2) for dm in range(halves)
    ]


def passed_along(x, by):
    length = lax.axis_size("z") * 2
    pairs = [(i, i + by) for i in range(length) if 0 <= i + by < length]
    return lax.ppermute(x, ("z", "c"), pairs)


def after(x, *others):
    return lax.optimization_barrier((x, *others))[0]


def on_device(tokens, gain, qkv_weight, out_weight, row_cells, upstream):
    heads = qkv_weight.shape[0]
    feats = heads * HEAD_WIDTH
    band_tokens = BAND_ROWS * LONGITUDES
    chunk = tokens.shape[0]
    halves, layers = lax.axis_size("m"), lax.axis_size("z")
    z, y, m, c = (lax.axis_index(axis) for axis in ("z",) + GROUP)
    grad_scale = 4.0 / math.sqrt(band_tokens * layers * 2)
    band_start = (z * 2 + c) * BAND_ROWS
    cells = lax.dynamic_slice_in_dim(jnp.pad(row_cells, (HALO, HALO)), band_start, EXT_ROWS)

    at = lambda y, m, c: (y * halves + m) * 2 + c
    spots = [(y, m, c) for y in range(2) for m in range(halves) for c in range(2)]
    slots = [[owner(*spot) for spot in spots] for owner in owners(halves)]
    here = lambda table: jnp.asarray(table, jnp.int32)[at(y, m, c)]
    order = here([[(slot[i][1] * 2 + slot[i][2]) * chunk for slot in slots] for i in range(len(spots))])

    def lead(slot, spot):
        far = spots[slot.index(spot)]
        return (far[0] - spot[2]) % 2 * halves + (far[1] - spot[1]) % halves

    leads = here([[lead(slot, spot) for slot in slots] for spot in spots])

    def permuted(x, pairs):
        return lax.ppermute(x, GROUP, [(at(*a), at(*b)) for a, b in pairs])

    def send_back(parts):
        return [permuted(x, list(zip(spots, slot))) for x, slot in zip(parts, slots)]

    def gathered(x, *others):
        sent = lambda slot: permuted(x, list(zip(slot, spots)))
        if halves != 2:
            parts = [sent(slot) for slot in slots]
            return parts, parts
        first, second = lax.optimization_barrier((sent(slots[0]), sent(slots[1])))
        hop = first, second
        first = after(first, *others)
        third = permuted(
            jnp.where(c == y, first, x),
            [(spot, (1 - spot[0], spot[1], spot[0]) if spot[2] == spot[0] else (spot[0], spot[1], spot[0])) for spot in spots],
        )
        fourth = permuted(
            first, [(spot, (spot[0], 1 - spot[1], spot[2])) for spot in spots if spot[2] != spot[0]]
        )
        third, fourth = lax.optimization_barrier((third, fourth))
        return [first, second, third, jnp.where(c == y, x, fourth)], hop

    def from_ahead(x, dm):
        return lax.ppermute(x, "m", [((i + dm) % halves, i) for i in range(halves)])

    def from_sibling(x):
        return lax.ppermute(x, "c", [(0, 1), (1, 0)])

    def split(qkv, out):
        eighth = jnp.asarray([HEAD_WIDTH ** -0.5, 1.0, 1.0], BF16)[None, :, None, None]
        qkv = (qkv.reshape(heads, 3, HEAD_WIDTH, WIDTH) * eighth).transpose(1, 0, 2, 3)
        return jnp.concatenate([qkv.reshape(3 * feats, WIDTH), out.reshape(feats, WIDTH)], axis=0)

    blocks = [split(qkv_weight, out_weight)]
    sibling = from_sibling(blocks[0])
    group = jnp.where(c == y, blocks[0], sibling)
    group_qkv, group_out = group[:3 * feats].T, group[3 * feats:]

    normed_parts, hop = gathered(norm(tokens, gain))
    *normed_parts, group_qkv, group_out = lax.optimization_barrier((*normed_parts, group_qkv, group_out))
    qkv, kv_up, kv_down, normed_up, normed_down = projections(order, group_qkv, normed_parts)
    kv_top, kv_bot = passed_along(kv_up, 1), passed_along(kv_down, -1)
    upstream_parts, _ = gathered(after(upstream, *normed_parts), qkv)

    kv_top, kv_bot, normed_up, normed_down, *upstream_parts = lax.optimization_barrier(
        (kv_top, kv_bot, normed_up, normed_down, *upstream_parts)
    )
    normed_halos = passed_along(normed_up, 1), passed_along(normed_down, -1)
    ahead = [from_ahead(after(blocks[0], *upstream_parts), dm) for dm in range(1, halves)]
    outq_parts, dkv, dkv_top, dkv_bot = attention(cells, order, qkv, kv_top, kv_bot, group_out, upstream_parts)

    from_above, from_below = passed_along(dkv_top, -1), passed_along(dkv_bot, 1)
    grads = weight_grads(
        order, outq_parts, upstream_parts, normed_parts, dkv, (dkv_top, dkv_bot), normed_halos
    )
    grads_sum = lax.psum(grads, ("z", "c"))
    parts = joined(after(order, grads), dkv, from_above, from_below, outq_parts)
    parts, ahead = lax.optimization_barrier((parts, ahead))
    parts_own = send_back(parts)
    ahead = [after(block, grads_sum) for block in ahead]
    blocks += ahead + [sibling] + [from_sibling(block) for block in ahead]
    update, grad_input = token_outputs(leads, tokens, gain, parts_own, blocks)
    grads = after(grads_sum, *parts_own)
    pairs = [((1 - y, m, 1 - y), (y, m, 1 - y)) for y in range(2) for m in range(halves)]
    flag = after(jnp.reshape(c == y, (1,)).astype(jnp.int32), grad_input, update)
    grad_qkv, grad_out = finished(grad_scale, flag, grads, permuted(grads, pairs))
    return update, grad_input, grad_qkv, grad_out


def solution(mesh):
    devices = mesh.devices.reshape(mesh.shape["lat"] // 2, 2, mesh.shape["mp"] // 2, 2)
    tokens, weights = P(("z", "y", "m", "c"), None), P(("m", "c"), None, None)
    return jax.shard_map(
        on_device,
        mesh=Mesh(devices, ("z", "y", "m", "c")),
        in_specs=(tokens, P(), weights, weights, P(), tokens),
        out_specs=(tokens, tokens, weights, weights),
        check_vma=False,
    )
```

```python
import functools
import math
import jax
import jax.numpy as jnp
from jax import lax
from jax.experimental import pallas as pl
from jax.experimental.pallas import tpu as pltpu

HEAD_WIDTH = 64
LONGITUDES = 256
BAND_ROWS = 8
HALO = 6
EXT_ROWS = BAND_ROWS + 2 * HALO
LANES = 256
QUERY_ROWS = 4
KEY_ROWS = QUERY_ROWS + 2 * HALO
BLOCK = 8
BLOCKS = LONGITUDES // BLOCK
KEYS = KEY_ROWS * BLOCK
MASKED = -1e30


def nn(a, b):
    return lax.dot_general(a, b, (((1,), (0,)), ((), ())), preferred_element_type=jnp.float32)


def nt(a, b):
    return lax.dot_general(a, b, (((1,), (1,)), ((), ())), preferred_element_type=jnp.float32)


def row_cols(row, start, size):
    return pl.ds(pl.multiple_of(row * LONGITUDES + start, 16), size)


def attention_kernel(
    heads, steps,
    cells, order, qkv, kv_top, kv_bot, weight, *refs,
):
    upstream, refs = refs[:steps], refs[steps:]
    outq_parts, refs = refs[:steps], refs[steps:]
    dkv_own, dkv_top, dkv_bot, held, outq, go, k_s, v_s, kt_s, vt_s, dk_s, dv_s, live_s, near_s, sems = refs
    feats = heads * HEAD_WIDTH
    chunk = BAND_ROWS * LONGITUDES // steps
    moves = [
        pltpu.make_async_copy(part, held.at[pl.ds(i * chunk, chunk)], sems.at[i]) for i, part in enumerate(upstream)
    ]
    for move in moves:
        move.start()
    tile_cols = LANES // heads // QUERY_ROWS
    tile_queries = QUERY_ROWS * tile_cols
    window = tile_cols // BLOCK + 2

    def load_pair(p, carry):
        for first, rows_s, turned_s in ((0, k_s, kt_s), (feats, v_s, vt_s)):
            both = jnp.stack(
                [kv_top[row_cols(row, p * 16, 16), first:first + feats] for row in range(HALO)]
                + [qkv[row_cols(row, p * 16, 16), feats + first:2 * feats + first] for row in range(BAND_ROWS)]
                + [kv_bot[row_cols(row, p * 16, 16), first:first + feats] for row in range(HALO)]
            ).astype(jnp.float32)
            for half in range(2):
                block = both[:, 8 * half:8 * half + 8, :].reshape(EXT_ROWS * BLOCK, feats)
                rows_s[2 * p + half] = block.astype(jnp.bfloat16)
                for upper in range(2):
                    low = upper * QUERY_ROWS * BLOCK
                    turned_s[upper, 2 * p + half] = block[low:low + KEYS].T.astype(jnp.bfloat16)
        for half in range(2):
            col = (2 * p + half) * BLOCK + lax.broadcasted_iota(jnp.int32, (BLOCK, 128), 0)
            for row in range(EXT_ROWS):
                live_s[2 * p + half, row * BLOCK:(row + 1) * BLOCK, :] = jnp.where(col < cells[row], 0.0, MASKED)
        return carry

    lax.fori_loop(0, BLOCKS // 2, load_pair, 0)
    dk_s[...] = jnp.zeros_like(dk_s)
    dv_s[...] = jnp.zeros_like(dv_s)

    lane = lax.broadcasted_iota(jnp.int32, (KEYS, LANES), 1) % tile_queries
    query_row = lane // tile_cols
    query_col = lane % tile_cols
    key = lax.broadcasted_iota(jnp.int32, (KEYS, LANES), 0)
    row_gap = key // BLOCK - query_row
    for j in range(window):
        col_gap = (j - 1) * BLOCK + key % BLOCK - query_col
        near = (row_gap >= 0) & (row_gap <= 2 * HALO) & (col_gap >= -HALO) & (col_gap <= HALO)
        near_s[j] = jnp.where(near, 0.0, MASKED)

    own_head = (
        lax.broadcasted_iota(jnp.int32, (LANES, feats), 0) // tile_queries
        == lax.broadcasted_iota(jnp.int32, (LANES, feats), 1) // HEAD_WIDTH
    )
    own_head_turned = (
        lax.broadcasted_iota(jnp.int32, (feats, LANES), 1) // tile_queries
        == lax.broadcasted_iota(jnp.int32, (feats, LANES), 0) // HEAD_WIDTH
    )
    query_lane = lax.broadcasted_iota(jnp.int32, (1, LANES), 1) % tile_queries

    def spread(ref, upper, start):
        tile = jnp.concatenate([
            ref[row_cols(upper * QUERY_ROWS + row, start, tile_cols), :feats] for row in range(QUERY_ROWS)
        ], axis=0)
        if heads == 1:
            return tile
        stacked = jnp.concatenate([tile] * heads, axis=0)
        return jnp.where(own_head, stacked, jnp.zeros_like(stacked))

    def gather(turned):
        if heads == 1:
            tile = turned.T
        else:
            tall = jnp.where(own_head_turned, turned, 0.0).T
            tile = sum(tall[h * tile_queries:(h + 1) * tile_queries] for h in range(heads))
        return tile.astype(jnp.bfloat16)

    def one_tile(upper, tile):
        start = pl.multiple_of(tile * tile_cols, 16)
        keys = pl.ds(upper * QUERY_ROWS * BLOCK, KEYS)
        index = [(tile * (tile_cols // BLOCK) + j + BLOCKS - 1) % BLOCKS for j in range(window)]
        queries = spread(qkv, upper, start)
        grads = spread(go, upper, start)
        scores = [
            nt(k_s[index[j], keys, :], queries)
            + near_s[j]
            + jnp.concatenate([live_s[index[j], keys, :]] * (LANES // 128), axis=1)
            for j in range(window)
        ]
        highest = jnp.max(functools.reduce(jnp.maximum, scores), axis=0, keepdims=True)
        terms = [jnp.exp(score - highest) for score in scores]
        total = jnp.sum(sum(terms), axis=0, keepdims=True)
        query_cells = jnp.zeros((1, LANES), jnp.int32)
        for row in range(QUERY_ROWS):
            cell = cells[HALO + upper * QUERY_ROWS + row]
            query_cells = jnp.where(query_lane // tile_cols == row, cell, query_cells)
        live = start + query_lane % tile_cols < query_cells
        inverse = jnp.where(live, 1.0 / total, 0.0)
        probs = [term * inverse for term in terms]
        grad_probs = [nt(v_s[index[j], keys, :], grads) for j in range(window)]
        delta = jnp.sum(sum(p * g for p, g in zip(probs, grad_probs)), axis=0, keepdims=True)
        weights = [p.astype(jnp.bfloat16) for p in probs]
        grad_scores = [(p * (g - delta)).astype(jnp.bfloat16) for p, g in zip(probs, grad_probs)]
        for j in range(window):
            dv_s[index[j], keys, :] += nn(weights[j], grads)
            dk_s[index[j], keys, :] += nn(grad_scores[j], queries)
        values_turned = jnp.concatenate([vt_s[upper, index[j]] for j in range(window)], axis=1)
        keys_turned = jnp.concatenate([kt_s[upper, index[j]] for j in range(window)], axis=1)
        heads_out = gather(nn(values_turned, jnp.concatenate(weights, axis=0)))
        grad_query = gather(nn(keys_turned, jnp.concatenate(grad_scores, axis=0)))
        for row in range(QUERY_ROWS):
            at = row_cols(upper * QUERY_ROWS + row, start, tile_cols)
            outq[at, :feats] = heads_out[row * tile_cols:(row + 1) * tile_cols]
            outq[at, feats:] = grad_query[row * tile_cols:(row + 1) * tile_cols]

    def tile_pair(tile, carry):
        for upper in range(2):
            one_tile(upper, tile)
        return carry

    for move in moves:
        move.wait()
    grad_heads = nt(held[...], weight[...]).astype(jnp.bfloat16)
    for i in range(steps):
        go[pl.ds(pl.multiple_of(order[i], 16), chunk)] = grad_heads[i * chunk:(i + 1) * chunk]
    lax.fori_loop(0, LONGITUDES // tile_cols, tile_pair, 0)
    moves = [
        pltpu.make_async_copy(outq.at[pl.ds(pl.multiple_of(order[i], 16), chunk)], part, sems.at[i])
        for i, part in enumerate(outq_parts)
    ]
    for move in moves:
        move.start()

    def store_pair(p, carry):
        for first, sums in ((0, dk_s), (feats, dv_s)):
            both = jnp.concatenate(
                [sums[2 * p + half].reshape(EXT_ROWS, BLOCK, feats) for half in range(2)], axis=1
            )
            for row in range(HALO):
                dkv_top[row_cols(row, p * 16, 16), first:first + feats] = both[row].astype(jnp.bfloat16)
                dkv_bot[row_cols(row, p * 16, 16), first:first + feats] = (
                    both[HALO + BAND_ROWS + row].astype(jnp.bfloat16)
                )
            for row in range(BAND_ROWS):
                dkv_own[row_cols(row, p * 16, 16), first:first + feats] = both[HALO + row]
        return carry

    lax.fori_loop(0, BLOCKS // 2, store_pair, 0)
    for move in moves:
        move.wait()


VMEM = pl.BlockSpec(memory_space=pltpu.VMEM)
SMEM = pl.BlockSpec(memory_space=pltpu.SMEM)
HBM = pl.BlockSpec(memory_space=pl.ANY)
BF16, F32 = jnp.bfloat16, jnp.float32


def shape(rows, cols, kind=BF16):
    return jax.ShapeDtypeStruct((rows, cols), kind)


def call(kernel, out_shape, in_specs, out_specs, args, flops, scratch=(), transcendentals=0):
    moved = sum(x.size * x.dtype.itemsize for x in (*args, *out_shape)) if flops else 0
    return pl.pallas_call(
        kernel,
        out_shape=tuple(out_shape),
        in_specs=list(in_specs),
        out_specs=tuple(out_specs),
        scratch_shapes=list(scratch),
        compiler_params=pltpu.CompilerParams(vmem_limit_bytes=60 * 2**20),
        cost_estimate=pl.CostEstimate(
            flops=flops, transcendentals=transcendentals, bytes_accessed=moved
        ),
    )(*args)


def attention(cells, order, qkv, kv_top, kv_bot, weight, upstream):
    steps, (feats, width), chunk = len(upstream), weight.shape, upstream[0].shape[0]
    heads = feats // HEAD_WIDTH
    window = LANES // heads // QUERY_ROWS // BLOCK + 2
    band, halo = BAND_ROWS * LONGITUDES, HALO * LONGITUDES
    pairs = band * heads * KEYS * window
    results = call(
        functools.partial(attention_kernel, heads, steps),
        [shape(chunk, 2 * feats)] * steps
        + [shape(band, 2 * feats, F32), shape(halo, 2 * feats), shape(halo, 2 * feats)],
        [SMEM, SMEM, VMEM, VMEM, VMEM, VMEM] + [HBM] * steps,
        [HBM] * steps + [VMEM] * 3,
        (cells, order, qkv, kv_top, kv_bot, weight, *upstream),
        flops=12 * pairs * HEAD_WIDTH * heads + 2 * band * weight.size,
        transcendentals=pairs,
        scratch=[
            pltpu.VMEM((band, width), BF16),
            pltpu.VMEM((band, 2 * feats), BF16),
            pltpu.VMEM((band, feats), BF16),
            pltpu.VMEM((BLOCKS, EXT_ROWS * BLOCK, feats), BF16),
            pltpu.VMEM((BLOCKS, EXT_ROWS * BLOCK, feats), BF16),
            pltpu.VMEM((2, BLOCKS, feats, KEYS), BF16),
            pltpu.VMEM((2, BLOCKS, feats, KEYS), BF16),
            pltpu.VMEM((BLOCKS, EXT_ROWS * BLOCK, feats), F32),
            pltpu.VMEM((BLOCKS, EXT_ROWS * BLOCK, feats), F32),
            pltpu.VMEM((BLOCKS, EXT_ROWS * BLOCK, 128), F32),
            pltpu.VMEM((window, KEYS, LANES), F32),
            pltpu.SemaphoreType.DMA((steps,)),
        ],
    )
    return (results[:steps], *results[steps:])


def norm_kernel(tokens, gain, normed):
    features = tokens[...].astype(F32)
    inverse = lax.rsqrt(jnp.mean(features * features, axis=1, keepdims=True) + 1e-06)
    normed[...] = (features * inverse * gain[...]).astype(BF16)


def norm(tokens, gain):
    return call(
        norm_kernel, [shape(*tokens.shape)], [VMEM] * 2, [VMEM], (tokens, gain[None, :]), flops=4 * tokens.size
    )[0]


def stacked_moves(parts, held, sems, first=0):
    chunk = parts[0].shape[0]
    return [
        pltpu.make_async_copy(part, held.at[pl.ds(i * chunk, chunk)], sems.at[first + i]) for i, part in enumerate(parts)
    ]


def carry_out(moves):
    for move in moves:
        move.start()
    for move in moves:
        move.wait()


def projection_kernel(steps, feats, order, weight, *refs):
    parts, (qkv, kv_up, kv_down, normed_up, normed_down, held, sems) = refs[:steps], refs[steps:]
    chunk = parts[0].shape[0]
    halo, rest = HALO * LONGITUDES, (BAND_ROWS - HALO) * LONGITUDES
    carry_out([
        pltpu.make_async_copy(part, held.at[pl.ds(pl.multiple_of(order[i], 16), chunk)], sems.at[i])
        for i, part in enumerate(parts)
    ])
    moves = [
        pltpu.make_async_copy(held.at[pl.ds(rest, halo)], normed_up, sems.at[0]),
        pltpu.make_async_copy(held.at[pl.ds(0, halo)], normed_down, sems.at[1]),
    ]
    for move in moves:
        move.start()
    for i in range(3):
        product = nn(held[...], weight[:, i * feats:(i + 1) * feats]).astype(BF16)
        qkv[:, i * feats:(i + 1) * feats] = product
        if i:
            kv_up[:, (i - 1) * feats:i * feats] = product[rest:]
            kv_down[:, (i - 1) * feats:i * feats] = product[:halo]
    for move in moves:
        move.wait()


def projections(order, weight, parts):
    steps, feats, width = len(parts), weight.shape[1] // 3, parts[0].shape[1]
    band, halo = BAND_ROWS * LONGITUDES, HALO * LONGITUDES
    return call(
        functools.partial(projection_kernel, steps, feats),
        [shape(band, 3 * feats)] + [shape(halo, 2 * feats)] * 2 + [shape(halo, width)] * 2,
        [SMEM, VMEM] + [HBM] * steps, [VMEM] * 3 + [HBM] * 2, (order, weight, *parts),
        flops=2 * band * weight.size,
        scratch=[pltpu.VMEM((band, width), BF16), pltpu.SemaphoreType.DMA((steps,))],
    )


def join_kernel(steps, order, own, above, below, *refs):
    outq_parts, parts, whole = refs[:steps], refs[steps:2 * steps], refs[-1]
    chunk, feats = outq_parts[0].shape
    low, high = (BAND_ROWS - HALO) * LONGITUDES, HALO * LONGITUDES
    for outq, part in zip(outq_parts, parts):
        part[:, :feats] = outq[...]
    whole[:low] = (own[:low] + below[:low].astype(F32)).astype(BF16)
    whole[low:high] = (own[low:high] + below[low:].astype(F32) + above[:high - low].astype(F32)).astype(BF16)
    whole[high:] = (own[high:] + above[high - low:].astype(F32)).astype(BF16)
    for i, part in enumerate(parts):
        part[:, feats:] = whole[pl.ds(pl.multiple_of(order[i], 16), chunk), :]


def joined(order, own, above, below, outq_parts):
    steps, (chunk, feats) = len(outq_parts), outq_parts[0].shape
    return call(
        functools.partial(join_kernel, steps),
        [shape(chunk, 2 * feats)] * steps,
        [SMEM] + [VMEM] * (3 + steps), [VMEM] * steps, (order, own, above, below, *outq_parts), flops=0,
        scratch=[pltpu.VMEM((steps * chunk, feats), BF16)],
    )


def weight_grad_kernel(steps, order, *refs):
    (outq_parts, upstream, normed), refs = [refs[i * steps:(i + 1) * steps] for i in range(3)], refs[3 * steps:]
    wide, (grad, outq, up, own, sums, dkv_halos, normed_halos, sems, wide_sems) = refs[:5], refs[5:]
    feats, chunk, halo = outq.shape[1] // 2, outq_parts[0].shape[0], HALO * LONGITUDES
    groups = [
        [
            pltpu.make_async_copy(part, held.at[pl.ds(pl.multiple_of(order[i], 16), chunk)], sems.at[group, i])
            for i, part in enumerate(parts)
        ]
        for group, (parts, held) in enumerate(((outq_parts, outq), (upstream, up), (normed, own)))
    ]
    places = [sums] + [held.at[pl.ds(at, halo)] for held in (dkv_halos, normed_halos) for at in (0, halo)]
    wide_moves = [
        pltpu.make_async_copy(part, held, wide_sems.at[i]) for i, (part, held) in enumerate(zip(wide, places))
    ]
    for move in groups[0] + groups[1] + groups[2] + wide_moves:
        move.start()

    def product(left, right):
        return lax.dot_general(left, right, (((0,), (0,)), ((), ())), preferred_element_type=F32)

    for move in groups[0] + groups[1]:
        move.wait()
    grad[:feats, :] = product(outq[:, :feats], up[...]).astype(BF16)
    for move in groups[2]:
        move.wait()
    grad[feats:2 * feats, :] = product(outq[:, feats:], own[...]).astype(BF16)
    for move in wide_moves:
        move.wait()
    keyval = product(sums[...].astype(BF16), own[...])
    grad[2 * feats:, :] = (keyval + product(dkv_halos[...], normed_halos[...])).astype(BF16)


def weight_grads(order, outq_parts, upstream, normed, dkv, dkv_halos, normed_halos):
    steps, (chunk, rows), width = len(normed), outq_parts[0].shape, normed[0].shape[1]
    band, halos = steps * chunk, 2 * HALO * LONGITUDES
    return call(
        functools.partial(weight_grad_kernel, steps),
        [shape(2 * rows, width)], [SMEM] + [HBM] * (3 * steps + 5), [VMEM],
        (order, *outq_parts, *upstream, *normed, dkv, *dkv_halos, *normed_halos),
        flops=2 * width * rows * (2 * band + halos),
        scratch=[
            pltpu.VMEM((band, rows), BF16), pltpu.VMEM((band, width), BF16), pltpu.VMEM((band, width), BF16),
            pltpu.VMEM((band, rows), F32), pltpu.VMEM((halos, rows), BF16), pltpu.VMEM((halos, width), BF16),
            pltpu.SemaphoreType.DMA((3, steps)), pltpu.SemaphoreType.DMA((5,)),
        ],
    )[0]


def token_kernel(steps, leads, tokens, gain, *refs):
    parts, blocks, (update, grad, left, qkv, out, sems) = refs[:steps], refs[steps:2 * steps], refs[2 * steps:]
    feats = out.shape[0] // steps
    carry_out([
        move for i, block in enumerate(blocks) for move in (
            pltpu.make_async_copy(block.at[pl.ds(0, 3 * feats)], qkv.at[pl.ds(3 * i * feats, 3 * feats)], sems.at[i]),
            pltpu.make_async_copy(block.at[pl.ds(3 * feats, feats)], out.at[pl.ds(i * feats, feats)], sems.at[steps + i]),
        )
    ])
    for i, part in enumerate(parts):
        left[leads[i]] = part[...]
    side_by_side = lambda cut: jnp.concatenate([left[i, :, cut] for i in range(steps)], axis=1)
    update[...] = nn(side_by_side(slice(0, feats)), out[...]).astype(BF16)
    grad_normed = nn(side_by_side(slice(feats, None)), qkv[...])
    features = tokens[...].astype(F32)
    inverse = lax.rsqrt(jnp.mean(features * features, axis=1, keepdims=True) + 1e-06)
    centred = features * inverse
    scaled = gain[...] * grad_normed
    grad[...] = (inverse * (scaled - centred * jnp.mean(scaled * centred, axis=1, keepdims=True))).astype(BF16)


def token_outputs(leads, tokens, gain, parts, blocks):
    steps, (rows, width), chunk = len(blocks), blocks[0].shape, tokens.shape[0]
    feats = rows // 4
    return call(
        functools.partial(token_kernel, steps),
        [shape(chunk, width)] * 2, [SMEM] + [VMEM] * (2 + steps) + [HBM] * steps, [VMEM] * 2,
        (leads, tokens, gain[None, :], *parts, *blocks), flops=2 * steps * chunk * rows * width,
        scratch=[
            pltpu.VMEM((steps, chunk, rows), BF16),
            pltpu.VMEM((3 * steps * feats, width), BF16),
            pltpu.VMEM((steps * feats, width), BF16),
            pltpu.SemaphoreType.DMA((2 * steps,)),
        ],
    )


def finish_kernel(scale, flag, mine, other, grad_qkv, grad_out):
    for i in range(4):
        part = jnp.where(flag[0] == 1, mine[i, 0], other[i, 0]).astype(F32)
        if i == 0:
            grad_out[0] = part * scale
        else:
            factor = scale * HEAD_WIDTH ** -0.5 if i == 1 else scale
            grad_qkv[0, (i - 1) * HEAD_WIDTH:i * HEAD_WIDTH, :] = part * factor


def finished(scale, flag, mine, other):
    heads, width = mine.shape[0] // (4 * HEAD_WIDTH), mine.shape[1]
    by_head = lambda x: x.reshape(4, heads, HEAD_WIDTH, width)
    sums = pl.BlockSpec((4, 1, HEAD_WIDTH, width), lambda h: (0, h, 0, 0))
    result = lambda rows: pl.BlockSpec((1, rows, width), lambda h: (h, 0, 0))
    return pl.pallas_call(
        functools.partial(finish_kernel, scale),
        grid=(heads,),
        out_shape=(
            jax.ShapeDtypeStruct((heads, 3 * HEAD_WIDTH, width), F32),
            jax.ShapeDtypeStruct((heads, HEAD_WIDTH, width), F32),
        ),
        in_specs=[SMEM, sums, sums],
        out_specs=(result(3 * HEAD_WIDTH), result(HEAD_WIDTH)),
        compiler_params=pltpu.CompilerParams(vmem_limit_bytes=32 * 2**20),
        cost_estimate=pl.CostEstimate(flops=mine.size, transcendentals=0, bytes_accessed=8 * mine.size),
    )(flag, by_head(mine), by_head(other))


from jax.sharding import Mesh, PartitionSpec as P

WIDTH = 1024
GROUP = ("y", "m", "c")


def owners(halves):
    if halves == 2:
        return [
            lambda y, m, c: (c, 1 - m if c == y else m, y),
            lambda y, m, c: (c, 1 - m if c == y else m, 1 - y),
            lambda y, m, c: (c, m if c == y else 1 - m, 1 - y),
            lambda y, m, c: (c, m if c == y else 1 - m, y),
        ]
    return [
        lambda y, m, c, dm=dm, dc=dc: (c, (m + dm) % halves, (y + dc) % 2) for dc in range(2) for dm in range(halves)
    ]


def passed_along(x, by):
    length = lax.axis_size("z") * 2
    pairs = [(i, i + by) for i in range(length) if 0 <= i + by < length]
    return lax.ppermute(x, ("z", "c"), pairs)


def after(x, *others):
    return lax.optimization_barrier((x, *others))[0]


def on_device(tokens, gain, qkv_weight, out_weight, row_cells, upstream):
    heads = qkv_weight.shape[0]
    feats = heads * HEAD_WIDTH
    band_tokens = BAND_ROWS * LONGITUDES
    chunk = tokens.shape[0]
    halves, layers = lax.axis_size("m"), lax.axis_size("z")
    z, y, m, c = (lax.axis_index(axis) for axis in ("z",) + GROUP)
    grad_scale = 4.0 / math.sqrt(band_tokens * layers * 2)
    band_start = (z * 2 + c) * BAND_ROWS
    cells = lax.dynamic_slice_in_dim(jnp.pad(row_cells, (HALO, HALO)), band_start, EXT_ROWS)

    at = lambda y, m, c: (y * halves + m) * 2 + c
    spots = [(y, m, c) for y in range(2) for m in range(halves) for c in range(2)]
    slots = [[owner(*spot) for spot in spots] for owner in owners(halves)]
    here = lambda table: jnp.asarray(table, jnp.int32)[at(y, m, c)]
    order = here([[(slot[i][1] * 2 + slot[i][2]) * chunk for slot in slots] for i in range(len(spots))])

    def lead(slot, spot):
        far = spots[slot.index(spot)]
        return (far[0] - spot[2]) % 2 * halves + (far[1] - spot[1]) % halves

    leads = here([[lead(slot, spot) for slot in slots] for spot in spots])

    def permuted(x, pairs):
        return lax.ppermute(x, GROUP, [(at(*a), at(*b)) for a, b in pairs])

    def send_back(parts):
        return [permuted(x, list(zip(spots, slot))) for x, slot in zip(parts, slots)]

    def gathered(x, *others):
        sent = lambda slot: permuted(x, list(zip(slot, spots)))
        if halves != 2:
            parts = [sent(slot) for slot in slots]
            return parts, parts
        first, second = lax.optimization_barrier((sent(slots[0]), sent(slots[1])))
        hop = first, second
        first = after(first, *others)
        third = permuted(
            jnp.where(c == y, first, x),
            [(spot, (1 - spot[0], spot[1], spot[0]) if spot[2] == spot[0] else (spot[0], spot[1], spot[0])) for spot in spots],
        )
        fourth = permuted(
            first, [(spot, (spot[0], 1 - spot[1], spot[2])) for spot in spots if spot[2] != spot[0]]
        )
        third, fourth = lax.optimization_barrier((third, fourth))
        return [first, second, third, jnp.where(c == y, x, fourth)], hop

    def from_ahead(x, dm):
        return lax.ppermute(x, "m", [((i + dm) % halves, i) for i in range(halves)])

    def from_sibling(x):
        return lax.ppermute(x, "c", [(0, 1), (1, 0)])

    normed = norm(tokens, gain)
    normed, qkv_weight, out_weight = lax.optimization_barrier((normed, qkv_weight, out_weight))

    def split(qkv, out):
        eighth = jnp.asarray([HEAD_WIDTH ** -0.5, 1.0, 1.0], BF16)[None, :, None, None]
        qkv = (qkv.reshape(heads, 3, HEAD_WIDTH, WIDTH) * eighth).transpose(1, 0, 2, 3)
        return jnp.concatenate([qkv.reshape(3 * feats, WIDTH), out.reshape(feats, WIDTH)], axis=0)

    blocks = [split(qkv_weight, out_weight)]
    normed_parts, hop = gathered(normed)
    sibling = from_sibling(after(blocks[0], *hop))
    group = jnp.where(c == y, blocks[0], sibling)
    group_qkv, group_out = group[:3 * feats].T, group[3 * feats:]

    *normed_parts, group_qkv, group_out = lax.optimization_barrier((*normed_parts, group_qkv, group_out))
    qkv, kv_up, kv_down, normed_up, normed_down = projections(order, group_qkv, normed_parts)
    kv_top, kv_bot = passed_along(kv_up, 1), passed_along(kv_down, -1)
    upstream_parts, _ = gathered(after(upstream, *normed_parts), qkv)

    kv_top, kv_bot, normed_up, normed_down, *upstream_parts = lax.optimization_barrier(
        (kv_top, kv_bot, normed_up, normed_down, *upstream_parts)
    )
    normed_halos = passed_along(normed_up, 1), passed_along(normed_down, -1)
    ahead = [from_ahead(after(blocks[0], *upstream_parts), dm) for dm in range(1, halves)]
    outq_parts, dkv, dkv_top, dkv_bot = attention(cells, order, qkv, kv_top, kv_bot, group_out, upstream_parts)

    from_above, from_below = passed_along(dkv_top, -1), passed_along(dkv_bot, 1)
    grads = weight_grads(
        order, outq_parts, upstream_parts, normed_parts, dkv, (dkv_top, dkv_bot), normed_halos
    )
    grads_sum = lax.psum(grads, ("z", "c"))
    parts = joined(after(order, grads), dkv, from_above, from_below, outq_parts)
    parts, ahead = lax.optimization_barrier((parts, ahead))
    parts_own = send_back(parts)
    ahead = [after(block, grads_sum) for block in ahead]
    blocks += ahead + [sibling] + [from_sibling(block) for block in ahead]
    update, grad_input = token_outputs(leads, tokens, gain, parts_own, blocks)
    grads = after(grads_sum, *parts_own)
    pairs = [((1 - y, m, 1 - y), (y, m, 1 - y)) for y in range(2) for m in range(halves)]
    flag = after(jnp.reshape(c == y, (1,)).astype(jnp.int32), grad_input, update)
    grad_qkv, grad_out = finished(grad_scale, flag, grads, permuted(grads, pairs))
    return update, grad_input, grad_qkv, grad_out


def solution(mesh):
    devices = mesh.devices.reshape(mesh.shape["lat"] // 2, 2, mesh.shape["mp"] // 2, 2)
    tokens, weights = P(("z", "y", "m", "c"), None), P(("m", "c"), None, None)
    return jax.shard_map(
        on_device,
        mesh=Mesh(devices, ("z", "y", "m", "c")),
        in_specs=(tokens, P(), weights, weights, P(), tokens),
        out_specs=(tokens, tokens, weights, weights),
        check_vma=False,
    )
```

```python
import functools
import math
import jax
import jax.numpy as jnp
from jax import lax
from jax.experimental import pallas as pl
from jax.experimental.pallas import tpu as pltpu

HEAD_WIDTH = 64
LONGITUDES = 256
BAND_ROWS = 8
HALO = 6
EXT_ROWS = BAND_ROWS + 2 * HALO
LANES = 256
QUERY_ROWS = 4
KEY_ROWS = QUERY_ROWS + 2 * HALO
BLOCK = 8
BLOCKS = LONGITUDES // BLOCK
KEYS = KEY_ROWS * BLOCK
MASKED = -1e30


def nn(a, b):
    return lax.dot_general(a, b, (((1,), (0,)), ((), ())), preferred_element_type=jnp.float32)


def nt(a, b):
    return lax.dot_general(a, b, (((1,), (1,)), ((), ())), preferred_element_type=jnp.float32)


def row_cols(row, start, size):
    return pl.ds(pl.multiple_of(row * LONGITUDES + start, 16), size)


def attention_kernel(
    heads, steps,
    cells, order, qkv, kv_top, kv_bot, weight, *refs,
):
    upstream, refs = refs[:steps], refs[steps:]
    outq_parts, refs = refs[:steps], refs[steps:]
    dkv_own, dkv_top, dkv_bot, held, outq, go, k_s, v_s, kt_s, vt_s, dk_s, dv_s, live_s, near_s, sems = refs
    feats = heads * HEAD_WIDTH
    chunk = BAND_ROWS * LONGITUDES // steps
    moves = [
        pltpu.make_async_copy(part, held.at[pl.ds(i * chunk, chunk)], sems.at[i]) for i, part in enumerate(upstream)
    ]
    for move in moves:
        move.start()
    tile_cols = LANES // heads // QUERY_ROWS
    tile_queries = QUERY_ROWS * tile_cols
    window = tile_cols // BLOCK + 2

    def load_pair(p, carry):
        for first, rows_s, turned_s in ((0, k_s, kt_s), (feats, v_s, vt_s)):
            both = jnp.stack(
                [kv_top[row_cols(row, p * 16, 16), first:first + feats] for row in range(HALO)]
                + [qkv[row_cols(row, p * 16, 16), feats + first:2 * feats + first] for row in range(BAND_ROWS)]
                + [kv_bot[row_cols(row, p * 16, 16), first:first + feats] for row in range(HALO)]
            ).astype(jnp.float32)
            for half in range(2):
                block = both[:, 8 * half:8 * half + 8, :].reshape(EXT_ROWS * BLOCK, feats)
                rows_s[2 * p + half] = block.astype(jnp.bfloat16)
                for upper in range(2):
                    low = upper * QUERY_ROWS * BLOCK
                    turned_s[upper, 2 * p + half] = block[low:low + KEYS].T.astype(jnp.bfloat16)
        for half in range(2):
            col = (2 * p + half) * BLOCK + lax.broadcasted_iota(jnp.int32, (BLOCK, 128), 0)
            for row in range(EXT_ROWS):
                live_s[2 * p + half, row * BLOCK:(row + 1) * BLOCK, :] = jnp.where(col < cells[row], 0.0, MASKED)
        return carry

    lax.fori_loop(0, BLOCKS // 2, load_pair, 0)
    dk_s[...] = jnp.zeros_like(dk_s)
    dv_s[...] = jnp.zeros_like(dv_s)

    lane = lax.broadcasted_iota(jnp.int32, (KEYS, LANES), 1) % tile_queries
    query_row = lane // tile_cols
    query_col = lane % tile_cols
    key = lax.broadcasted_iota(jnp.int32, (KEYS, LANES), 0)
    row_gap = key // BLOCK - query_row
    for j in range(window):
        col_gap = (j - 1) * BLOCK + key % BLOCK - query_col
        near = (row_gap >= 0) & (row_gap <= 2 * HALO) & (col_gap >= -HALO) & (col_gap <= HALO)
        near_s[j] = jnp.where(near, 0.0, MASKED)

    own_head = (
        lax.broadcasted_iota(jnp.int32, (LANES, feats), 0) // tile_queries
        == lax.broadcasted_iota(jnp.int32, (LANES, feats), 1) // HEAD_WIDTH
    )
    own_head_turned = (
        lax.broadcasted_iota(jnp.int32, (feats, LANES), 1) // tile_queries
        == lax.broadcasted_iota(jnp.int32, (feats, LANES), 0) // HEAD_WIDTH
    )
    query_lane = lax.broadcasted_iota(jnp.int32, (1, LANES), 1) % tile_queries

    def spread(ref, upper, start):
        tile = jnp.concatenate([
            ref[row_cols(upper * QUERY_ROWS + row, start, tile_cols), :feats] for row in range(QUERY_ROWS)
        ], axis=0)
        if heads == 1:
            return tile
        stacked = jnp.concatenate([tile] * heads, axis=0)
        return jnp.where(own_head, stacked, jnp.zeros_like(stacked))

    def gather(turned):
        if heads == 1:
            tile = turned.T
        else:
            tall = jnp.where(own_head_turned, turned, 0.0).T
            tile = sum(tall[h * tile_queries:(h + 1) * tile_queries] for h in range(heads))
        return tile.astype(jnp.bfloat16)

    def one_tile(upper, tile):
        start = pl.multiple_of(tile * tile_cols, 16)
        keys = pl.ds(upper * QUERY_ROWS * BLOCK, KEYS)
        index = [(tile * (tile_cols // BLOCK) + j + BLOCKS - 1) % BLOCKS for j in range(window)]
        queries = spread(qkv, upper, start)
        grads = spread(go, upper, start)
        scores = [
            nt(k_s[index[j], keys, :], queries)
            + near_s[j]
            + jnp.concatenate([live_s[index[j], keys, :]] * (LANES // 128), axis=1)
            for j in range(window)
        ]
        grad_probs = [nt(v_s[index[j], keys, :], grads) for j in range(window)]
        yield
        highest = jnp.max(functools.reduce(jnp.maximum, scores), axis=0, keepdims=True)
        terms = [jnp.exp(score - highest) for score in scores]
        total = jnp.sum(sum(terms), axis=0, keepdims=True)
        query_cells = jnp.zeros((1, LANES), jnp.int32)
        for row in range(QUERY_ROWS):
            cell = cells[HALO + upper * QUERY_ROWS + row]
            query_cells = jnp.where(query_lane // tile_cols == row, cell, query_cells)
        live = start + query_lane % tile_cols < query_cells
        inverse = jnp.where(live, 1.0 / total, 0.0)
        probs = [term * inverse for term in terms]
        delta = jnp.sum(sum(p * g for p, g in zip(probs, grad_probs)), axis=0, keepdims=True)
        weights = [p.astype(jnp.bfloat16) for p in probs]
        grad_scores = [(p * (g - delta)).astype(jnp.bfloat16) for p, g in zip(probs, grad_probs)]
        yield
        for j in range(window):
            dv_s[index[j], keys, :] += nn(weights[j], grads)
            dk_s[index[j], keys, :] += nn(grad_scores[j], queries)
        values_turned = jnp.concatenate([vt_s[upper, index[j]] for j in range(window)], axis=1)
        keys_turned = jnp.concatenate([kt_s[upper, index[j]] for j in range(window)], axis=1)
        heads_out = gather(nn(values_turned, jnp.concatenate(weights, axis=0)))
        grad_query = gather(nn(keys_turned, jnp.concatenate(grad_scores, axis=0)))
        for row in range(QUERY_ROWS):
            at = row_cols(upper * QUERY_ROWS + row, start, tile_cols)
            outq[at, :feats] = heads_out[row * tile_cols:(row + 1) * tile_cols]
            outq[at, feats:] = grad_query[row * tile_cols:(row + 1) * tile_cols]

    def tile_pair(tile, carry):
        low, high = one_tile(0, tile), one_tile(1, tile)
        for stage in (low, high, low, low, high, high):
            next(stage, None)
        return carry

    for move in moves:
        move.wait()
    grad_heads = nt(held[...], weight[...]).astype(jnp.bfloat16)
    for i in range(steps):
        go[pl.ds(pl.multiple_of(order[i], 16), chunk)] = grad_heads[i * chunk:(i + 1) * chunk]
    lax.fori_loop(0, LONGITUDES // tile_cols, tile_pair, 0)
    moves = [
        pltpu.make_async_copy(outq.at[pl.ds(pl.multiple_of(order[i], 16), chunk)], part, sems.at[i])
        for i, part in enumerate(outq_parts)
    ]
    for move in moves:
        move.start()

    def store_pair(p, carry):
        for first, sums in ((0, dk_s), (feats, dv_s)):
            both = jnp.concatenate(
                [sums[2 * p + half].reshape(EXT_ROWS, BLOCK, feats) for half in range(2)], axis=1
            )
            for row in range(HALO):
                dkv_top[row_cols(row, p * 16, 16), first:first + feats] = both[row].astype(jnp.bfloat16)
                dkv_bot[row_cols(row, p * 16, 16), first:first + feats] = (
                    both[HALO + BAND_ROWS + row].astype(jnp.bfloat16)
                )
            for row in range(BAND_ROWS):
                dkv_own[row_cols(row, p * 16, 16), first:first + feats] = both[HALO + row]
        return carry

    lax.fori_loop(0, BLOCKS // 2, store_pair, 0)
    for move in moves:
        move.wait()


VMEM = pl.BlockSpec(memory_space=pltpu.VMEM)
SMEM = pl.BlockSpec(memory_space=pltpu.SMEM)
HBM = pl.BlockSpec(memory_space=pl.ANY)
BF16, F32 = jnp.bfloat16, jnp.float32


def shape(rows, cols, kind=BF16):
    return jax.ShapeDtypeStruct((rows, cols), kind)


def call(kernel, out_shape, in_specs, out_specs, args, flops, scratch=(), transcendentals=0):
    moved = sum(x.size * x.dtype.itemsize for x in (*args, *out_shape)) if flops else 0
    return pl.pallas_call(
        kernel,
        out_shape=tuple(out_shape),
        in_specs=list(in_specs),
        out_specs=tuple(out_specs),
        scratch_shapes=list(scratch),
        compiler_params=pltpu.CompilerParams(vmem_limit_bytes=60 * 2**20),
        cost_estimate=pl.CostEstimate(
            flops=flops, transcendentals=transcendentals, bytes_accessed=moved
        ),
    )(*args)


def attention(cells, order, qkv, kv_top, kv_bot, weight, upstream):
    steps, (feats, width), chunk = len(upstream), weight.shape, upstream[0].shape[0]
    heads = feats // HEAD_WIDTH
    window = LANES // heads // QUERY_ROWS // BLOCK + 2
    band, halo = BAND_ROWS * LONGITUDES, HALO * LONGITUDES
    pairs = band * heads * KEYS * window
    results = call(
        functools.partial(attention_kernel, heads, steps),
        [shape(chunk, 2 * feats)] * steps
        + [shape(band, 2 * feats, F32), shape(halo, 2 * feats), shape(halo, 2 * feats)],
        [SMEM, SMEM, VMEM, VMEM, VMEM, VMEM] + [HBM] * steps,
        [HBM] * steps + [VMEM] * 3,
        (cells, order, qkv, kv_top, kv_bot, weight, *upstream),
        flops=12 * pairs * HEAD_WIDTH * heads + 2 * band * weight.size,
        transcendentals=pairs,
        scratch=[
            pltpu.VMEM((band, width), BF16),
            pltpu.VMEM((band, 2 * feats), BF16),
            pltpu.VMEM((band, feats), BF16),
            pltpu.VMEM((BLOCKS, EXT_ROWS * BLOCK, feats), BF16),
            pltpu.VMEM((BLOCKS, EXT_ROWS * BLOCK, feats), BF16),
            pltpu.VMEM((2, BLOCKS, feats, KEYS), BF16),
            pltpu.VMEM((2, BLOCKS, feats, KEYS), BF16),
            pltpu.VMEM((BLOCKS, EXT_ROWS * BLOCK, feats), F32),
            pltpu.VMEM((BLOCKS, EXT_ROWS * BLOCK, feats), F32),
            pltpu.VMEM((BLOCKS, EXT_ROWS * BLOCK, 128), F32),
            pltpu.VMEM((window, KEYS, LANES), F32),
            pltpu.SemaphoreType.DMA((steps,)),
        ],
    )
    return (results[:steps], *results[steps:])


def norm_kernel(tokens, gain, normed):
    features = tokens[...].astype(F32)
    inverse = lax.rsqrt(jnp.mean(features * features, axis=1, keepdims=True) + 1e-06)
    normed[...] = (features * inverse * gain[...]).astype(BF16)


def norm(tokens, gain):
    return call(
        norm_kernel, [shape(*tokens.shape)], [VMEM] * 2, [VMEM], (tokens, gain[None, :]), flops=4 * tokens.size
    )[0]


def stacked_moves(parts, held, sems, first=0):
    chunk = parts[0].shape[0]
    return [
        pltpu.make_async_copy(part, held.at[pl.ds(i * chunk, chunk)], sems.at[first + i]) for i, part in enumerate(parts)
    ]


def carry_out(moves):
    for move in moves:
        move.start()
    for move in moves:
        move.wait()


def projection_kernel(steps, feats, order, weight, *refs):
    parts, (qkv, kv_up, kv_down, normed_up, normed_down, held, sems) = refs[:steps], refs[steps:]
    chunk = parts[0].shape[0]
    halo, rest = HALO * LONGITUDES, (BAND_ROWS - HALO) * LONGITUDES
    carry_out([
        pltpu.make_async_copy(part, held.at[pl.ds(pl.multiple_of(order[i], 16), chunk)], sems.at[i])
        for i, part in enumerate(parts)
    ])
    moves = [
        pltpu.make_async_copy(held.at[pl.ds(rest, halo)], normed_up, sems.at[0]),
        pltpu.make_async_copy(held.at[pl.ds(0, halo)], normed_down, sems.at[1]),
    ]
    for move in moves:
        move.start()
    for i in range(3):
        product = nn(held[...], weight[:, i * feats:(i + 1) * feats]).astype(BF16)
        qkv[:, i * feats:(i + 1) * feats] = product
        if i:
            kv_up[:, (i - 1) * feats:i * feats] = product[rest:]
            kv_down[:, (i - 1) * feats:i * feats] = product[:halo]
    for move in moves:
        move.wait()


def projections(order, weight, parts):
    steps, feats, width = len(parts), weight.shape[1] // 3, parts[0].shape[1]
    band, halo = BAND_ROWS * LONGITUDES, HALO * LONGITUDES
    return call(
        functools.partial(projection_kernel, steps, feats),
        [shape(band, 3 * feats)] + [shape(halo, 2 * feats)] * 2 + [shape(halo, width)] * 2,
        [SMEM, VMEM] + [HBM] * steps, [VMEM] * 3 + [HBM] * 2, (order, weight, *parts),
        flops=2 * band * weight.size,
        scratch=[pltpu.VMEM((band, width), BF16), pltpu.SemaphoreType.DMA((steps,))],
    )


def join_kernel(steps, order, own, above, below, *refs):
    outq_parts, parts, whole = refs[:steps], refs[steps:2 * steps], refs[-1]
    chunk, feats = outq_parts[0].shape
    low, high = (BAND_ROWS - HALO) * LONGITUDES, HALO * LONGITUDES
    for outq, part in zip(outq_parts, parts):
        part[:, :feats] = outq[...]
    whole[:low] = (own[:low] + below[:low].astype(F32)).astype(BF16)
    whole[low:high] = (own[low:high] + below[low:].astype(F32) + above[:high - low].astype(F32)).astype(BF16)
    whole[high:] = (own[high:] + above[high - low:].astype(F32)).astype(BF16)
    for i, part in enumerate(parts):
        part[:, feats:] = whole[pl.ds(pl.multiple_of(order[i], 16), chunk), :]


def joined(order, own, above, below, outq_parts):
    steps, (chunk, feats) = len(outq_parts), outq_parts[0].shape
    return call(
        functools.partial(join_kernel, steps),
        [shape(chunk, 2 * feats)] * steps,
        [SMEM] + [VMEM] * (3 + steps), [VMEM] * steps, (order, own, above, below, *outq_parts), flops=0,
        scratch=[pltpu.VMEM((steps * chunk, feats), BF16)],
    )


def weight_grad_kernel(steps, order, *refs):
    (outq_parts, upstream, normed), refs = [refs[i * steps:(i + 1) * steps] for i in range(3)], refs[3 * steps:]
    dkv, dkv_top, dkv_bot, normed_top, normed_bot, grad, outq, up, own, sems = refs
    feats, chunk = outq.shape[1] // 2, outq_parts[0].shape[0]
    groups = [
        [
            pltpu.make_async_copy(part, held.at[pl.ds(pl.multiple_of(order[i], 16), chunk)], sems.at[group, i])
            for i, part in enumerate(parts)
        ]
        for group, (parts, held) in enumerate(((outq_parts, outq), (normed, own), (upstream, up)))
    ]
    for moves in groups:
        for move in moves:
            move.start()

    def product(left, right):
        return lax.dot_general(left, right, (((0,), (0,)), ((), ())), preferred_element_type=F32)

    keyval = product(dkv_top[...], normed_top[...]) + product(dkv_bot[...], normed_bot[...])
    for moves in groups[:2]:
        for move in moves:
            move.wait()
    grad[2 * feats:, :] = (keyval + product(dkv[...].astype(BF16), own[...])).astype(BF16)
    grad[feats:2 * feats, :] = product(outq[:, feats:], own[...]).astype(BF16)
    for move in groups[2]:
        move.wait()
    grad[:feats, :] = product(outq[:, :feats], up[...]).astype(BF16)


def weight_grads(order, outq_parts, upstream, normed, dkv, dkv_halos, normed_halos):
    steps, (chunk, rows), width = len(normed), outq_parts[0].shape, normed[0].shape[1]
    band = steps * chunk
    return call(
        functools.partial(weight_grad_kernel, steps),
        [shape(2 * rows, width)], [SMEM] + [HBM] * (3 * steps) + [VMEM] * 5, [VMEM],
        (order, *outq_parts, *upstream, *normed, dkv, *dkv_halos, *normed_halos),
        flops=2 * width * rows * (2 * band + 2 * HALO * LONGITUDES),
        scratch=[
            pltpu.VMEM((band, rows), BF16), pltpu.VMEM((band, width), BF16), pltpu.VMEM((band, width), BF16),
            pltpu.SemaphoreType.DMA((3, steps)),
        ],
    )[0]


def token_kernel(steps, leads, tokens, gain, *refs):
    parts, blocks, (update, grad, left, qkv, out, sems) = refs[:steps], refs[steps:2 * steps], refs[2 * steps:]
    feats = out.shape[0] // steps
    carry_out([
        move for i, block in enumerate(blocks) for move in (
            pltpu.make_async_copy(block.at[pl.ds(0, 3 * feats)], qkv.at[pl.ds(3 * i * feats, 3 * feats)], sems.at[i]),
            pltpu.make_async_copy(block.at[pl.ds(3 * feats, feats)], out.at[pl.ds(i * feats, feats)], sems.at[steps + i]),
        )
    ])
    for i, part in enumerate(parts):
        left[leads[i]] = part[...]
    side_by_side = lambda cut: jnp.concatenate([left[i, :, cut] for i in range(steps)], axis=1)
    update[...] = nn(side_by_side(slice(0, feats)), out[...]).astype(BF16)
    grad_normed = nn(side_by_side(slice(feats, None)), qkv[...])
    features = tokens[...].astype(F32)
    inverse = lax.rsqrt(jnp.mean(features * features, axis=1, keepdims=True) + 1e-06)
    centred = features * inverse
    scaled = gain[...] * grad_normed
    grad[...] = (inverse * (scaled - centred * jnp.mean(scaled * centred, axis=1, keepdims=True))).astype(BF16)


def token_outputs(leads, tokens, gain, parts, blocks):
    steps, (rows, width), chunk = len(blocks), blocks[0].shape, tokens.shape[0]
    feats = rows // 4
    return call(
        functools.partial(token_kernel, steps),
        [shape(chunk, width)] * 2, [SMEM] + [VMEM] * (2 + steps) + [HBM] * steps, [VMEM] * 2,
        (leads, tokens, gain[None, :], *parts, *blocks), flops=2 * steps * chunk * rows * width,
        scratch=[
            pltpu.VMEM((steps, chunk, rows), BF16),
            pltpu.VMEM((3 * steps * feats, width), BF16),
            pltpu.VMEM((steps * feats, width), BF16),
            pltpu.SemaphoreType.DMA((2 * steps,)),
        ],
    )


def finish_kernel(scale, flag, mine, other, grad_qkv, grad_out):
    for i in range(4):
        part = jnp.where(flag[0] == 1, mine[i, 0], other[i, 0]).astype(F32)
        if i == 0:
            grad_out[0] = part * scale
        else:
            factor = scale * HEAD_WIDTH ** -0.5 if i == 1 else scale
            grad_qkv[0, (i - 1) * HEAD_WIDTH:i * HEAD_WIDTH, :] = part * factor


def finished(scale, flag, mine, other):
    heads, width = mine.shape[0] // (4 * HEAD_WIDTH), mine.shape[1]
    by_head = lambda x: x.reshape(4, heads, HEAD_WIDTH, width)
    sums = pl.BlockSpec((4, 1, HEAD_WIDTH, width), lambda h: (0, h, 0, 0))
    result = lambda rows: pl.BlockSpec((1, rows, width), lambda h: (h, 0, 0))
    return pl.pallas_call(
        functools.partial(finish_kernel, scale),
        grid=(heads,),
        out_shape=(
            jax.ShapeDtypeStruct((heads, 3 * HEAD_WIDTH, width), F32),
            jax.ShapeDtypeStruct((heads, HEAD_WIDTH, width), F32),
        ),
        in_specs=[SMEM, sums, sums],
        out_specs=(result(3 * HEAD_WIDTH), result(HEAD_WIDTH)),
        compiler_params=pltpu.CompilerParams(vmem_limit_bytes=32 * 2**20),
        cost_estimate=pl.CostEstimate(flops=mine.size, transcendentals=0, bytes_accessed=8 * mine.size),
    )(flag, by_head(mine), by_head(other))


from jax.sharding import Mesh, PartitionSpec as P

WIDTH = 1024
GROUP = ("y", "m", "c")


def owners(halves):
    if halves == 2:
        return [
            lambda y, m, c: (c, 1 - m if c == y else m, y),
            lambda y, m, c: (c, 1 - m if c == y else m, 1 - y),
            lambda y, m, c: (c, m if c == y else 1 - m, 1 - y),
            lambda y, m, c: (c, m if c == y else 1 - m, y),
        ]
    return [
        lambda y, m, c, dm=dm, dc=dc: (c, (m + dm) % halves, (y + dc) % 2) for dc in range(2) for dm in range(halves)
    ]


def passed_along(x, by):
    length = lax.axis_size("z") * 2
    pairs = [(i, i + by) for i in range(length) if 0 <= i + by < length]
    return lax.ppermute(x, ("z", "c"), pairs)


def after(x, *others):
    return lax.optimization_barrier((x, *others))[0]


def on_device(tokens, gain, qkv_weight, out_weight, row_cells, upstream):
    heads = qkv_weight.shape[0]
    feats = heads * HEAD_WIDTH
    band_tokens = BAND_ROWS * LONGITUDES
    chunk = tokens.shape[0]
    halves, layers = lax.axis_size("m"), lax.axis_size("z")
    z, y, m, c = (lax.axis_index(axis) for axis in ("z",) + GROUP)
    grad_scale = 4.0 / math.sqrt(band_tokens * layers * 2)
    band_start = (z * 2 + c) * BAND_ROWS
    cells = lax.dynamic_slice_in_dim(jnp.pad(row_cells, (HALO, HALO)), band_start, EXT_ROWS)

    at = lambda y, m, c: (y * halves + m) * 2 + c
    spots = [(y, m, c) for y in range(2) for m in range(halves) for c in range(2)]
    slots = [[owner(*spot) for spot in spots] for owner in owners(halves)]
    here = lambda table: jnp.asarray(table, jnp.int32)[at(y, m, c)]
    order = here([[(slot[i][1] * 2 + slot[i][2]) * chunk for slot in slots] for i in range(len(spots))])

    def lead(slot, spot):
        far = spots[slot.index(spot)]
        return (far[0] - spot[2]) % 2 * halves + (far[1] - spot[1]) % halves

    leads = here([[lead(slot, spot) for slot in slots] for spot in spots])

    def permuted(x, pairs):
        return lax.ppermute(x, GROUP, [(at(*a), at(*b)) for a, b in pairs])

    def send_back(parts):
        return [permuted(x, list(zip(spots, slot))) for x, slot in zip(parts, slots)]

    def gathered(x, *others):
        sent = lambda slot: permuted(x, list(zip(slot, spots)))
        if halves != 2:
            parts = [sent(slot) for slot in slots]
            return parts, parts
        first, second = lax.optimization_barrier((sent(slots[0]), sent(slots[1])))
        hop = first, second
        first = after(first, *others)
        third = permuted(
            jnp.where(c == y, first, x),
            [(spot, (1 - spot[0], spot[1], spot[0]) if spot[2] == spot[0] else (spot[0], spot[1], spot[0])) for spot in spots],
        )
        fourth = permuted(
            first, [(spot, (spot[0], 1 - spot[1], spot[2])) for spot in spots if spot[2] != spot[0]]
        )
        third, fourth = lax.optimization_barrier((third, fourth))
        return [first, second, third, jnp.where(c == y, x, fourth)], hop

    def from_ahead(x, dm):
        return lax.ppermute(x, "m", [((i + dm) % halves, i) for i in range(halves)])

    def from_sibling(x):
        return lax.ppermute(x, "c", [(0, 1), (1, 0)])

    normed = norm(tokens, gain)
    normed, qkv_weight, out_weight = lax.optimization_barrier((normed, qkv_weight, out_weight))

    def split(qkv, out):
        eighth = jnp.asarray([HEAD_WIDTH ** -0.5, 1.0, 1.0], BF16)[None, :, None, None]
        qkv = (qkv.reshape(heads, 3, HEAD_WIDTH, WIDTH) * eighth).transpose(1, 0, 2, 3)
        return jnp.concatenate([qkv.reshape(3 * feats, WIDTH), out.reshape(feats, WIDTH)], axis=0)

    blocks = [split(qkv_weight, out_weight)]
    normed_parts, hop = gathered(normed)
    sibling = from_sibling(after(blocks[0], *hop))
    group = jnp.where(c == y, blocks[0], sibling)
    group_qkv, group_out = group[:3 * feats].T, group[3 * feats:]

    *normed_parts, group_qkv, group_out = lax.optimization_barrier((*normed_parts, group_qkv, group_out))
    qkv, kv_up, kv_down, normed_up, normed_down = projections(order, group_qkv, normed_parts)
    kv_top, kv_bot = passed_along(kv_up, 1), passed_along(kv_down, -1)
    upstream_parts, _ = gathered(after(upstream, *normed_parts), qkv)

    kv_top, kv_bot, normed_up, normed_down, *upstream_parts = lax.optimization_barrier(
        (kv_top, kv_bot, normed_up, normed_down, *upstream_parts)
    )
    normed_halos = passed_along(normed_up, 1), passed_along(normed_down, -1)
    ahead = [from_ahead(after(blocks[0], *upstream_parts), dm) for dm in range(1, halves)]
    outq_parts, dkv, dkv_top, dkv_bot = attention(cells, order, qkv, kv_top, kv_bot, group_out, upstream_parts)

    from_above, from_below = passed_along(dkv_top, -1), passed_along(dkv_bot, 1)
    grads = weight_grads(
        order, outq_parts, upstream_parts, normed_parts, dkv, (dkv_top, dkv_bot), normed_halos
    )
    grads_sum = lax.psum(grads, ("z", "c"))
    parts = joined(after(order, grads), dkv, from_above, from_below, outq_parts)
    parts, ahead = lax.optimization_barrier((parts, ahead))
    parts_own = send_back(parts)
    ahead = [after(block, grads_sum) for block in ahead]
    blocks += ahead + [sibling] + [from_sibling(block) for block in ahead]
    update, grad_input = token_outputs(leads, tokens, gain, parts_own, blocks)
    grads = after(grads_sum, *parts_own)
    pairs = [((1 - y, m, 1 - y), (y, m, 1 - y)) for y in range(2) for m in range(halves)]
    flag = after(jnp.reshape(c == y, (1,)).astype(jnp.int32), grad_input, update)
    grad_qkv, grad_out = finished(grad_scale, flag, grads, permuted(grads, pairs))
    return update, grad_input, grad_qkv, grad_out


def solution(mesh):
    devices = mesh.devices.reshape(mesh.shape["lat"] // 2, 2, mesh.shape["mp"] // 2, 2)
    tokens, weights = P(("z", "y", "m", "c"), None), P(("m", "c"), None, None)
    return jax.shard_map(
        on_device,
        mesh=Mesh(devices, ("z", "y", "m", "c")),
        in_specs=(tokens, P(), weights, weights, P(), tokens),
        out_specs=(tokens, tokens, weights, weights),
        check_vma=False,
    )
```

```python
import functools
import math
import jax
import jax.numpy as jnp
from jax import lax
from jax.experimental import pallas as pl
from jax.experimental.pallas import tpu as pltpu

HEAD_WIDTH = 64
LONGITUDES = 256
BAND_ROWS = 8
HALO = 6
EXT_ROWS = BAND_ROWS + 2 * HALO
LANES = 256
QUERY_ROWS = 4
KEY_ROWS = QUERY_ROWS + 2 * HALO
BLOCK = 8
BLOCKS = LONGITUDES // BLOCK
KEYS = KEY_ROWS * BLOCK
MASKED = -1e30


def nn(a, b):
    return lax.dot_general(a, b, (((1,), (0,)), ((), ())), preferred_element_type=jnp.float32)


def nt(a, b):
    return lax.dot_general(a, b, (((1,), (1,)), ((), ())), preferred_element_type=jnp.float32)


def row_cols(row, start, size):
    return pl.ds(pl.multiple_of(row * LONGITUDES + start, 16), size)


def attention_kernel(
    heads, steps,
    cells, order, qkv, kv_top, kv_bot, weight, *refs,
):
    upstream, refs = refs[:steps], refs[steps:]
    outq_parts, refs = refs[:steps], refs[steps:]
    dkv_own, dkv_top, dkv_bot, held, outq, go, k_s, v_s, kt_s, vt_s, dk_s, dv_s, live_s, near_s, sems = refs
    feats = heads * HEAD_WIDTH
    chunk = BAND_ROWS * LONGITUDES // steps
    moves = [
        pltpu.make_async_copy(part, held.at[pl.ds(i * chunk, chunk)], sems.at[i]) for i, part in enumerate(upstream)
    ]
    for move in moves:
        move.start()
    tile_cols = LANES // heads // QUERY_ROWS
    tile_queries = QUERY_ROWS * tile_cols
    window = tile_cols // BLOCK + 2

    def load_pair(p, carry):
        for first, rows_s, turned_s in ((0, k_s, kt_s), (feats, v_s, vt_s)):
            both = jnp.stack(
                [kv_top[row_cols(row, p * 16, 16), first:first + feats] for row in range(HALO)]
                + [qkv[row_cols(row, p * 16, 16), feats + first:2 * feats + first] for row in range(BAND_ROWS)]
                + [kv_bot[row_cols(row, p * 16, 16), first:first + feats] for row in range(HALO)]
            ).astype(jnp.float32)
            for half in range(2):
                block = both[:, 8 * half:8 * half + 8, :].reshape(EXT_ROWS * BLOCK, feats)
                rows_s[2 * p + half] = block.astype(jnp.bfloat16)
                for upper in range(2):
                    low = upper * QUERY_ROWS * BLOCK
                    turned_s[upper, 2 * p + half] = block[low:low + KEYS].T.astype(jnp.bfloat16)
        for half in range(2):
            col = (2 * p + half) * BLOCK + lax.broadcasted_iota(jnp.int32, (BLOCK, 128), 0)
            for row in range(EXT_ROWS):
                live_s[2 * p + half, row * BLOCK:(row + 1) * BLOCK, :] = jnp.where(col < cells[row], 0.0, MASKED)
        return carry

    lax.fori_loop(0, BLOCKS // 2, load_pair, 0)
    dk_s[...] = jnp.zeros_like(dk_s)
    dv_s[...] = jnp.zeros_like(dv_s)

    lane = lax.broadcasted_iota(jnp.int32, (KEYS, LANES), 1) % tile_queries
    query_row = lane // tile_cols
    query_col = lane % tile_cols
    key = lax.broadcasted_iota(jnp.int32, (KEYS, LANES), 0)
    row_gap = key // BLOCK - query_row
    for j in range(window):
        col_gap = (j - 1) * BLOCK + key % BLOCK - query_col
        near = (row_gap >= 0) & (row_gap <= 2 * HALO) & (col_gap >= -HALO) & (col_gap <= HALO)
        near_s[j] = jnp.where(near, 0.0, MASKED)

    own_head = (
        lax.broadcasted_iota(jnp.int32, (LANES, feats), 0) // tile_queries
        == lax.broadcasted_iota(jnp.int32, (LANES, feats), 1) // HEAD_WIDTH
    )
    own_head_turned = (
        lax.broadcasted_iota(jnp.int32, (feats, LANES), 1) // tile_queries
        == lax.broadcasted_iota(jnp.int32, (feats, LANES), 0) // HEAD_WIDTH
    )
    query_lane = lax.broadcasted_iota(jnp.int32, (1, LANES), 1) % tile_queries

    def spread(ref, upper, start):
        tile = jnp.concatenate([
            ref[row_cols(upper * QUERY_ROWS + row, start, tile_cols), :feats] for row in range(QUERY_ROWS)
        ], axis=0)
        if heads == 1:
            return tile
        stacked = jnp.concatenate([tile] * heads, axis=0)
        return jnp.where(own_head, stacked, jnp.zeros_like(stacked))

    def gather(turned):
        if heads == 1:
            tile = turned.T
        else:
            tall = jnp.where(own_head_turned, turned, 0.0).T
            tile = sum(tall[h * tile_queries:(h + 1) * tile_queries] for h in range(heads))
        return tile.astype(jnp.bfloat16)

    def one_tile(upper, tile):
        start = pl.multiple_of(tile * tile_cols, 16)
        keys = pl.ds(upper * QUERY_ROWS * BLOCK, KEYS)
        index = [(tile * (tile_cols // BLOCK) + j + BLOCKS - 1) % BLOCKS for j in range(window)]
        queries = spread(qkv, upper, start)
        grads = spread(go, upper, start)
        scores = [
            nt(k_s[index[j], keys, :], queries)
            + near_s[j]
            + jnp.concatenate([live_s[index[j], keys, :]] * (LANES // 128), axis=1)
            for j in range(window)
        ]
        grad_probs = [nt(v_s[index[j], keys, :], grads) for j in range(window)]
        yield
        highest = jnp.max(functools.reduce(jnp.maximum, scores), axis=0, keepdims=True)
        terms = [jnp.exp(score - highest) for score in scores]
        total = jnp.sum(sum(terms), axis=0, keepdims=True)
        query_cells = jnp.zeros((1, LANES), jnp.int32)
        for row in range(QUERY_ROWS):
            cell = cells[HALO + upper * QUERY_ROWS + row]
            query_cells = jnp.where(query_lane // tile_cols == row, cell, query_cells)
        live = start + query_lane % tile_cols < query_cells
        inverse = jnp.where(live, 1.0 / total, 0.0)
        probs = [term * inverse for term in terms]
        delta = jnp.sum(sum(p * g for p, g in zip(probs, grad_probs)), axis=0, keepdims=True)
        weights = [p.astype(jnp.bfloat16) for p in probs]
        grad_scores = [(p * (g - delta)).astype(jnp.bfloat16) for p, g in zip(probs, grad_probs)]
        yield
        for j in range(window):
            dv_s[index[j], keys, :] += nn(weights[j], grads)
            dk_s[index[j], keys, :] += nn(grad_scores[j], queries)
        values_turned = jnp.concatenate([vt_s[upper, index[j]] for j in range(window)], axis=1)
        keys_turned = jnp.concatenate([kt_s[upper, index[j]] for j in range(window)], axis=1)
        heads_out = gather(nn(values_turned, jnp.concatenate(weights, axis=0)))
        grad_query = gather(nn(keys_turned, jnp.concatenate(grad_scores, axis=0)))
        for row in range(QUERY_ROWS):
            at = row_cols(upper * QUERY_ROWS + row, start, tile_cols)
            outq[at, :feats] = heads_out[row * tile_cols:(row + 1) * tile_cols]
            outq[at, feats:] = grad_query[row * tile_cols:(row + 1) * tile_cols]

    def tile_pair(tile, carry):
        low, high = one_tile(0, tile), one_tile(1, tile)
        for stage in (low, high, low, low, high, high):
            next(stage, None)
        return carry

    for move in moves:
        move.wait()
    grad_heads = nt(held[...], weight[...]).astype(jnp.bfloat16)
    for i in range(steps):
        go[pl.ds(pl.multiple_of(order[i], 16), chunk)] = grad_heads[i * chunk:(i + 1) * chunk]
    lax.fori_loop(0, LONGITUDES // tile_cols, tile_pair, 0)
    moves = [
        pltpu.make_async_copy(outq.at[pl.ds(pl.multiple_of(order[i], 16), chunk)], part, sems.at[i])
        for i, part in enumerate(outq_parts)
    ]
    for move in moves:
        move.start()

    def store_pair(p, carry):
        for first, sums in ((0, dk_s), (feats, dv_s)):
            both = jnp.concatenate(
                [sums[2 * p + half].reshape(EXT_ROWS, BLOCK, feats) for half in range(2)], axis=1
            )
            for row in range(HALO):
                dkv_top[row_cols(row, p * 16, 16), first:first + feats] = both[row].astype(jnp.bfloat16)
                dkv_bot[row_cols(row, p * 16, 16), first:first + feats] = (
                    both[HALO + BAND_ROWS + row].astype(jnp.bfloat16)
                )
            for row in range(BAND_ROWS):
                dkv_own[row_cols(row, p * 16, 16), first:first + feats] = both[HALO + row]
        return carry

    lax.fori_loop(0, BLOCKS // 2, store_pair, 0)
    for move in moves:
        move.wait()


VMEM = pl.BlockSpec(memory_space=pltpu.VMEM)
SMEM = pl.BlockSpec(memory_space=pltpu.SMEM)
HBM = pl.BlockSpec(memory_space=pl.ANY)
BF16, F32 = jnp.bfloat16, jnp.float32


def shape(rows, cols, kind=BF16):
    return jax.ShapeDtypeStruct((rows, cols), kind)


def call(kernel, out_shape, in_specs, out_specs, args, flops, scratch=(), transcendentals=0):
    moved = sum(x.size * x.dtype.itemsize for x in (*args, *out_shape)) if flops else 0
    return pl.pallas_call(
        kernel,
        out_shape=tuple(out_shape),
        in_specs=list(in_specs),
        out_specs=tuple(out_specs),
        scratch_shapes=list(scratch),
        compiler_params=pltpu.CompilerParams(vmem_limit_bytes=60 * 2**20),
        cost_estimate=pl.CostEstimate(
            flops=flops, transcendentals=transcendentals, bytes_accessed=moved
        ),
    )(*args)


def attention(cells, order, qkv, kv_top, kv_bot, weight, upstream):
    steps, (feats, width), chunk = len(upstream), weight.shape, upstream[0].shape[0]
    heads = feats // HEAD_WIDTH
    window = LANES // heads // QUERY_ROWS // BLOCK + 2
    band, halo = BAND_ROWS * LONGITUDES, HALO * LONGITUDES
    pairs = band * heads * KEYS * window
    results = call(
        functools.partial(attention_kernel, heads, steps),
        [shape(chunk, 2 * feats)] * steps
        + [shape(band, 2 * feats, F32), shape(halo, 2 * feats), shape(halo, 2 * feats)],
        [SMEM, SMEM, VMEM, VMEM, VMEM, VMEM] + [HBM] * steps,
        [HBM] * steps + [VMEM] * 3,
        (cells, order, qkv, kv_top, kv_bot, weight, *upstream),
        flops=12 * pairs * HEAD_WIDTH * heads + 2 * band * weight.size,
        transcendentals=pairs,
        scratch=[
            pltpu.VMEM((band, width), BF16),
            pltpu.VMEM((band, 2 * feats), BF16),
            pltpu.VMEM((band, feats), BF16),
            pltpu.VMEM((BLOCKS, EXT_ROWS * BLOCK, feats), BF16),
            pltpu.VMEM((BLOCKS, EXT_ROWS * BLOCK, feats), BF16),
            pltpu.VMEM((2, BLOCKS, feats, KEYS), BF16),
            pltpu.VMEM((2, BLOCKS, feats, KEYS), BF16),
            pltpu.VMEM((BLOCKS, EXT_ROWS * BLOCK, feats), F32),
            pltpu.VMEM((BLOCKS, EXT_ROWS * BLOCK, feats), F32),
            pltpu.VMEM((BLOCKS, EXT_ROWS * BLOCK, 128), F32),
            pltpu.VMEM((window, KEYS, LANES), F32),
            pltpu.SemaphoreType.DMA((steps,)),
        ],
    )
    return (results[:steps], *results[steps:])


def norm_kernel(tokens, gain, normed):
    features = tokens[...].astype(F32)
    inverse = lax.rsqrt(jnp.mean(features * features, axis=1, keepdims=True) + 1e-06)
    normed[...] = (features * inverse * gain[...]).astype(BF16)


def norm(tokens, gain):
    return call(
        norm_kernel, [shape(*tokens.shape)], [VMEM] * 2, [VMEM], (tokens, gain[None, :]), flops=4 * tokens.size
    )[0]


def stacked_moves(parts, held, sems, first=0):
    chunk = parts[0].shape[0]
    return [
        pltpu.make_async_copy(part, held.at[pl.ds(i * chunk, chunk)], sems.at[first + i]) for i, part in enumerate(parts)
    ]


def carry_out(moves):
    for move in moves:
        move.start()
    for move in moves:
        move.wait()


def projection_kernel(steps, feats, order, flag, mine, sibling, *refs):
    parts, (qkv, kv_up, kv_down, normed_up, normed_down, held, sems) = refs[:steps], refs[steps:]
    chunk = parts[0].shape[0]
    halo, rest = HALO * LONGITUDES, (BAND_ROWS - HALO) * LONGITUDES
    carry_out([
        pltpu.make_async_copy(part, held.at[pl.ds(pl.multiple_of(order[i], 16), chunk)], sems.at[i])
        for i, part in enumerate(parts)
    ])
    moves = [
        pltpu.make_async_copy(held.at[pl.ds(rest, halo)], normed_up, sems.at[0]),
        pltpu.make_async_copy(held.at[pl.ds(0, halo)], normed_down, sems.at[1]),
    ]
    for move in moves:
        move.start()
    for i in range(3):
        at = slice(i * feats, (i + 1) * feats)
        product = nt(held[...], jnp.where(flag[0] == 1, mine[at, :], sibling[at, :])).astype(BF16)
        qkv[:, i * feats:(i + 1) * feats] = product
        if i:
            kv_up[:, (i - 1) * feats:i * feats] = product[rest:]
            kv_down[:, (i - 1) * feats:i * feats] = product[:halo]
    for move in moves:
        move.wait()


def projections(order, flag, mine, sibling, parts):
    steps, feats, width = len(parts), mine.shape[0] // 4, parts[0].shape[1]
    band, halo = BAND_ROWS * LONGITUDES, HALO * LONGITUDES
    return call(
        functools.partial(projection_kernel, steps, feats),
        [shape(band, 3 * feats)] + [shape(halo, 2 * feats)] * 2 + [shape(halo, width)] * 2,
        [SMEM, SMEM, VMEM, VMEM] + [HBM] * steps, [VMEM] * 3 + [HBM] * 2, (order, flag, mine, sibling, *parts),
        flops=6 * band * feats * width,
        scratch=[pltpu.VMEM((band, width), BF16), pltpu.SemaphoreType.DMA((steps,))],
    )


def join_kernel(steps, order, own, above, below, *refs):
    outq_parts, parts, whole = refs[:steps], refs[steps:2 * steps], refs[-1]
    chunk, feats = outq_parts[0].shape
    low, high = (BAND_ROWS - HALO) * LONGITUDES, HALO * LONGITUDES
    for outq, part in zip(outq_parts, parts):
        part[:, :feats] = outq[...]
    whole[:low] = (own[:low] + below[:low].astype(F32)).astype(BF16)
    whole[low:high] = (own[low:high] + below[low:].astype(F32) + above[:high - low].astype(F32)).astype(BF16)
    whole[high:] = (own[high:] + above[high - low:].astype(F32)).astype(BF16)
    for i, part in enumerate(parts):
        part[:, feats:] = whole[pl.ds(pl.multiple_of(order[i], 16), chunk), :]


def joined(order, own, above, below, outq_parts):
    steps, (chunk, feats) = len(outq_parts), outq_parts[0].shape
    return call(
        functools.partial(join_kernel, steps),
        [shape(chunk, 2 * feats)] * steps,
        [SMEM] + [VMEM] * (3 + steps), [VMEM] * steps, (order, own, above, below, *outq_parts), flops=0,
        scratch=[pltpu.VMEM((steps * chunk, feats), BF16)],
    )


def weight_grad_kernel(steps, order, *refs):
    (outq_parts, upstream, normed), refs = [refs[i * steps:(i + 1) * steps] for i in range(3)], refs[3 * steps:]
    dkv, dkv_top, dkv_bot, normed_top, normed_bot, grad, outq, up, own, sems = refs
    feats, chunk = outq.shape[1] // 2, outq_parts[0].shape[0]
    groups = [
        [
            pltpu.make_async_copy(part, held.at[pl.ds(pl.multiple_of(order[i], 16), chunk)], sems.at[group, i])
            for i, part in enumerate(parts)
        ]
        for group, (parts, held) in enumerate(((outq_parts, outq), (normed, own), (upstream, up)))
    ]
    for moves in groups:
        for move in moves:
            move.start()

    def product(left, right):
        return lax.dot_general(left, right, (((0,), (0,)), ((), ())), preferred_element_type=F32)

    keyval = product(dkv_top[...], normed_top[...]) + product(dkv_bot[...], normed_bot[...])
    for moves in groups[:2]:
        for move in moves:
            move.wait()
    grad[2 * feats:, :] = (keyval + product(dkv[...].astype(BF16), own[...])).astype(BF16)
    grad[feats:2 * feats, :] = product(outq[:, feats:], own[...]).astype(BF16)
    for move in groups[2]:
        move.wait()
    grad[:feats, :] = product(outq[:, :feats], up[...]).astype(BF16)


def weight_grads(order, outq_parts, upstream, normed, dkv, dkv_halos, normed_halos):
    steps, (chunk, rows), width = len(normed), outq_parts[0].shape, normed[0].shape[1]
    band = steps * chunk
    return call(
        functools.partial(weight_grad_kernel, steps),
        [shape(2 * rows, width)], [SMEM] + [HBM] * (3 * steps) + [VMEM] * 5, [VMEM],
        (order, *outq_parts, *upstream, *normed, dkv, *dkv_halos, *normed_halos),
        flops=2 * width * rows * (2 * band + 2 * HALO * LONGITUDES),
        scratch=[
            pltpu.VMEM((band, rows), BF16), pltpu.VMEM((band, width), BF16), pltpu.VMEM((band, width), BF16),
            pltpu.SemaphoreType.DMA((3, steps)),
        ],
    )[0]


def token_kernel(steps, leads, tokens, gain, *refs):
    parts, blocks, (update, grad, left, qkv, out, sems) = refs[:steps], refs[steps:2 * steps], refs[2 * steps:]
    feats = out.shape[0] // steps
    carry_out([
        move for i, block in enumerate(blocks) for move in (
            pltpu.make_async_copy(block.at[pl.ds(0, 3 * feats)], qkv.at[pl.ds(3 * i * feats, 3 * feats)], sems.at[i]),
            pltpu.make_async_copy(block.at[pl.ds(3 * feats, feats)], out.at[pl.ds(i * feats, feats)], sems.at[steps + i]),
        )
    ])
    for i, part in enumerate(parts):
        left[leads[i]] = part[...]
    side_by_side = lambda cut: jnp.concatenate([left[i, :, cut] for i in range(steps)], axis=1)
    update[...] = nn(side_by_side(slice(0, feats)), out[...]).astype(BF16)
    grad_normed = nn(side_by_side(slice(feats, None)), qkv[...])
    features = tokens[...].astype(F32)
    inverse = lax.rsqrt(jnp.mean(features * features, axis=1, keepdims=True) + 1e-06)
    centred = features * inverse
    scaled = gain[...] * grad_normed
    grad[...] = (inverse * (scaled - centred * jnp.mean(scaled * centred, axis=1, keepdims=True))).astype(BF16)


def token_outputs(leads, tokens, gain, parts, blocks):
    steps, (rows, width), chunk = len(blocks), blocks[0].shape, tokens.shape[0]
    feats = rows // 4
    return call(
        functools.partial(token_kernel, steps),
        [shape(chunk, width)] * 2, [SMEM] + [VMEM] * (2 + steps) + [HBM] * steps, [VMEM] * 2,
        (leads, tokens, gain[None, :], *parts, *blocks), flops=2 * steps * chunk * rows * width,
        scratch=[
            pltpu.VMEM((steps, chunk, rows), BF16),
            pltpu.VMEM((3 * steps * feats, width), BF16),
            pltpu.VMEM((steps * feats, width), BF16),
            pltpu.SemaphoreType.DMA((2 * steps,)),
        ],
    )


def finish_kernel(scale, flag, mine, other, grad_qkv, grad_out):
    for i in range(4):
        part = jnp.where(flag[0] == 1, mine[i, 0], other[i, 0]).astype(F32)
        if i == 0:
            grad_out[0] = part * scale
        else:
            factor = scale * HEAD_WIDTH ** -0.5 if i == 1 else scale
            grad_qkv[0, (i - 1) * HEAD_WIDTH:i * HEAD_WIDTH, :] = part * factor


def finished(scale, flag, mine, other):
    heads, width = mine.shape[0] // (4 * HEAD_WIDTH), mine.shape[1]
    by_head = lambda x: x.reshape(4, heads, HEAD_WIDTH, width)
    sums = pl.BlockSpec((4, 1, HEAD_WIDTH, width), lambda h: (0, h, 0, 0))
    result = lambda rows: pl.BlockSpec((1, rows, width), lambda h: (h, 0, 0))
    return pl.pallas_call(
        functools.partial(finish_kernel, scale),
        grid=(heads,),
        out_shape=(
            jax.ShapeDtypeStruct((heads, 3 * HEAD_WIDTH, width), F32),
            jax.ShapeDtypeStruct((heads, HEAD_WIDTH, width), F32),
        ),
        in_specs=[SMEM, sums, sums],
        out_specs=(result(3 * HEAD_WIDTH), result(HEAD_WIDTH)),
        compiler_params=pltpu.CompilerParams(vmem_limit_bytes=32 * 2**20),
        cost_estimate=pl.CostEstimate(flops=mine.size, transcendentals=0, bytes_accessed=8 * mine.size),
    )(flag, by_head(mine), by_head(other))


from jax.sharding import Mesh, PartitionSpec as P

WIDTH = 1024
GROUP = ("y", "m", "c")


def owners(halves):
    if halves == 2:
        return [
            lambda y, m, c: (c, 1 - m if c == y else m, y),
            lambda y, m, c: (c, 1 - m if c == y else m, 1 - y),
            lambda y, m, c: (c, m if c == y else 1 - m, 1 - y),
            lambda y, m, c: (c, m if c == y else 1 - m, y),
        ]
    return [
        lambda y, m, c, dm=dm, dc=dc: (c, (m + dm) % halves, (y + dc) % 2) for dc in range(2) for dm in range(halves)
    ]


def passed_along(x, by):
    length = lax.axis_size("z") * 2
    pairs = [(i, i + by) for i in range(length) if 0 <= i + by < length]
    return lax.ppermute(x, ("z", "c"), pairs)


def after(x, *others):
    return lax.optimization_barrier((x, *others))[0]


def on_device(tokens, gain, qkv_weight, out_weight, row_cells, upstream):
    heads = qkv_weight.shape[0]
    feats = heads * HEAD_WIDTH
    band_tokens = BAND_ROWS * LONGITUDES
    chunk = tokens.shape[0]
    halves, layers = lax.axis_size("m"), lax.axis_size("z")
    z, y, m, c = (lax.axis_index(axis) for axis in ("z",) + GROUP)
    grad_scale = 4.0 / math.sqrt(band_tokens * layers * 2)
    band_start = (z * 2 + c) * BAND_ROWS
    cells = lax.dynamic_slice_in_dim(jnp.pad(row_cells, (HALO, HALO)), band_start, EXT_ROWS)

    at = lambda y, m, c: (y * halves + m) * 2 + c
    spots = [(y, m, c) for y in range(2) for m in range(halves) for c in range(2)]
    slots = [[owner(*spot) for spot in spots] for owner in owners(halves)]
    here = lambda table: jnp.asarray(table, jnp.int32)[at(y, m, c)]
    order = here([[(slot[i][1] * 2 + slot[i][2]) * chunk for slot in slots] for i in range(len(spots))])

    def lead(slot, spot):
        far = spots[slot.index(spot)]
        return (far[0] - spot[2]) % 2 * halves + (far[1] - spot[1]) % halves

    leads = here([[lead(slot, spot) for slot in slots] for spot in spots])

    def permuted(x, pairs):
        return lax.ppermute(x, GROUP, [(at(*a), at(*b)) for a, b in pairs])

    def send_back(parts):
        return [permuted(x, list(zip(spots, slot))) for x, slot in zip(parts, slots)]

    def gathered(x, *others, extra=()):
        sent = lambda slot: permuted(x, list(zip(slot, spots)))
        if halves != 2:
            parts = [sent(slot) for slot in slots]
            return parts, (*parts, *extra)
        hop = lax.optimization_barrier((sent(slots[0]), sent(slots[1]), *extra))
        first, second = hop[:2]
        first = after(first, *others)
        third = permuted(
            jnp.where(c == y, first, x),
            [(spot, (1 - spot[0], spot[1], spot[0]) if spot[2] == spot[0] else (spot[0], spot[1], spot[0])) for spot in spots],
        )
        fourth = permuted(
            first, [(spot, (spot[0], 1 - spot[1], spot[2])) for spot in spots if spot[2] != spot[0]]
        )
        third, fourth = lax.optimization_barrier((third, fourth))
        return [first, second, third, jnp.where(c == y, x, fourth)], hop

    def from_ahead(x, dm):
        return lax.ppermute(x, "m", [((i + dm) % halves, i) for i in range(halves)])

    def from_sibling(x):
        return lax.ppermute(x, "c", [(0, 1), (1, 0)])

    normed = norm(tokens, gain)
    normed, qkv_weight, out_weight = lax.optimization_barrier((normed, qkv_weight, out_weight))

    def split(qkv, out):
        eighth = jnp.asarray([HEAD_WIDTH ** -0.5, 1.0, 1.0], BF16)[None, :, None, None]
        qkv = (qkv.reshape(heads, 3, HEAD_WIDTH, WIDTH) * eighth).transpose(1, 0, 2, 3)
        return jnp.concatenate([qkv.reshape(3 * feats, WIDTH), out.reshape(feats, WIDTH)], axis=0)

    blocks = [split(qkv_weight, out_weight)]
    flag = jnp.reshape(c == y, (1,)).astype(jnp.int32)
    normed_parts, (*hop, order, leads, flag) = gathered(normed, extra=(order, leads, flag))
    sibling = from_sibling(after(blocks[0], *hop))
    group_out = jnp.where(c == y, blocks[0][3 * feats:], sibling[3 * feats:])
    *normed_parts, sibling = lax.optimization_barrier((*normed_parts, sibling))
    qkv, kv_up, kv_down, normed_up, normed_down = projections(order, flag, blocks[0], sibling, normed_parts)
    kv_top, kv_bot = passed_along(kv_up, 1), passed_along(kv_down, -1)
    upstream_parts, _ = gathered(after(upstream, *normed_parts), qkv)

    kv_top, kv_bot, normed_up, normed_down, *upstream_parts = lax.optimization_barrier(
        (kv_top, kv_bot, normed_up, normed_down, *upstream_parts)
    )
    normed_halos = passed_along(normed_up, 1), passed_along(normed_down, -1)
    ahead = [from_ahead(after(blocks[0], *upstream_parts), dm) for dm in range(1, halves)]
    outq_parts, dkv, dkv_top, dkv_bot = attention(cells, order, qkv, kv_top, kv_bot, group_out, upstream_parts)

    from_above, from_below = passed_along(dkv_top, -1), passed_along(dkv_bot, 1)
    grads = weight_grads(
        order, outq_parts, upstream_parts, normed_parts, dkv, (dkv_top, dkv_bot), normed_halos
    )
    grads_sum = lax.psum(grads, ("z", "c"))
    parts = joined(after(order, grads), dkv, from_above, from_below, outq_parts)
    parts, ahead = lax.optimization_barrier((parts, ahead))
    parts_own = send_back(parts)
    ahead = [after(block, grads_sum) for block in ahead]
    blocks += ahead + [sibling] + [from_sibling(block) for block in ahead]
    update, grad_input = token_outputs(leads, tokens, gain, parts_own, blocks)
    grads = after(grads_sum, *parts_own)
    pairs = [((1 - y, m, 1 - y), (y, m, 1 - y)) for y in range(2) for m in range(halves)]
    flag = after(flag, grad_input, update)
    grad_qkv, grad_out = finished(grad_scale, flag, grads, permuted(grads, pairs))
    return update, grad_input, grad_qkv, grad_out


def solution(mesh):
    devices = mesh.devices.reshape(mesh.shape["lat"] // 2, 2, mesh.shape["mp"] // 2, 2)
    tokens, weights = P(("z", "y", "m", "c"), None), P(("m", "c"), None, None)
    return jax.shard_map(
        on_device,
        mesh=Mesh(devices, ("z", "y", "m", "c")),
        in_specs=(tokens, P(), weights, weights, P(), tokens),
        out_specs=(tokens, tokens, weights, weights),
        check_vma=False,
    )
```
